32 devices in a mesh: tower: 4 (over y, x), intra: 8 (over z, core).
Axes of the slice: x: 2, y: 2, z: 4, core: 2. Of those that a mesh axis runs over, the one named last changes fastest.
Arguments:
- embeddings: bfloat16 [256, 16384], P(None, ('tower', 'intra')), may hold values from -6 to 6
- feature_assign: int32 [4, 32], P('tower'), may hold values from 0 to 31, each once within a row
- sample_owner: int32 [256], replicated, may hold values from 0 to 255, each once
- first_weight: bfloat16 [8, 2048, 1024], P('tower'), may hold values from -0.125 to 0.125
- first_bias: float32 [8, 1024], P('tower'), may hold values from -3 to 3
- tower_weight: bfloat16 [8, 1024, 256], P('tower'), may hold values from -0.1875 to 0.1875
- tower_bias: float32 [8, 256], P('tower'), may hold values from -3 to 3
- proj_weight: bfloat16 [16, 128], replicated, may hold values from -1.5 to 1.5
Outputs:
- interaction: bfloat16 [256, 16, 128], P(('tower', 'intra'))
The draws below stay inside these ranges and needn't reach their ends.
Inputs may be any that keep to these rules, and one draw needn't show every extreme that they name: `feature_assign`: each row is a permutation of 0 to 31. `sample_owner`: a permutation of 0 to 255.
All inputs are finite; a program needn't handle non-finite values.
Results may differ from the reference program's by a relative error of at most 0.0034.
Values may be sent and summed in bfloat16 or wider, within the bound.
No kernel may reach another device: no remote copies, remote signals or barrier semaphores. Data moves between devices by JAX's collectives and lax.ppermute only.
A program may use at most 64 MiB of HBM per device.

```python
import jax
import jax.numpy as jnp
from jax import lax

EDIM = 128
TFEAT = 16
HID = 1024
TOUT = 256
TOW_DEV = 2
SD = 8
TIN = 2048
TVEC = 2
FPT = 32
TOWERS = 8
NVEC = 16
FEATURES = 128
SAMPLES = 256
N_TOWER = 4
N_INTRA = 8


def shard_levels(own_key, shape, shards, smallest, high):
    factor_of, own = 1.0, jax.random.fold_in(own_key, 6)
    for dim, parts in shards:
        draws = jnp.exp(jax.random.uniform(jax.random.fold_in(own, dim), (parts,), jnp.float32, smallest / len(shards), high / len(shards)))
        factor_of = factor_of * jnp.repeat(draws, shape[dim] // parts).reshape([-1 if axis == dim else 1 for axis in range(len(shape))])
    return factor_of


def scatter_about(rng, shape, deviation, bound, cuts=(), kind=jnp.bfloat16):
    level = shard_levels(rng, shape, cuts, -0.22, 0.18) if cuts else 1.0
    values = jax.random.normal(rng, shape, jnp.float32) * deviation * level
    return jnp.minimum(jnp.maximum(values, -bound), bound).astype(kind)


def setup_inputs(seed: int = 0) -> dict:
    arg_keys = jax.random.split(jax.random.key(seed), 9)
    return {
        "embeddings": scatter_about(arg_keys[0], (SAMPLES, FEATURES * EDIM), 1.0, 6.0, ((1, 32),)),
        "feature_assign": jax.vmap(lambda own: jax.random.permutation(own, FPT))(jax.random.split(arg_keys[1], N_TOWER)).reshape((N_TOWER, FPT)).astype(jnp.int32),
        "sample_owner": jax.random.permutation(arg_keys[2], SAMPLES).astype(jnp.int32),
        "first_weight": scatter_about(arg_keys[3], (TOWERS, TIN, HID), TIN ** -0.5, 0.125, ((0, 4),)),
        "first_bias": scatter_about(arg_keys[4], (TOWERS, HID), 0.5, 3.0, ((0, 4),), jnp.float32),
        "tower_weight": scatter_about(arg_keys[5], (TOWERS, HID, TOUT), HID ** -0.5, 0.1875, ((0, 4),)),
        "tower_bias": scatter_about(arg_keys[6], (TOWERS, TOUT), 0.5, 3.0, ((0, 4),), jnp.float32),
        "proj_weight": scatter_about(arg_keys[7], (NVEC, EDIM), NVEC ** -0.5, 1.5),
    }


def reference(embeddings, feature_assign, sample_owner, first_weight, first_bias, tower_weight, tower_bias, proj_weight):
    ordered = jnp.take(embeddings, sample_owner, axis=0)
    tower_ids = jnp.arange(TOWERS, dtype=jnp.int32)

    def one_tower(tower_number):
        tower_index = tower_number // TOW_DEV
        slot_index = tower_number % TOW_DEV
        assign_row = feature_assign[tower_index]
        selected = lax.dynamic_slice_in_dim(assign_row, (slot_index * TFEAT).astype(jnp.int32), TFEAT)
        feature_ids = (tower_index * FPT + selected).astype(jnp.int32)
        columns = (feature_ids[:, None] * EDIM + jnp.arange(EDIM, dtype=jnp.int32)[None, :]).reshape(-1)
        inputs = jnp.take(ordered, columns, axis=1).astype(jnp.float32)
        hidden = jnp.dot(inputs, first_weight[tower_number].astype(jnp.float32), precision=lax.Precision.HIGHEST)
        hidden = jnp.maximum(hidden + first_bias[tower_number], 0.0).astype(jnp.bfloat16)
        result = jnp.dot(hidden.astype(jnp.float32), tower_weight[tower_number].astype(jnp.float32), precision=lax.Precision.HIGHEST)
        result = result + tower_bias[tower_number]
        return jnp.maximum(result, 0.0).astype(jnp.bfloat16)

    tower_outputs = lax.map(one_tower, tower_ids)
    vectors = tower_outputs.reshape(TOWERS, SAMPLES, TVEC, EDIM).transpose(1, 0, 2, 3).reshape(SAMPLES, NVEC, EDIM)
    block = SD * N_INTRA
    blocks = vectors.reshape(SAMPLES // block, block, NVEC, EDIM)
    weight_wide = proj_weight.astype(jnp.float32)

    def interact(vector_block):
        vector_wide = vector_block.astype(jnp.float32)
        gram_matrix = jnp.einsum("pie,pje->pij", vector_wide, vector_wide, precision=lax.Precision.HIGHEST) / EDIM
        result = jnp.einsum("pij,je->pie", gram_matrix, weight_wide, precision=lax.Precision.HIGHEST)
        return result.astype(jnp.bfloat16)

    return lax.map(interact, blocks).reshape(SAMPLES, NVEC, EDIM)
```

```python
import functools

import jax
import jax.numpy as jnp
from jax import lax
from jax.experimental import pallas as pl
from jax.experimental.pallas import tpu as pltpu
from jax.sharding import PartitionSpec as P

EDIM = 128
FEW_SAMPLES = 1024


def swap(block, axis, size, offset):
    if offset == 0:
        return block
    return lax.ppermute(block, axis, [(i, i ^ offset) for i in range(size)])


def gather_kernel(towers, intra, owner_ref, emb_ref, *rest):
    outs, acc_ref = rest[:intra], rest[intra]
    samples, width = emb_ref.shape
    per = samples // (towers * intra)
    me = lax.axis_index("intra")
    owner = jnp.broadcast_to(owner_ref[...].reshape(1, samples), (samples, samples))
    picks = lax.broadcasted_iota(jnp.int32, (samples, samples), 0) == owner
    picks = jnp.where(picks, 1.0, 0.0).astype(jnp.bfloat16)
    acc_ref[...] = lax.dot_general(
        picks, emb_ref[...], (((0,), (0,)), ((), ())), preferred_element_type=jnp.float32
    )
    for o, out in enumerate(outs):
        block = me ^ o
        starts = [pl.multiple_of((t * intra + block) * per, per) for t in range(towers)]
        for f in range(width // EDIM):
            columns = slice(f * EDIM, (f + 1) * EDIM)
            rows = [acc_ref[pl.ds(start, per), columns] for start in starts]
            out[f] = jnp.concatenate(rows, axis=0).astype(out.dtype)


def gather_blocks(owner, embeddings, towers, intra):
    samples, width = embeddings.shape
    rows, held = samples // intra, width // EDIM
    shape = jax.ShapeDtypeStruct((held, rows, EDIM), embeddings.dtype)
    if samples <= FEW_SAMPLES:
        return pl.pallas_call(
            functools.partial(gather_kernel, towers, intra),
            out_shape=[shape] * intra,
            in_specs=[pl.BlockSpec(memory_space=pltpu.VMEM)] * 2,
            out_specs=[pl.BlockSpec(memory_space=pltpu.VMEM)] * intra,
            scratch_shapes=[pltpu.VMEM((samples, width), jnp.float32)],
            compiler_params=pltpu.CompilerParams(vmem_limit_bytes=8 << 20),
            name="gather_rows",
        )(owner, embeddings)
    order = owner.reshape(towers, intra, -1).transpose(1, 0, 2).reshape(-1)
    blocks = jnp.take(embeddings, order, axis=0).reshape(intra, rows, held, EDIM).transpose(0, 2, 1, 3)
    me = lax.axis_index("intra")
    return [lax.dynamic_index_in_dim(blocks, me ^ o, keepdims=False) for o in range(intra)]


def tower_kernel(towers, intra, assign_ref, w1_ref, b1_ref, w2_ref, b2_ref, *rest):
    blocks, outs = rest[:intra], rest[intra : intra + towers]
    pool_ref, x_ref, y_ref = rest[intra + towers :]
    held, rows, _ = blocks[0].shape
    count, depth, _ = w1_ref.shape
    vectors = w2_ref.shape[2] // EDIM
    per = rows // towers
    slots = depth // EDIM
    me = lax.axis_index("intra")
    for o, block in enumerate(blocks):
        pool_ref[pl.ds((me ^ o) * held, held)] = block[...]
    for k in range(count):
        for j in range(slots):
            x_ref[k, :, j * EDIM : (j + 1) * EDIM] = pool_ref[assign_ref[0, k * slots + j]]
    for k in range(count):
        hidden = jnp.dot(x_ref[k], w1_ref[k], preferred_element_type=jnp.float32)
        hidden = jnp.maximum(hidden + b1_ref[k : k + 1, :], 0.0).astype(jnp.bfloat16)
        result = jnp.dot(hidden, w2_ref[k], preferred_element_type=jnp.float32)
        y_ref[k] = jnp.maximum(result + b2_ref[k : k + 1, :], 0.0)
    place = lax.axis_index("tower")
    for o, out in enumerate(outs):
        start = pl.multiple_of((place ^ o) * per, per)
        pieces = [
            y_ref[k, pl.ds(start, per), v * EDIM : (v + 1) * EDIM]
            for k in range(count)
            for v in range(vectors)
        ]
        out[...] = jnp.concatenate(pieces, axis=0).astype(out.dtype)


def run_towers(assign, w1, b1, w2, b2, blocks, towers):
    intra = len(blocks)
    held, rows, _ = blocks[0].shape
    count, depth, _ = w1.shape
    width = w2.shape[2]
    local = count * (width // EDIM) * (rows // towers)
    w1 = pltpu.with_memory_space_constraint(w1, pltpu.VMEM)
    w2 = pltpu.with_memory_space_constraint(w2, pltpu.VMEM)
    return pl.pallas_call(
        functools.partial(tower_kernel, towers, intra),
        out_shape=[jax.ShapeDtypeStruct((local, EDIM), jnp.bfloat16)] * towers,
        in_specs=[pl.BlockSpec(memory_space=pltpu.SMEM)]
        + [pl.BlockSpec(memory_space=pltpu.VMEM)] * (4 + intra),
        out_specs=[pl.BlockSpec(memory_space=pltpu.VMEM)] * towers,
        scratch_shapes=[
            pltpu.VMEM((intra * held, rows, EDIM), jnp.bfloat16),
            pltpu.VMEM((count, rows, depth), jnp.bfloat16),
            pltpu.VMEM((count, rows, width), jnp.float32),
        ],
        compiler_params=pltpu.CompilerParams(vmem_limit_bytes=16 << 20),
        name="towers",
    )(assign, w1, b1, w2, b2, *blocks)


def interact_kernel(towers, proj_ref, *rest):
    blocks, out, all_ref = rest[:towers], rest[towers], rest[towers + 1]
    per, count, _ = out.shape
    local = blocks[0].shape[0]
    place = lax.axis_index("tower")
    for o, block in enumerate(blocks):
        start = pl.multiple_of((place ^ o) * local, local)
        all_ref[pl.ds(start, local), :] = block[...].astype(jnp.float32)
    group = max(1, min(per, 128 // count))
    proj = jnp.concatenate([proj_ref[...]] * (2 * group), axis=0)
    for first in range(0, per, group):
        samples = range(first, first + group)
        vectors = [all_ref[pl.ds(d, count, stride=per), :] for d in samples]
        vectors = jnp.concatenate(vectors, axis=0).astype(jnp.bfloat16)
        gram = lax.dot_general(
            vectors, vectors, (((1,), (1,)), ((), ())), preferred_element_type=jnp.float32
        )
        gram = gram * (1.0 / EDIM)
        column = lax.broadcasted_iota(jnp.int32, (count, gram.shape[1]), 1)
        own = [
            jnp.where(
                (column >= g * count) & (column < (g + 1) * count),
                gram[g * count : (g + 1) * count, :],
                0.0,
            )
            for g in range(group)
        ]
        gram = jnp.concatenate(own, axis=0)
        high = gram.astype(jnp.bfloat16)
        low = (gram - high.astype(jnp.float32)).astype(jnp.bfloat16)
        result = jnp.dot(
            jnp.concatenate([high, low], axis=1), proj, preferred_element_type=jnp.float32
        )
        for g, d in enumerate(samples):
            out[d] = result[g * count : (g + 1) * count, :].astype(out.dtype)


def interact(proj, blocks):
    towers = len(blocks)
    local = blocks[0].shape[0]
    count = proj.shape[0]
    per = towers * local // count
    return pl.pallas_call(
        functools.partial(interact_kernel, towers),
        out_shape=jax.ShapeDtypeStruct((per, count, EDIM), jnp.bfloat16),
        in_specs=[pl.BlockSpec(memory_space=pltpu.VMEM)] * (1 + towers),
        out_specs=pl.BlockSpec(memory_space=pltpu.VMEM),
        scratch_shapes=[pltpu.VMEM((towers * local, EDIM), jnp.float32)],
        compiler_params=pltpu.CompilerParams(vmem_limit_bytes=8 << 20),
        name="interact",
    )(proj, *blocks)


def shards(
    embeddings,
    feature_assign,
    sample_owner,
    first_weight,
    first_bias,
    tower_weight,
    tower_bias,
    proj_weight,
):
    towers, intra = lax.axis_size("tower"), lax.axis_size("intra")
    blocks = gather_blocks(sample_owner, embeddings, towers, intra)
    blocks = [swap(block, "intra", intra, o) for o, block in enumerate(blocks)]
    vectors = run_towers(
        feature_assign, first_weight, first_bias, tower_weight, tower_bias, blocks, towers
    )
    vectors = [swap(block, "tower", towers, o) for o, block in enumerate(vectors)]
    return interact(proj_weight, vectors)


def solution(mesh):
    return jax.shard_map(
        shards,
        mesh=mesh,
        in_specs=(
            P(None, ("tower", "intra")),
            P("tower", None),
            P(),
            P("tower", None, None),
            P("tower", None),
            P("tower", None, None),
            P("tower", None),
            P(),
        ),
        out_specs=P(("tower", "intra"), None, None),
        check_vma=False,
    )
```

```python
import functools

import jax
import jax.numpy as jnp
from jax import lax
from jax.experimental import pallas as pl
from jax.experimental.pallas import tpu as pltpu
from jax.sharding import PartitionSpec as P

EDIM = 128
FEW_SAMPLES = 1024


def offsets(size):
    return range(size - 1, -1, -1)


def exchange(blocks, axis, size):
    return [
        lax.ppermute(block, axis, [(i, i ^ o) for i in range(size)]) if o else block
        for block, o in zip(blocks, offsets(size))
    ]


def gather_kernel(towers, intra, count, owner_hbm, emb_hbm, *rest):
    small, rest = rest[:count], rest[count:]
    outs, rest = rest[:intra], rest[intra:]
    copies, (owner_ref, emb_ref, acc_ref, sems) = rest[:count], rest[count:]
    pairs = [(owner_hbm, owner_ref), (emb_hbm, emb_ref), *zip(small, copies)]
    loads = [pltpu.make_async_copy(a, b, sems.at[i]) for i, (a, b) in enumerate(pairs)]
    for load in loads:
        load.start()
    samples, width = emb_ref.shape
    per = samples // (towers * intra)
    me = lax.axis_index("intra")
    loads[0].wait()
    owner = jnp.broadcast_to(owner_ref[...].reshape(1, samples), (samples, samples))
    picks = lax.broadcasted_iota(jnp.int32, (samples, samples), 0) == owner
    picks = jnp.where(picks, 1.0, 0.0).astype(jnp.bfloat16)
    loads[1].wait()
    acc_ref[...] = lax.dot_general(
        picks, emb_ref[...], (((0,), (0,)), ((), ())), preferred_element_type=jnp.float32
    )
    for o, out in zip(offsets(intra), outs):
        block = me ^ o
        starts = [pl.multiple_of((t * intra + block) * per, per) for t in range(towers)]
        for f in range(width // EDIM):
            columns = slice(f * EDIM, (f + 1) * EDIM)
            rows = [acc_ref[pl.ds(start, per), columns] for start in starts]
            out[f] = jnp.concatenate(rows, axis=0).astype(out.dtype)
    for load in loads[2:]:
        load.wait()


def gather_blocks(owner, embeddings, small, towers, intra, ahead):
    samples, width = embeddings.shape
    rows, held = samples // intra, width // EDIM
    if samples <= FEW_SAMPLES:
        count = len(small)
        shape = pltpu.VMEM((held, rows, EDIM), embeddings.dtype)
        given = [pltpu.with_memory_space_constraint(a, pltpu.HBM) for a in (owner, embeddings, *small)]
        spaces = [pltpu.SMEM if jnp.issubdtype(a.dtype, jnp.integer) else pltpu.VMEM for a in small]
        results = pl.pallas_call(
            functools.partial(gather_kernel, towers, intra, count),
            out_shape=[shape] * intra + [space(a.shape, a.dtype) for space, a in zip(spaces, small)],
            in_specs=[pl.BlockSpec(memory_space=pltpu.HBM)] * len(given),
            out_specs=[pl.BlockSpec(memory_space=pltpu.VMEM)] * intra
            + [pl.BlockSpec(memory_space=space) for space in spaces],
            scratch_shapes=[
                pltpu.VMEM(owner.shape, owner.dtype),
                pltpu.VMEM(embeddings.shape, embeddings.dtype),
                pltpu.VMEM((samples, width), jnp.float32),
                pltpu.SemaphoreType.DMA((len(given),)),
            ],
            compiler_params=pltpu.CompilerParams(vmem_limit_bytes=8 << 20),
            cost_estimate=pl.CostEstimate(flops=ahead, bytes_accessed=0, transcendentals=0),
            name="gather_rows",
        )(*given)
        return results[:intra], results[intra:]
    order = owner.reshape(towers, intra, -1).transpose(1, 0, 2).reshape(-1)
    blocks = jnp.take(embeddings, order, axis=0).reshape(intra, rows, held, EDIM).transpose(0, 2, 1, 3)
    me = lax.axis_index("intra")
    return [lax.dynamic_index_in_dim(blocks, me ^ o, keepdims=False) for o in offsets(intra)], small


def tower_kernel(towers, intra, assign_ref, w1_ref, b1_ref, w2_ref, b2_ref, *rest):
    blocks, outs = rest[:intra], rest[intra : intra + towers]
    pool_ref, x_ref, y_ref = rest[intra + towers :]
    held, rows, _ = blocks[0].shape
    count, depth, _ = w1_ref.shape
    vectors = w2_ref.shape[2] // EDIM
    per = rows // towers
    slots = depth // EDIM
    me = lax.axis_index("intra")
    for o, block in zip(offsets(intra), blocks):
        pool_ref[pl.ds((me ^ o) * held, held)] = block[...]
    for k in range(count):
        for j in range(slots):
            x_ref[k, :, j * EDIM : (j + 1) * EDIM] = pool_ref[assign_ref[0, k * slots + j]]
    for k in range(count):
        hidden = jnp.dot(x_ref[k], w1_ref[k], preferred_element_type=jnp.float32)
        hidden = jnp.maximum(hidden + b1_ref[k : k + 1, :], 0.0).astype(jnp.bfloat16)
        result = jnp.dot(hidden, w2_ref[k], preferred_element_type=jnp.float32)
        y_ref[k] = jnp.maximum(result + b2_ref[k : k + 1, :], 0.0)
    place = lax.axis_index("tower")
    for o, out in zip(offsets(towers), outs):
        start = pl.multiple_of((place ^ o) * per, per)
        pieces = [
            y_ref[k, pl.ds(start, per), v * EDIM : (v + 1) * EDIM]
            for k in range(count)
            for v in range(vectors)
        ]
        out[...] = jnp.concatenate(pieces, axis=0).astype(out.dtype)


def run_towers(assign, w1, b1, w2, b2, blocks, towers):
    intra = len(blocks)
    held, rows, _ = blocks[0].shape
    count, depth, _ = w1.shape
    width = w2.shape[2]
    local = count * (width // EDIM) * (rows // towers)
    w1 = pltpu.with_memory_space_constraint(w1, pltpu.VMEM)
    w2 = pltpu.with_memory_space_constraint(w2, pltpu.VMEM)
    return pl.pallas_call(
        functools.partial(tower_kernel, towers, intra),
        out_shape=[jax.ShapeDtypeStruct((local, EDIM), jnp.bfloat16)] * towers,
        in_specs=[pl.BlockSpec(memory_space=pltpu.SMEM)]
        + [pl.BlockSpec(memory_space=pltpu.VMEM)] * (4 + intra),
        out_specs=[pl.BlockSpec(memory_space=pltpu.VMEM)] * towers,
        scratch_shapes=[
            pltpu.VMEM((intra * held, rows, EDIM), jnp.bfloat16),
            pltpu.VMEM((count, rows, depth), jnp.bfloat16),
            pltpu.VMEM((count, rows, width), jnp.float32),
        ],
        compiler_params=pltpu.CompilerParams(vmem_limit_bytes=16 << 20),
        name="towers",
    )(assign, w1, b1, w2, b2, *blocks)


def interact_kernel(towers, proj_ref, *rest):
    blocks, out, all_ref = rest[:towers], rest[towers], rest[towers + 1]
    per, count, _ = out.shape
    local = blocks[0].shape[0]
    place = lax.axis_index("tower")
    for o, block in zip(offsets(towers), blocks):
        start = pl.multiple_of((place ^ o) * local, local)
        all_ref[pl.ds(start, local), :] = block[...].astype(jnp.float32)
    group = max(1, min(per, 128 // count))
    proj = jnp.concatenate([proj_ref[...]] * (2 * group), axis=0)
    for first in range(0, per, group):
        samples = range(first, first + group)
        vectors = [all_ref[pl.ds(d, count, stride=per), :] for d in samples]
        vectors = jnp.concatenate(vectors, axis=0).astype(jnp.bfloat16)
        gram = lax.dot_general(
            vectors, vectors, (((1,), (1,)), ((), ())), preferred_element_type=jnp.float32
        )
        gram = gram * (1.0 / EDIM)
        column = lax.broadcasted_iota(jnp.int32, (count, gram.shape[1]), 1)
        own = [
            jnp.where(
                (column >= g * count) & (column < (g + 1) * count),
                gram[g * count : (g + 1) * count, :],
                0.0,
            )
            for g in range(group)
        ]
        gram = jnp.concatenate(own, axis=0)
        high = gram.astype(jnp.bfloat16)
        low = (gram - high.astype(jnp.float32)).astype(jnp.bfloat16)
        result = jnp.dot(
            jnp.concatenate([high, low], axis=1), proj, preferred_element_type=jnp.float32
        )
        for g, d in enumerate(samples):
            out[d] = result[g * count : (g + 1) * count, :].astype(out.dtype)


def interact(proj, blocks):
    towers = len(blocks)
    local = blocks[0].shape[0]
    count = proj.shape[0]
    per = towers * local // count
    return pl.pallas_call(
        functools.partial(interact_kernel, towers),
        out_shape=jax.ShapeDtypeStruct((per, count, EDIM), jnp.bfloat16),
        in_specs=[pl.BlockSpec(memory_space=pltpu.VMEM)] * (1 + towers),
        out_specs=pl.BlockSpec(memory_space=pltpu.VMEM),
        scratch_shapes=[pltpu.VMEM((towers * local, EDIM), jnp.float32)],
        compiler_params=pltpu.CompilerParams(vmem_limit_bytes=8 << 20),
        name="interact",
    )(proj, *blocks)


def shards(
    embeddings,
    feature_assign,
    sample_owner,
    first_weight,
    first_bias,
    tower_weight,
    tower_bias,
    proj_weight,
):
    towers, intra = lax.axis_size("tower"), lax.axis_size("intra")
    small = (feature_assign, first_bias, tower_bias, proj_weight)
    ahead = 10_000 * (first_weight.size + tower_weight.size)
    blocks, small = gather_blocks(sample_owner, embeddings, small, towers, intra, ahead)
    feature_assign, first_bias, tower_bias, proj_weight = small
    blocks = exchange(blocks, "intra", intra)
    vectors = run_towers(
        feature_assign, first_weight, first_bias, tower_weight, tower_bias, blocks, towers
    )
    vectors = exchange(vectors, "tower", towers)
    return interact(proj_weight, vectors)


def solution(mesh):
    return jax.shard_map(
        shards,
        mesh=mesh,
        in_specs=(
            P(None, ("tower", "intra")),
            P("tower", None),
            P(),
            P("tower", None, None),
            P("tower", None),
            P("tower", None, None),
            P("tower", None),
            P(),
        ),
        out_specs=P(("tower", "intra"), None, None),
        check_vma=False,
    )
```

```python
import functools

import jax
import jax.numpy as jnp
from jax import lax
from jax.experimental import pallas as pl
from jax.experimental.pallas import tpu as pltpu
from jax.sharding import PartitionSpec as P

EDIM = 128
FEW_SAMPLES = 1024


def offsets(size):
    return range(size - 1, -1, -1)


def exchange(blocks, axis, size):
    return [
        lax.ppermute(block, axis, [(i, i ^ o) for i in range(size)]) if o else block
        for block, o in zip(blocks, offsets(size))
    ]


def other_core(intra):
    return 1 if intra > 1 else 0


def exchange_groups(blocks, towers, intra):
    received = []
    for block, o in zip(blocks, offsets(towers)):
        pairs = [
            (t * intra + i, (t ^ o) * intra + (i ^ other_core(intra)))
            for t in range(towers)
            for i in range(intra)
        ]
        received.append(lax.ppermute(block, ("tower", "intra"), pairs) if o else block)
    return received


def gather_kernel(towers, intra, count, owner_hbm, emb_hbm, *rest):
    small, rest = rest[:count], rest[count:]
    outs, rest = rest[:intra], rest[intra:]
    copies, (owner_ref, emb_ref, acc_ref, sems) = rest[:count], rest[count:]
    pairs = [(owner_hbm, owner_ref), (emb_hbm, emb_ref), *zip(small, copies)]
    loads = [pltpu.make_async_copy(a, b, sems.at[i]) for i, (a, b) in enumerate(pairs)]
    for load in loads:
        load.start()
    samples, width = emb_ref.shape
    per = samples // (towers * intra)
    me, place = lax.axis_index("intra"), lax.axis_index("tower")
    loads[0].wait()
    owner = jnp.broadcast_to(owner_ref[...].reshape(1, samples), (samples, samples))
    picks = lax.broadcasted_iota(jnp.int32, (samples, samples), 0) == owner
    picks = jnp.where(picks, 1.0, 0.0).astype(jnp.bfloat16)
    loads[1].wait()
    acc_ref[...] = lax.dot_general(
        picks, emb_ref[...], (((0,), (0,)), ((), ())), preferred_element_type=jnp.float32
    )
    for o, out in zip(offsets(intra), outs):
        block = me ^ o
        owners = [jnp.where(place == t, block, block ^ other_core(intra)) for t in range(towers)]
        starts = [pl.multiple_of((t * intra + owners[t]) * per, per) for t in range(towers)]
        for f in range(width // EDIM):
            columns = slice(f * EDIM, (f + 1) * EDIM)
            rows = [acc_ref[pl.ds(start, per), columns] for start in starts]
            out[f] = jnp.concatenate(rows, axis=0).astype(out.dtype)
    for load in loads[2:]:
        load.wait()


def gather_blocks(owner, embeddings, small, towers, intra, ahead):
    samples, width = embeddings.shape
    rows, held = samples // intra, width // EDIM
    if samples <= FEW_SAMPLES:
        count = len(small)
        shape = pltpu.VMEM((held, rows, EDIM), embeddings.dtype)
        given = [pltpu.with_memory_space_constraint(a, pltpu.HBM) for a in (owner, embeddings, *small)]
        spaces = [pltpu.SMEM if jnp.issubdtype(a.dtype, jnp.integer) else pltpu.VMEM for a in small]
        results = pl.pallas_call(
            functools.partial(gather_kernel, towers, intra, count),
            out_shape=[shape] * intra + [space(a.shape, a.dtype) for space, a in zip(spaces, small)],
            in_specs=[pl.BlockSpec(memory_space=pltpu.HBM)] * len(given),
            out_specs=[pl.BlockSpec(memory_space=pltpu.VMEM)] * intra
            + [pl.BlockSpec(memory_space=space) for space in spaces],
            scratch_shapes=[
                pltpu.VMEM(owner.shape, owner.dtype),
                pltpu.VMEM(embeddings.shape, embeddings.dtype),
                pltpu.VMEM((samples, width), jnp.float32),
                pltpu.SemaphoreType.DMA((len(given),)),
            ],
            compiler_params=pltpu.CompilerParams(vmem_limit_bytes=8 << 20),
            cost_estimate=pl.CostEstimate(flops=ahead, bytes_accessed=0, transcendentals=0),
            name="gather_rows",
        )(*given)
        return results[:intra], results[intra:]
    order = owner.reshape(towers, intra, -1)
    crossed = order[:, jnp.arange(intra) ^ other_core(intra)]
    own = jnp.arange(towers)[:, None, None] == lax.axis_index("tower")
    order = jnp.where(own, order, crossed).transpose(1, 0, 2).reshape(-1)
    blocks = jnp.take(embeddings, order, axis=0).reshape(intra, rows, held, EDIM).transpose(0, 2, 1, 3)
    me = lax.axis_index("intra")
    return [lax.dynamic_index_in_dim(blocks, me ^ o, keepdims=False) for o in offsets(intra)], small


def tower_kernel(towers, intra, assign_ref, w1_ref, b1_ref, w2_ref, b2_ref, *rest):
    blocks, outs = rest[:intra], rest[intra : intra + towers]
    pool_ref, x_ref, y_ref = rest[intra + towers :]
    held, rows, _ = blocks[0].shape
    count, depth, _ = w1_ref.shape
    vectors = w2_ref.shape[2] // EDIM
    per = rows // towers
    slots = depth // EDIM
    me = lax.axis_index("intra")
    for o, block in zip(offsets(intra), blocks):
        pool_ref[pl.ds((me ^ o) * held, held)] = block[...]
    for k in range(count):
        for j in range(slots):
            x_ref[k, :, j * EDIM : (j + 1) * EDIM] = pool_ref[assign_ref[0, k * slots + j]]
    for k in range(count):
        hidden = jnp.dot(x_ref[k], w1_ref[k], preferred_element_type=jnp.float32)
        hidden = jnp.maximum(hidden + b1_ref[k : k + 1, :], 0.0).astype(jnp.bfloat16)
        result = jnp.dot(hidden, w2_ref[k], preferred_element_type=jnp.float32)
        y_ref[k] = jnp.maximum(result + b2_ref[k : k + 1, :], 0.0)
    place = lax.axis_index("tower")
    for o, out in zip(offsets(towers), outs):
        start = pl.multiple_of((place ^ o) * per, per)
        pieces = [
            y_ref[k, pl.ds(start, per), v * EDIM : (v + 1) * EDIM]
            for k in range(count)
            for v in range(vectors)
        ]
        out[...] = jnp.concatenate(pieces, axis=0).astype(out.dtype)


def run_towers(assign, w1, b1, w2, b2, blocks, towers):
    intra = len(blocks)
    held, rows, _ = blocks[0].shape
    count, depth, _ = w1.shape
    width = w2.shape[2]
    local = count * (width // EDIM) * (rows // towers)
    w1 = pltpu.with_memory_space_constraint(w1, pltpu.VMEM)
    w2 = pltpu.with_memory_space_constraint(w2, pltpu.VMEM)
    return pl.pallas_call(
        functools.partial(tower_kernel, towers, intra),
        out_shape=[jax.ShapeDtypeStruct((local, EDIM), jnp.bfloat16)] * towers,
        in_specs=[pl.BlockSpec(memory_space=pltpu.SMEM)]
        + [pl.BlockSpec(memory_space=pltpu.VMEM)] * (4 + intra),
        out_specs=[pl.BlockSpec(memory_space=pltpu.VMEM)] * towers,
        scratch_shapes=[
            pltpu.VMEM((intra * held, rows, EDIM), jnp.bfloat16),
            pltpu.VMEM((count, rows, depth), jnp.bfloat16),
            pltpu.VMEM((count, rows, width), jnp.float32),
        ],
        compiler_params=pltpu.CompilerParams(vmem_limit_bytes=16 << 20),
        name="towers",
    )(assign, w1, b1, w2, b2, *blocks)


def interact_kernel(towers, proj_ref, *rest):
    blocks, out, all_ref = rest[:towers], rest[towers], rest[towers + 1]
    per, count, _ = out.shape
    local = blocks[0].shape[0]
    place = lax.axis_index("tower")
    for o, block in zip(offsets(towers), blocks):
        start = pl.multiple_of((place ^ o) * local, local)
        all_ref[pl.ds(start, local), :] = block[...].astype(jnp.float32)
    group = max(1, min(per, 128 // count))
    proj = jnp.concatenate([proj_ref[...]] * (2 * group), axis=0)
    for first in range(0, per, group):
        samples = range(first, first + group)
        vectors = [all_ref[pl.ds(d, count, stride=per), :] for d in samples]
        vectors = jnp.concatenate(vectors, axis=0).astype(jnp.bfloat16)
        gram = lax.dot_general(
            vectors, vectors, (((1,), (1,)), ((), ())), preferred_element_type=jnp.float32
        )
        gram = gram * (1.0 / EDIM)
        column = lax.broadcasted_iota(jnp.int32, (count, gram.shape[1]), 1)
        own = [
            jnp.where(
                (column >= g * count) & (column < (g + 1) * count),
                gram[g * count : (g + 1) * count, :],
                0.0,
            )
            for g in range(group)
        ]
        gram = jnp.concatenate(own, axis=0)
        high = gram.astype(jnp.bfloat16)
        low = (gram - high.astype(jnp.float32)).astype(jnp.bfloat16)
        result = jnp.dot(
            jnp.concatenate([high, low], axis=1), proj, preferred_element_type=jnp.float32
        )
        for g, d in enumerate(samples):
            out[d] = result[g * count : (g + 1) * count, :].astype(out.dtype)


def interact(proj, blocks):
    towers = len(blocks)
    local = blocks[0].shape[0]
    count = proj.shape[0]
    per = towers * local // count
    return pl.pallas_call(
        functools.partial(interact_kernel, towers),
        out_shape=jax.ShapeDtypeStruct((per, count, EDIM), jnp.bfloat16),
        in_specs=[pl.BlockSpec(memory_space=pltpu.VMEM)] * (1 + towers),
        out_specs=pl.BlockSpec(memory_space=pltpu.VMEM),
        scratch_shapes=[pltpu.VMEM((towers * local, EDIM), jnp.float32)],
        compiler_params=pltpu.CompilerParams(vmem_limit_bytes=8 << 20),
        name="interact",
    )(proj, *blocks)


def shards(
    embeddings,
    feature_assign,
    sample_owner,
    first_weight,
    first_bias,
    tower_weight,
    tower_bias,
    proj_weight,
):
    towers, intra = lax.axis_size("tower"), lax.axis_size("intra")
    small = (feature_assign, first_bias, tower_bias, proj_weight)
    ahead = 10_000 * (first_weight.size + tower_weight.size)
    blocks, small = gather_blocks(sample_owner, embeddings, small, towers, intra, ahead)
    feature_assign, first_bias, tower_bias, proj_weight = small
    blocks = exchange(blocks, "intra", intra)
    vectors = run_towers(
        feature_assign, first_weight, first_bias, tower_weight, tower_bias, blocks, towers
    )
    vectors = exchange_groups(vectors, towers, intra)
    return interact(proj_weight, vectors)


def solution(mesh):
    return jax.shard_map(
        shards,
        mesh=mesh,
        in_specs=(
            P(None, ("tower", "intra")),
            P("tower", None),
            P(),
            P("tower", None, None),
            P("tower", None),
            P("tower", None, None),
            P("tower", None),
            P(),
        ),
        out_specs=P(("tower", "intra"), None, None),
        check_vma=False,
    )
```

```python
import functools

import jax
import jax.numpy as jnp
from jax import lax
from jax.experimental import pallas as pl
from jax.experimental.pallas import tpu as pltpu
from jax.sharding import PartitionSpec as P

EDIM = 128
FEW_SAMPLES = 1024


def offsets(size, step=1):
    return range(size - step, -1, -step)


def exchange(blocks, axis, size, step=1):
    return [
        lax.ppermute(block, axis, [(i, i ^ o) for i in range(size)]) if o else block
        for block, o in zip(blocks, offsets(size, step))
    ]


def other_core(intra):
    return 1 if intra > 1 else 0


def exchange_groups(blocks, towers, intra):
    received = []
    for block, o in zip(blocks, offsets(towers)):
        pairs = [
            (t * intra + i, (t ^ o) * intra + (i ^ other_core(intra)))
            for t in range(towers)
            for i in range(intra)
        ]
        received.append(lax.ppermute(block, ("tower", "intra"), pairs) if o else block)
    return received


def load_kernel(count, owner_hbm, emb_hbm, *rest):
    small, (picks_ref, emb_ref), copies = rest[:count], rest[count : count + 2], rest[count + 2 : -2]
    owner_ref, sems = rest[-2:]
    pairs = [(owner_hbm, owner_ref), (emb_hbm, emb_ref), *zip(small, copies)]
    loads = [pltpu.make_async_copy(a, b, sems.at[i]) for i, (a, b) in enumerate(pairs)]
    for load in loads:
        load.start()
    samples = emb_ref.shape[0]
    loads[0].wait()
    owner = jnp.broadcast_to(owner_ref[...].reshape(1, samples), (samples, samples))
    picks = lax.broadcasted_iota(jnp.int32, (samples, samples), 0) == owner
    picks_ref[...] = jnp.where(picks, 1.0, 0.0).astype(jnp.bfloat16)
    for load in loads[1:]:
        load.wait()


def gather_kernel(towers, intra, pair, picks_ref, *rest):
    parts, outs, acc_ref = rest[:pair], rest[pair:-1], rest[-1]
    samples, width = parts[0].shape
    per = samples // (towers * intra)
    held = width // EDIM
    me, place = lax.axis_index("intra"), lax.axis_index("tower")
    for q, part in enumerate(parts):
        acc_ref[:, q * width : (q + 1) * width] = lax.dot_general(
            picks_ref[...], part[...], (((0,), (0,)), ((), ())), preferred_element_type=jnp.float32
        )
    for o, out in zip(offsets(intra, pair), outs):
        block = me ^ o
        owners = [jnp.where(place == t, block, block ^ other_core(intra)) for t in range(towers)]
        starts = [pl.multiple_of((t * intra + owners[t]) * per, per) for t in range(towers)]
        for f in range(pair * held):
            columns = slice(f * EDIM, (f + 1) * EDIM)
            rows = [acc_ref[pl.ds(start, per), columns] for start in starts]
            out[f] = jnp.concatenate(rows, axis=0).astype(out.dtype)


def gather_blocks(owner, embeddings, small, towers, intra, pair, ahead):
    samples, width = embeddings.shape
    rows, held = samples // intra, pair * width // EDIM
    parts = [lax.ppermute(embeddings, "intra", [(i, i ^ q) for i in range(intra)]) for q in range(1, pair)]
    if samples <= FEW_SAMPLES:
        given = [pltpu.with_memory_space_constraint(a, pltpu.HBM) for a in (owner, embeddings, *small)]
        spaces = [pltpu.SMEM if jnp.issubdtype(a.dtype, jnp.integer) else pltpu.VMEM for a in small]
        picks, embeddings, *small = pl.pallas_call(
            functools.partial(load_kernel, len(small)),
            out_shape=[
                pltpu.VMEM((samples, samples), jnp.bfloat16),
                pltpu.VMEM(embeddings.shape, embeddings.dtype),
            ]
            + [space(a.shape, a.dtype) for space, a in zip(spaces, small)],
            in_specs=[pl.BlockSpec(memory_space=pltpu.HBM)] * len(given),
            out_specs=[pl.BlockSpec(memory_space=pltpu.VMEM)] * 2
            + [pl.BlockSpec(memory_space=space) for space in spaces],
            scratch_shapes=[
                pltpu.VMEM(owner.shape, owner.dtype),
                pltpu.SemaphoreType.DMA((len(given),)),
            ],
            compiler_params=pltpu.CompilerParams(vmem_limit_bytes=8 << 20),
            cost_estimate=pl.CostEstimate(flops=ahead, bytes_accessed=0, transcendentals=0),
            name="load",
        )(*given)
        blocks = pl.pallas_call(
            functools.partial(gather_kernel, towers, intra, pair),
            out_shape=[pltpu.VMEM((held, rows, EDIM), embeddings.dtype)] * (intra // pair),
            in_specs=[pl.BlockSpec(memory_space=pltpu.VMEM)] * (1 + pair),
            out_specs=[pl.BlockSpec(memory_space=pltpu.VMEM)] * (intra // pair),
            scratch_shapes=[pltpu.VMEM((samples, pair * width), jnp.float32)],
            compiler_params=pltpu.CompilerParams(vmem_limit_bytes=8 << 20),
            name="gather_rows",
        )(picks, embeddings, *parts)
        return blocks, small
    order = owner.reshape(towers, intra, -1)
    crossed = order[:, jnp.arange(intra) ^ other_core(intra)]
    own = jnp.arange(towers)[:, None, None] == lax.axis_index("tower")
    order = jnp.where(own, order, crossed).transpose(1, 0, 2)
    me = lax.axis_index("intra")
    table = jnp.concatenate([embeddings, *parts], axis=1)
    blocks = []
    for o in offsets(intra, pair):
        mine = lax.dynamic_index_in_dim(order, me ^ o, keepdims=False).reshape(-1)
        blocks.append(jnp.take(table, mine, axis=0).reshape(rows, held, EDIM).transpose(1, 0, 2))
    return blocks, small


def tower_kernel(towers, intra, pair, assign_ref, w1_ref, b1_ref, w2_ref, b2_ref, *rest):
    blocks, outs, (pool_ref, x_ref, y_ref) = rest[: intra // pair], rest[intra // pair : -3], rest[-3:]
    held, rows, _ = blocks[0].shape
    held //= pair
    count, depth, _ = w1_ref.shape
    vectors = w2_ref.shape[2] // EDIM
    per = rows // towers
    slots = depth // EDIM
    me = lax.axis_index("intra")
    for o, block in zip(offsets(intra, pair), blocks):
        for q in range(pair):
            pool_ref[pl.ds((me ^ o ^ q) * held, held)] = block[q * held : (q + 1) * held]
    for k in range(count):
        for j in range(slots):
            x_ref[k, :, j * EDIM : (j + 1) * EDIM] = pool_ref[assign_ref[0, k * slots + j]]
    for k in range(count):
        hidden = jnp.dot(x_ref[k], w1_ref[k], preferred_element_type=jnp.float32)
        hidden = jnp.maximum(hidden + b1_ref[k : k + 1, :], 0.0).astype(jnp.bfloat16)
        result = jnp.dot(hidden, w2_ref[k], preferred_element_type=jnp.float32)
        y_ref[k] = jnp.maximum(result + b2_ref[k : k + 1, :], 0.0)
    place = lax.axis_index("tower")
    for o, out in zip(offsets(towers), outs):
        start = pl.multiple_of((place ^ o) * per, per)
        pieces = [
            y_ref[k, pl.ds(start, per), v * EDIM : (v + 1) * EDIM]
            for k in range(count)
            for v in range(vectors)
        ]
        out[...] = jnp.concatenate(pieces, axis=0).astype(out.dtype)


def run_towers(assign, w1, b1, w2, b2, blocks, towers, intra, pair):
    held, rows, _ = blocks[0].shape
    count, depth, _ = w1.shape
    width = w2.shape[2]
    local = count * (width // EDIM) * (rows // towers)
    w1 = pltpu.with_memory_space_constraint(w1, pltpu.VMEM)
    w2 = pltpu.with_memory_space_constraint(w2, pltpu.VMEM)
    return pl.pallas_call(
        functools.partial(tower_kernel, towers, intra, pair),
        out_shape=[jax.ShapeDtypeStruct((local, EDIM), jnp.bfloat16)] * towers,
        in_specs=[pl.BlockSpec(memory_space=pltpu.SMEM)]
        + [pl.BlockSpec(memory_space=pltpu.VMEM)] * (4 + len(blocks)),
        out_specs=[pl.BlockSpec(memory_space=pltpu.VMEM)] * towers,
        scratch_shapes=[
            pltpu.VMEM((len(blocks) * held, rows, EDIM), jnp.bfloat16),
            pltpu.VMEM((count, rows, depth), jnp.bfloat16),
            pltpu.VMEM((count, rows, width), jnp.float32),
        ],
        compiler_params=pltpu.CompilerParams(vmem_limit_bytes=16 << 20),
        name="towers",
    )(assign, w1, b1, w2, b2, *blocks)


def interact_kernel(towers, proj_ref, *rest):
    blocks, out, all_ref = rest[:towers], rest[towers], rest[towers + 1]
    per, count, _ = out.shape
    local = blocks[0].shape[0]
    place = lax.axis_index("tower")
    for o, block in zip(offsets(towers), blocks):
        start = pl.multiple_of((place ^ o) * local, local)
        all_ref[pl.ds(start, local), :] = block[...].astype(jnp.float32)
    group = max(1, min(per, 128 // count))
    proj = jnp.concatenate([proj_ref[...]] * (2 * group), axis=0)
    for first in range(0, per, group):
        samples = range(first, first + group)
        vectors = [all_ref[pl.ds(d, count, stride=per), :] for d in samples]
        vectors = jnp.concatenate(vectors, axis=0).astype(jnp.bfloat16)
        gram = lax.dot_general(
            vectors, vectors, (((1,), (1,)), ((), ())), preferred_element_type=jnp.float32
        )
        gram = gram * (1.0 / EDIM)
        column = lax.broadcasted_iota(jnp.int32, (count, gram.shape[1]), 1)
        own = [
            jnp.where(
                (column >= g * count) & (column < (g + 1) * count),
                gram[g * count : (g + 1) * count, :],
                0.0,
            )
            for g in range(group)
        ]
        gram = jnp.concatenate(own, axis=0)
        high = gram.astype(jnp.bfloat16)
        low = (gram - high.astype(jnp.float32)).astype(jnp.bfloat16)
        result = jnp.dot(
            jnp.concatenate([high, low], axis=1), proj, preferred_element_type=jnp.float32
        )
        for g, d in enumerate(samples):
            out[d] = result[g * count : (g + 1) * count, :].astype(out.dtype)


def interact(proj, blocks):
    towers = len(blocks)
    local = blocks[0].shape[0]
    count = proj.shape[0]
    per = towers * local // count
    return pl.pallas_call(
        functools.partial(interact_kernel, towers),
        out_shape=jax.ShapeDtypeStruct((per, count, EDIM), jnp.bfloat16),
        in_specs=[pl.BlockSpec(memory_space=pltpu.VMEM)] * (1 + towers),
        out_specs=pl.BlockSpec(memory_space=pltpu.VMEM),
        scratch_shapes=[pltpu.VMEM((towers * local, EDIM), jnp.float32)],
        compiler_params=pltpu.CompilerParams(vmem_limit_bytes=8 << 20),
        name="interact",
    )(proj, *blocks)


def shards(
    embeddings,
    feature_assign,
    sample_owner,
    first_weight,
    first_bias,
    tower_weight,
    tower_bias,
    proj_weight,
):
    towers, intra = lax.axis_size("tower"), lax.axis_size("intra")
    small = (feature_assign, first_bias, tower_bias, proj_weight)
    ahead = 10_000 * (first_weight.size + tower_weight.size)
    pair = 2 if intra % 2 == 0 else 1
    blocks, small = gather_blocks(sample_owner, embeddings, small, towers, intra, pair, ahead)
    feature_assign, first_bias, tower_bias, proj_weight = small
    blocks = exchange(blocks, "intra", intra, pair)
    vectors = run_towers(
        feature_assign, first_weight, first_bias, tower_weight, tower_bias, blocks, towers, intra, pair
    )
    vectors = exchange_groups(vectors, towers, intra)
    return interact(proj_weight, vectors)


def solution(mesh):
    return jax.shard_map(
        shards,
        mesh=mesh,
        in_specs=(
            P(None, ("tower", "intra")),
            P("tower", None),
            P(),
            P("tower", None, None),
            P("tower", None),
            P("tower", None, None),
            P("tower", None),
            P(),
        ),
        out_specs=P(("tower", "intra"), None, None),
        check_vma=False,
    )
```

```python
import functools

import jax
import jax.numpy as jnp
from jax import lax
from jax.experimental import pallas as pl
from jax.experimental.pallas import tpu as pltpu
from jax.sharding import PartitionSpec as P

EDIM = 128
FEW_SAMPLES = 1024


def offsets(size, step=1):
    return [o + step - 1 if o else 0 for o in range(size - step, -1, -step)]


def exchange(blocks, axis, size, step=1):
    return [
        lax.ppermute(block, axis, [(i, i ^ o) for i in range(size)]) if o else block
        for block, o in zip(blocks, offsets(size, step))
    ]


def other_core(intra):
    return 1 if intra > 1 else 0


def exchange_groups(blocks, towers, intra):
    received = []
    for block, o in zip(blocks, offsets(towers)):
        pairs = [
            (t * intra + i, (t ^ o) * intra + (i ^ other_core(intra)))
            for t in range(towers)
            for i in range(intra)
        ]
        received.append(lax.ppermute(block, ("tower", "intra"), pairs) if o else block)
    return received


def load_kernel(count, owner_hbm, emb_hbm, *rest):
    small, (picks_ref, emb_ref), copies = rest[:count], rest[count : count + 2], rest[count + 2 : -2]
    owner_ref, sems = rest[-2:]
    pairs = [(owner_hbm, owner_ref), (emb_hbm, emb_ref), *zip(small, copies)]
    loads = [pltpu.make_async_copy(a, b, sems.at[i]) for i, (a, b) in enumerate(pairs)]
    for load in loads:
        load.start()
    samples = emb_ref.shape[0]
    loads[0].wait()
    owner = jnp.broadcast_to(owner_ref[...].reshape(1, samples), (samples, samples))
    picks = lax.broadcasted_iota(jnp.int32, (samples, samples), 0) == owner
    picks_ref[...] = jnp.where(picks, 1.0, 0.0).astype(jnp.bfloat16)
    for load in loads[1:]:
        load.wait()


def gather_kernel(towers, intra, pair, picks_ref, *rest):
    parts, outs, acc_ref = rest[:pair], rest[pair:-1], rest[-1]
    samples, width = parts[0].shape
    per = samples // (towers * intra)
    held = width // EDIM
    me, place = lax.axis_index("intra"), lax.axis_index("tower")
    for q, part in enumerate(parts):
        acc_ref[:, q * width : (q + 1) * width] = lax.dot_general(
            picks_ref[...], part[...], (((0,), (0,)), ((), ())), preferred_element_type=jnp.float32
        )
    for o, out in zip(offsets(intra, pair), outs):
        block = me ^ o
        owners = [jnp.where(place == t, block, block ^ other_core(intra)) for t in range(towers)]
        starts = [pl.multiple_of((t * intra + owners[t]) * per, per) for t in range(towers)]
        for f in range(pair * held):
            columns = slice(f * EDIM, (f + 1) * EDIM)
            rows = [acc_ref[pl.ds(start, per), columns] for start in starts]
            out[f] = jnp.concatenate(rows, axis=0).astype(out.dtype)


def gather_blocks(owner, embeddings, small, towers, intra, pair, ahead):
    samples, width = embeddings.shape
    rows, held = samples // intra, pair * width // EDIM
    parts = [lax.ppermute(embeddings, "intra", [(i, i ^ q) for i in range(intra)]) for q in range(1, pair)]
    if samples <= FEW_SAMPLES:
        given = [pltpu.with_memory_space_constraint(a, pltpu.HBM) for a in (owner, embeddings, *small)]
        spaces = [pltpu.SMEM if jnp.issubdtype(a.dtype, jnp.integer) else pltpu.VMEM for a in small]
        picks, embeddings, *small = pl.pallas_call(
            functools.partial(load_kernel, len(small)),
            out_shape=[
                pltpu.VMEM((samples, samples), jnp.bfloat16),
                pltpu.VMEM(embeddings.shape, embeddings.dtype),
            ]
            + [space(a.shape, a.dtype) for space, a in zip(spaces, small)],
            in_specs=[pl.BlockSpec(memory_space=pltpu.HBM)] * len(given),
            out_specs=[pl.BlockSpec(memory_space=pltpu.VMEM)] * 2
            + [pl.BlockSpec(memory_space=space) for space in spaces],
            scratch_shapes=[
                pltpu.VMEM(owner.shape, owner.dtype),
                pltpu.SemaphoreType.DMA((len(given),)),
            ],
            compiler_params=pltpu.CompilerParams(vmem_limit_bytes=8 << 20),
            name="load",
        )(*given)
        blocks = pl.pallas_call(
            functools.partial(gather_kernel, towers, intra, pair),
            out_shape=[pltpu.VMEM((held, rows, EDIM), embeddings.dtype)] * (intra // pair),
            in_specs=[pl.BlockSpec(memory_space=pltpu.VMEM)] * (1 + pair),
            out_specs=[pl.BlockSpec(memory_space=pltpu.VMEM)] * (intra // pair),
            scratch_shapes=[pltpu.VMEM((samples, pair * width), jnp.float32)],
            compiler_params=pltpu.CompilerParams(vmem_limit_bytes=8 << 20),
            cost_estimate=pl.CostEstimate(flops=ahead, bytes_accessed=0, transcendentals=0),
            name="gather_rows",
        )(picks, embeddings, *parts)
        return blocks, small
    order = owner.reshape(towers, intra, -1)
    crossed = order[:, jnp.arange(intra) ^ other_core(intra)]
    own = jnp.arange(towers)[:, None, None] == lax.axis_index("tower")
    order = jnp.where(own, order, crossed).transpose(1, 0, 2)
    me = lax.axis_index("intra")
    table = jnp.concatenate([embeddings, *parts], axis=1)
    blocks = []
    for o in offsets(intra, pair):
        mine = lax.dynamic_index_in_dim(order, me ^ o, keepdims=False).reshape(-1)
        blocks.append(jnp.take(table, mine, axis=0).reshape(rows, held, EDIM).transpose(1, 0, 2))
    return blocks, small


def tower_kernel(towers, intra, pair, assign_ref, w1_ref, b1_ref, w2_ref, b2_ref, *rest):
    blocks, outs, (pool_ref, x_ref, y_ref) = rest[: intra // pair], rest[intra // pair : -3], rest[-3:]
    held, rows, _ = blocks[0].shape
    held //= pair
    count, depth, _ = w1_ref.shape
    vectors = w2_ref.shape[2] // EDIM
    per = rows // towers
    slots = depth // EDIM
    me = lax.axis_index("intra")
    for o, block in zip(offsets(intra, pair), blocks):
        for q in range(pair):
            pool_ref[pl.ds((me ^ o ^ q) * held, held)] = block[q * held : (q + 1) * held]
    for k in range(count):
        for j in range(slots):
            x_ref[k, :, j * EDIM : (j + 1) * EDIM] = pool_ref[assign_ref[0, k * slots + j]]
    for k in range(count):
        hidden = jnp.dot(x_ref[k], w1_ref[k], preferred_element_type=jnp.float32)
        hidden = jnp.maximum(hidden + b1_ref[k : k + 1, :], 0.0).astype(jnp.bfloat16)
        result = jnp.dot(hidden, w2_ref[k], preferred_element_type=jnp.float32)
        y_ref[k] = jnp.maximum(result + b2_ref[k : k + 1, :], 0.0)
    place = lax.axis_index("tower")
    for o, out in zip(offsets(towers), outs):
        start = pl.multiple_of((place ^ o) * per, per)
        pieces = [
            y_ref[k, pl.ds(start, per), v * EDIM : (v + 1) * EDIM]
            for k in range(count)
            for v in range(vectors)
        ]
        out[...] = jnp.concatenate(pieces, axis=0).astype(out.dtype)


def run_towers(assign, w1, b1, w2, b2, blocks, towers, intra, pair):
    held, rows, _ = blocks[0].shape
    count, depth, _ = w1.shape
    width = w2.shape[2]
    local = count * (width // EDIM) * (rows // towers)
    w1 = pltpu.with_memory_space_constraint(w1, pltpu.VMEM)
    w2 = pltpu.with_memory_space_constraint(w2, pltpu.VMEM)
    return pl.pallas_call(
        functools.partial(tower_kernel, towers, intra, pair),
        out_shape=[jax.ShapeDtypeStruct((local, EDIM), jnp.bfloat16)] * towers,
        in_specs=[pl.BlockSpec(memory_space=pltpu.SMEM)]
        + [pl.BlockSpec(memory_space=pltpu.VMEM)] * (4 + len(blocks)),
        out_specs=[pl.BlockSpec(memory_space=pltpu.VMEM)] * towers,
        scratch_shapes=[
            pltpu.VMEM((len(blocks) * held, rows, EDIM), jnp.bfloat16),
            pltpu.VMEM((count, rows, depth), jnp.bfloat16),
            pltpu.VMEM((count, rows, width), jnp.float32),
        ],
        compiler_params=pltpu.CompilerParams(vmem_limit_bytes=16 << 20),
        name="towers",
    )(assign, w1, b1, w2, b2, *blocks)


def interact_kernel(towers, proj_ref, *rest):
    blocks, out, all_ref = rest[:towers], rest[towers], rest[towers + 1]
    per, count, _ = out.shape
    local = blocks[0].shape[0]
    place = lax.axis_index("tower")
    for o, block in zip(offsets(towers), blocks):
        start = pl.multiple_of((place ^ o) * local, local)
        all_ref[pl.ds(start, local), :] = block[...].astype(jnp.float32)
    group = max(1, min(per, 128 // count))
    proj = jnp.concatenate([proj_ref[...]] * (2 * group), axis=0)
    for first in range(0, per, group):
        samples = range(first, first + group)
        vectors = [all_ref[pl.ds(d, count, stride=per), :] for d in samples]
        vectors = jnp.concatenate(vectors, axis=0).astype(jnp.bfloat16)
        gram = lax.dot_general(
            vectors, vectors, (((1,), (1,)), ((), ())), preferred_element_type=jnp.float32
        )
        gram = gram * (1.0 / EDIM)
        column = lax.broadcasted_iota(jnp.int32, (count, gram.shape[1]), 1)
        own = [
            jnp.where(
                (column >= g * count) & (column < (g + 1) * count),
                gram[g * count : (g + 1) * count, :],
                0.0,
            )
            for g in range(group)
        ]
        gram = jnp.concatenate(own, axis=0)
        high = gram.astype(jnp.bfloat16)
        low = (gram - high.astype(jnp.float32)).astype(jnp.bfloat16)
        result = jnp.dot(
            jnp.concatenate([high, low], axis=1), proj, preferred_element_type=jnp.float32
        )
        for g, d in enumerate(samples):
            out[d] = result[g * count : (g + 1) * count, :].astype(out.dtype)


def interact(proj, blocks):
    towers = len(blocks)
    local = blocks[0].shape[0]
    count = proj.shape[0]
    per = towers * local // count
    return pl.pallas_call(
        functools.partial(interact_kernel, towers),
        out_shape=jax.ShapeDtypeStruct((per, count, EDIM), jnp.bfloat16),
        in_specs=[pl.BlockSpec(memory_space=pltpu.VMEM)] * (1 + towers),
        out_specs=pl.BlockSpec(memory_space=pltpu.VMEM),
        scratch_shapes=[pltpu.VMEM((towers * local, EDIM), jnp.float32)],
        compiler_params=pltpu.CompilerParams(vmem_limit_bytes=8 << 20),
        name="interact",
    )(proj, *blocks)


def shards(
    embeddings,
    feature_assign,
    sample_owner,
    first_weight,
    first_bias,
    tower_weight,
    tower_bias,
    proj_weight,
):
    towers, intra = lax.axis_size("tower"), lax.axis_size("intra")
    small = (feature_assign, first_bias, tower_bias, proj_weight)
    ahead = 10_000 * (first_weight.size + tower_weight.size)
    pair = 2 if intra % 2 == 0 else 1
    blocks, small = gather_blocks(sample_owner, embeddings, small, towers, intra, pair, ahead)
    feature_assign, first_bias, tower_bias, proj_weight = small
    blocks = exchange(blocks, "intra", intra, pair)
    vectors = run_towers(
        feature_assign, first_weight, first_bias, tower_weight, tower_bias, blocks, towers, intra, pair
    )
    vectors = exchange_groups(vectors, towers, intra)
    return interact(proj_weight, vectors)


def solution(mesh):
    return jax.shard_map(
        shards,
        mesh=mesh,
        in_specs=(
            P(None, ("tower", "intra")),
            P("tower", None),
            P(),
            P("tower", None, None),
            P("tower", None),
            P("tower", None, None),
            P("tower", None),
            P(),
        ),
        out_specs=P(("tower", "intra"), None, None),
        check_vma=False,
    )
```

```python
import functools

import jax
import jax.numpy as jnp
from jax import lax
from jax.experimental import pallas as pl
from jax.experimental.pallas import tpu as pltpu
from jax.sharding import PartitionSpec as P

EDIM = 128
FEW_SAMPLES = 1024


def offsets(size, step=1):
    return [o + step - 1 if o else 0 for o in range(size - step, -1, -step)]


def exchange(blocks, axis, size, step=1):
    return [
        lax.ppermute(block, axis, [(i, i ^ o) for i in range(size)]) if o else block
        for block, o in zip(blocks, offsets(size, step))
    ]


def other_core(intra):
    return 1 if intra > 1 else 0


def exchange_groups(blocks, towers, intra):
    received = []
    for block, o in zip(blocks, offsets(towers)):
        pairs = [
            (t * intra + i, (t ^ o) * intra + (i ^ other_core(intra)))
            for t in range(towers)
            for i in range(intra)
        ]
        received.append(lax.ppermute(block, ("tower", "intra"), pairs) if o else block)
    return received


def load_kernel(count, owner_hbm, emb_hbm, *rest):
    small, (picks_ref, emb_ref, slots_ref), copies = rest[:count], rest[count : count + 3], rest[count + 3 : -3]
    owner_ref, assign_ref, sems = rest[-3:]
    targets = (assign_ref, *copies)
    pairs = [(owner_hbm, owner_ref), (emb_hbm, emb_ref), *zip(small, targets)]
    loads = [pltpu.make_async_copy(a, b, sems.at[i]) for i, (a, b) in enumerate(pairs)]
    for load in loads:
        load.start()
    samples = emb_ref.shape[0]
    loads[0].wait()
    owner = jnp.broadcast_to(owner_ref[...].reshape(1, samples), (samples, samples))
    picks = lax.broadcasted_iota(jnp.int32, (samples, samples), 0) == owner
    picks_ref[...] = jnp.where(picks, 1.0, 0.0).astype(jnp.bfloat16)
    loads[2].wait()
    for slot in range(assign_ref.shape[1]):
        slots_ref[0, assign_ref[0, slot]] = slot
    for load in (loads[1], *loads[3:]):
        load.wait()


def gather_kernel(towers, intra, pair, picks_ref, *rest):
    parts, outs, acc_ref = rest[:pair], rest[pair:-1], rest[-1]
    samples, width = parts[0].shape
    per = samples // (towers * intra)
    held = width // EDIM
    me, place = lax.axis_index("intra"), lax.axis_index("tower")
    for q, part in enumerate(parts):
        acc_ref[:, q * width : (q + 1) * width] = lax.dot_general(
            picks_ref[...], part[...], (((0,), (0,)), ((), ())), preferred_element_type=jnp.float32
        )
    for o, out in zip(offsets(intra, pair), outs):
        block = me ^ o
        owners = [jnp.where(place == t, block, block ^ other_core(intra)) for t in range(towers)]
        starts = [pl.multiple_of((t * intra + owners[t]) * per, per) for t in range(towers)]
        for f in range(pair * held):
            columns = slice(f * EDIM, (f + 1) * EDIM)
            rows = [acc_ref[pl.ds(start, per), columns] for start in starts]
            out[f] = jnp.concatenate(rows, axis=0).astype(out.dtype)


def gather_blocks(owner, embeddings, small, towers, intra, pair, ahead):
    samples, width = embeddings.shape
    rows, held = samples // intra, pair * width // EDIM
    parts = [lax.ppermute(embeddings, "intra", [(i, i ^ q) for i in range(intra)]) for q in range(1, pair)]
    if samples <= FEW_SAMPLES:
        given = [pltpu.with_memory_space_constraint(a, pltpu.HBM) for a in (owner, embeddings, *small)]
        picks, embeddings, *small = pl.pallas_call(
            functools.partial(load_kernel, len(small)),
            out_shape=[
                pltpu.VMEM((samples, samples), jnp.bfloat16),
                pltpu.VMEM(embeddings.shape, embeddings.dtype),
                pltpu.SMEM(small[0].shape, small[0].dtype),
            ]
            + [pltpu.VMEM(a.shape, a.dtype) for a in small[1:]],
            in_specs=[pl.BlockSpec(memory_space=pltpu.HBM)] * len(given),
            out_specs=[pl.BlockSpec(memory_space=pltpu.VMEM)] * 2
            + [pl.BlockSpec(memory_space=pltpu.SMEM)]
            + [pl.BlockSpec(memory_space=pltpu.VMEM)] * (len(small) - 1),
            scratch_shapes=[
                pltpu.VMEM(owner.shape, owner.dtype),
                pltpu.SMEM(small[0].shape, small[0].dtype),
                pltpu.SemaphoreType.DMA((len(given),)),
            ],
            compiler_params=pltpu.CompilerParams(vmem_limit_bytes=8 << 20),
            name="load",
        )(*given)
        blocks = pl.pallas_call(
            functools.partial(gather_kernel, towers, intra, pair),
            out_shape=[pltpu.VMEM((held, rows, EDIM), embeddings.dtype)] * (intra // pair),
            in_specs=[pl.BlockSpec(memory_space=pltpu.VMEM)] * (1 + pair),
            out_specs=[pl.BlockSpec(memory_space=pltpu.VMEM)] * (intra // pair),
            scratch_shapes=[pltpu.VMEM((samples, pair * width), jnp.float32)],
            compiler_params=pltpu.CompilerParams(vmem_limit_bytes=8 << 20),
            cost_estimate=pl.CostEstimate(flops=ahead, bytes_accessed=0, transcendentals=0),
            name="gather_rows",
        )(picks, embeddings, *parts)
        return blocks, small
    order = owner.reshape(towers, intra, -1)
    crossed = order[:, jnp.arange(intra) ^ other_core(intra)]
    own = jnp.arange(towers)[:, None, None] == lax.axis_index("tower")
    order = jnp.where(own, order, crossed).transpose(1, 0, 2)
    me = lax.axis_index("intra")
    table = jnp.concatenate([embeddings, *parts], axis=1)
    blocks = []
    for o in offsets(intra, pair):
        mine = lax.dynamic_index_in_dim(order, me ^ o, keepdims=False).reshape(-1)
        blocks.append(jnp.take(table, mine, axis=0).reshape(rows, held, EDIM).transpose(1, 0, 2))
    assign = small[0][0]
    same = assign[None, :] == jnp.arange(assign.size)[:, None]
    slots = jnp.sum(jnp.where(same, jnp.arange(assign.size)[None, :], 0), axis=1)
    return blocks, (slots.astype(assign.dtype)[None, :], *small[1:])


def first_layer(intra, pair, order, slots_ref, w1_ref, x_ref, blocks, before_ref=None):
    held, rows, _ = blocks[0].shape
    held //= pair
    count, depth, hid = w1_ref.shape
    per_tower = depth // EDIM
    me = lax.axis_index("intra")
    slots = []
    for o, block in zip(order, blocks):
        for q in range(pair):
            for f in range(held):
                slot = slots_ref[0, (me ^ o ^ q) * held + f]
                n = len(slots)
                slots.append((slot // per_tower, pl.multiple_of((slot % per_tower) * EDIM, EDIM)))
                for k in range(count):
                    own = jnp.where(slots[n][0] == k, 1.0, 0.0).astype(jnp.bfloat16)
                    x_ref[k * rows : (k + 1) * rows, n * EDIM : (n + 1) * EDIM] = block[q * held + f] * own
    wide = 2 * EDIM
    for h in range(0, hid, wide):
        columns = slice(h, min(h + wide, hid))
        total = None if before_ref is None else before_ref[:, columns]
        for n in range(0, len(slots), 2):
            some = slots[n : n + 2]
            weight = [w1_ref[k, pl.ds(start, EDIM), columns] for k, start in some]
            term = jnp.dot(
                x_ref[:, n * EDIM : (n + len(some)) * EDIM],
                jnp.concatenate(weight, axis=0),
                preferred_element_type=jnp.float32,
            )
            total = term if total is None else total + term
        yield columns, total


def early_kernel(intra, pair, order, slots_ref, w1_ref, *rest):
    blocks, out_ref, x_ref = rest[:-2], rest[-2], rest[-1]
    for columns, total in first_layer(intra, pair, order, slots_ref, w1_ref, x_ref, blocks):
        out_ref[:, columns] = total


def tower_kernel(towers, intra, pair, order, slots_ref, w1_ref, b1_ref, w2_ref, b2_ref, sums_ref, *rest):
    blocks, outs, (x_ref, hidden_ref, y_ref) = rest[: len(order)], rest[len(order) : -3], rest[-3:]
    count, rows, _ = y_ref.shape
    vectors = w2_ref.shape[2] // EDIM
    per = rows // towers
    for columns, total in first_layer(intra, pair, order, slots_ref, w1_ref, x_ref, blocks, sums_ref):
        for k in range(count):
            hidden = total[k * rows : (k + 1) * rows] + b1_ref[k : k + 1, columns]
            hidden_ref[k, :, columns] = jnp.maximum(hidden, 0.0).astype(jnp.bfloat16)
    for k in range(count):
        result = jnp.dot(hidden_ref[k], w2_ref[k], preferred_element_type=jnp.float32)
        y_ref[k] = jnp.maximum(result + b2_ref[k : k + 1, :], 0.0)
    place = lax.axis_index("tower")
    for o, out in zip(offsets(towers), outs):
        start = pl.multiple_of((place ^ o) * per, per)
        pieces = [
            y_ref[k, pl.ds(start, per), v * EDIM : (v + 1) * EDIM]
            for k in range(count)
            for v in range(vectors)
        ]
        out[...] = jnp.concatenate(pieces, axis=0).astype(out.dtype)


def run_towers(slots, w1, b1, w2, b2, blocks, towers, intra, pair):
    order = offsets(intra, pair)
    first = max(len(blocks) // 2 - 1, 0)
    early, late = (*blocks[:first], blocks[-1]), tuple(blocks[first:-1])
    held, rows, _ = blocks[0].shape
    count, depth, hid = w1.shape
    width = w2.shape[2]
    local = count * (width // EDIM) * (rows // towers)
    w1 = pltpu.with_memory_space_constraint(w1, pltpu.VMEM)
    w2 = pltpu.with_memory_space_constraint(w2, pltpu.VMEM)
    params = pltpu.CompilerParams(vmem_limit_bytes=16 << 20)
    sums = pl.pallas_call(
        functools.partial(early_kernel, intra, pair, (*order[:first], order[-1])),
        out_shape=pltpu.VMEM((count * rows, hid), jnp.float32),
        in_specs=[pl.BlockSpec(memory_space=pltpu.SMEM)]
        + [pl.BlockSpec(memory_space=pltpu.VMEM)] * (1 + len(early)),
        out_specs=pl.BlockSpec(memory_space=pltpu.VMEM),
        scratch_shapes=[pltpu.VMEM((count * rows, len(early) * held * EDIM), jnp.bfloat16)],
        compiler_params=params,
        cost_estimate=pl.CostEstimate(
            flops=2 * count * rows * depth * hid, bytes_accessed=0, transcendentals=0
        ),
        name="towers_early",
    )(slots, w1, *early)
    return pl.pallas_call(
        functools.partial(tower_kernel, towers, intra, pair, order[first:-1]),
        out_shape=[pltpu.VMEM((local, EDIM), jnp.bfloat16)] * towers,
        in_specs=[pl.BlockSpec(memory_space=pltpu.SMEM)]
        + [pl.BlockSpec(memory_space=pltpu.VMEM)] * (5 + len(late)),
        out_specs=[pl.BlockSpec(memory_space=pltpu.VMEM)] * towers,
        scratch_shapes=[
            pltpu.VMEM((count * rows, max(len(late), 1) * held * EDIM), jnp.bfloat16),
            pltpu.VMEM((count, rows, hid), jnp.bfloat16),
            pltpu.VMEM((count, rows, width), jnp.float32),
        ],
        compiler_params=params,
        name="towers",
    )(slots, w1, b1, w2, b2, sums, *late)


def interact_kernel(towers, proj_ref, *rest):
    blocks, out, all_ref = rest[:towers], rest[towers], rest[towers + 1]
    per, count, _ = out.shape
    local = blocks[0].shape[0]
    place = lax.axis_index("tower")
    for o, block in zip(offsets(towers), blocks):
        start = pl.multiple_of((place ^ o) * local, local)
        all_ref[pl.ds(start, local), :] = block[...].astype(jnp.float32)
    group = max(1, min(per, 128 // count))
    proj = jnp.concatenate([proj_ref[...]] * (2 * group), axis=0)
    for first in range(0, per, group):
        samples = range(first, first + group)
        vectors = [all_ref[pl.ds(d, count, stride=per), :] for d in samples]
        vectors = jnp.concatenate(vectors, axis=0).astype(jnp.bfloat16)
        gram = lax.dot_general(
            vectors, vectors, (((1,), (1,)), ((), ())), preferred_element_type=jnp.float32
        )
        gram = gram * (1.0 / EDIM)
        column = lax.broadcasted_iota(jnp.int32, (count, gram.shape[1]), 1)
        own = [
            jnp.where(
                (column >= g * count) & (column < (g + 1) * count),
                gram[g * count : (g + 1) * count, :],
                0.0,
            )
            for g in range(group)
        ]
        gram = jnp.concatenate(own, axis=0)
        high = gram.astype(jnp.bfloat16)
        low = (gram - high.astype(jnp.float32)).astype(jnp.bfloat16)
        result = jnp.dot(
            jnp.concatenate([high, low], axis=1), proj, preferred_element_type=jnp.float32
        )
        for g, d in enumerate(samples):
            out[d] = result[g * count : (g + 1) * count, :].astype(out.dtype)


def interact(proj, blocks):
    towers = len(blocks)
    local = blocks[0].shape[0]
    count = proj.shape[0]
    per = towers * local // count
    return pl.pallas_call(
        functools.partial(interact_kernel, towers),
        out_shape=jax.ShapeDtypeStruct((per, count, EDIM), jnp.bfloat16),
        in_specs=[pl.BlockSpec(memory_space=pltpu.VMEM)] * (1 + towers),
        out_specs=pl.BlockSpec(memory_space=pltpu.VMEM),
        scratch_shapes=[pltpu.VMEM((towers * local, EDIM), jnp.float32)],
        compiler_params=pltpu.CompilerParams(vmem_limit_bytes=8 << 20),
        name="interact",
    )(proj, *blocks)


def shards(
    embeddings,
    feature_assign,
    sample_owner,
    first_weight,
    first_bias,
    tower_weight,
    tower_bias,
    proj_weight,
):
    towers, intra = lax.axis_size("tower"), lax.axis_size("intra")
    small = (feature_assign, first_bias, tower_bias, proj_weight)
    ahead = 10_000 * (first_weight.size + tower_weight.size)
    pair = 2 if intra % 2 == 0 else 1
    blocks, small = gather_blocks(sample_owner, embeddings, small, towers, intra, pair, ahead)
    slots, first_bias, tower_bias, proj_weight = small
    blocks = exchange(blocks, "intra", intra, pair)
    vectors = run_towers(
        slots, first_weight, first_bias, tower_weight, tower_bias, blocks, towers, intra, pair
    )
    vectors = exchange_groups(vectors, towers, intra)
    return interact(proj_weight, vectors)


def solution(mesh):
    return jax.shard_map(
        shards,
        mesh=mesh,
        in_specs=(
            P(None, ("tower", "intra")),
            P("tower", None),
            P(),
            P("tower", None, None),
            P("tower", None),
            P("tower", None, None),
            P("tower", None),
            P(),
        ),
        out_specs=P(("tower", "intra"), None, None),
        check_vma=False,
    )
```

```python
import functools

import jax
import jax.numpy as jnp
from jax import lax
from jax.experimental import pallas as pl
from jax.experimental.pallas import tpu as pltpu
from jax.sharding import PartitionSpec as P

EDIM = 128
FEW_SAMPLES = 1024


def offsets(size):
    return range(size - 1, -1, -1)


def steps(intra, pair):
    return (*range(1, intra // pair), 0)


def partner(me, step, intra, pair):
    chips = intra // pair
    return (me // pair + step + chips) % chips * pair + (me % pair + (pair - 1 if step else 0)) % pair


def exchange_chips(blocks, intra, pair):
    return [
        lax.ppermute(block, "intra", [(i, partner(i, s, intra, pair)) for i in range(intra)]) if s else block
        for block, s in zip(blocks, steps(intra, pair))
    ]


def other_core(intra):
    return 1 if intra > 1 else 0


def exchange_groups(blocks, towers, intra):
    received = []
    for block, o in zip(blocks, offsets(towers)):
        pairs = [
            (t * intra + i, (t ^ o) * intra + (i ^ other_core(intra)))
            for t in range(towers)
            for i in range(intra)
        ]
        received.append(lax.ppermute(block, ("tower", "intra"), pairs) if o else block)
    return received


def load_kernel(count, owner_hbm, emb_hbm, *rest):
    small, (picks_ref, emb_ref, slots_ref), copies = rest[:count], rest[count : count + 3], rest[count + 3 : -3]
    owner_ref, assign_ref, sems = rest[-3:]
    targets = (assign_ref, *copies)
    pairs = [(owner_hbm, owner_ref), (emb_hbm, emb_ref), *zip(small, targets)]
    loads = [pltpu.make_async_copy(a, b, sems.at[i]) for i, (a, b) in enumerate(pairs)]
    for load in loads:
        load.start()
    samples = emb_ref.shape[0]
    loads[0].wait()
    owner = jnp.broadcast_to(owner_ref[...].reshape(1, samples), (samples, samples))
    picks = lax.broadcasted_iota(jnp.int32, (samples, samples), 0) == owner
    picks_ref[...] = jnp.where(picks, 1.0, 0.0).astype(jnp.bfloat16)
    loads[2].wait()
    for slot in range(assign_ref.shape[1]):
        slots_ref[0, assign_ref[0, slot]] = slot
    for load in (loads[1], *loads[3:]):
        load.wait()


def gather_kernel(towers, intra, pair, picks_ref, *rest):
    parts, outs, acc_ref = rest[:pair], rest[pair:-1], rest[-1]
    samples, width = parts[0].shape
    per = samples // (towers * intra)
    held = width // EDIM
    me, place = lax.axis_index("intra"), lax.axis_index("tower")
    for q, part in enumerate(parts):
        acc_ref[:, q * width : (q + 1) * width] = lax.dot_general(
            picks_ref[...], part[...], (((0,), (0,)), ((), ())), preferred_element_type=jnp.float32
        )
    for s, out in zip(steps(intra, pair), outs):
        block = partner(me, s, intra, pair)
        owners = [jnp.where(place == t, block, block ^ other_core(intra)) for t in range(towers)]
        starts = [pl.multiple_of((t * intra + owners[t]) * per, per) for t in range(towers)]
        for f in range(pair * held):
            columns = slice(f * EDIM, (f + 1) * EDIM)
            rows = [acc_ref[pl.ds(start, per), columns] for start in starts]
            out[f] = jnp.concatenate(rows, axis=0).astype(out.dtype)


def gather_blocks(owner, embeddings, small, towers, intra, pair, ahead):
    samples, width = embeddings.shape
    rows, held = samples // intra, pair * width // EDIM
    parts = [lax.ppermute(embeddings, "intra", [(i, i ^ q) for i in range(intra)]) for q in range(1, pair)]
    if samples <= FEW_SAMPLES:
        given = [pltpu.with_memory_space_constraint(a, pltpu.HBM) for a in (owner, embeddings, *small)]
        picks, embeddings, *small = pl.pallas_call(
            functools.partial(load_kernel, len(small)),
            out_shape=[
                pltpu.VMEM((samples, samples), jnp.bfloat16),
                pltpu.VMEM(embeddings.shape, embeddings.dtype),
                pltpu.SMEM(small[0].shape, small[0].dtype),
            ]
            + [pltpu.VMEM(a.shape, a.dtype) for a in small[1:]],
            in_specs=[pl.BlockSpec(memory_space=pltpu.HBM)] * len(given),
            out_specs=[pl.BlockSpec(memory_space=pltpu.VMEM)] * 2
            + [pl.BlockSpec(memory_space=pltpu.SMEM)]
            + [pl.BlockSpec(memory_space=pltpu.VMEM)] * (len(small) - 1),
            scratch_shapes=[
                pltpu.VMEM(owner.shape, owner.dtype),
                pltpu.SMEM(small[0].shape, small[0].dtype),
                pltpu.SemaphoreType.DMA((len(given),)),
            ],
            compiler_params=pltpu.CompilerParams(vmem_limit_bytes=8 << 20),
            name="load",
        )(*given)
        blocks = pl.pallas_call(
            functools.partial(gather_kernel, towers, intra, pair),
            out_shape=[pltpu.VMEM((held, rows, EDIM), embeddings.dtype)] * (intra // pair),
            in_specs=[pl.BlockSpec(memory_space=pltpu.VMEM)] * (1 + pair),
            out_specs=[pl.BlockSpec(memory_space=pltpu.VMEM)] * (intra // pair),
            scratch_shapes=[pltpu.VMEM((samples, pair * width), jnp.float32)],
            compiler_params=pltpu.CompilerParams(vmem_limit_bytes=8 << 20),
            cost_estimate=pl.CostEstimate(flops=ahead, bytes_accessed=0, transcendentals=0),
            name="gather_rows",
        )(picks, embeddings, *parts)
        return blocks, small
    order = owner.reshape(towers, intra, -1)
    crossed = order[:, jnp.arange(intra) ^ other_core(intra)]
    own = jnp.arange(towers)[:, None, None] == lax.axis_index("tower")
    order = jnp.where(own, order, crossed).transpose(1, 0, 2)
    me = lax.axis_index("intra")
    table = jnp.concatenate([embeddings, *parts], axis=1)
    blocks = []
    for s in steps(intra, pair):
        mine = lax.dynamic_index_in_dim(order, partner(me, s, intra, pair), keepdims=False).reshape(-1)
        blocks.append(jnp.take(table, mine, axis=0).reshape(rows, held, EDIM).transpose(1, 0, 2))
    assign = small[0][0]
    same = assign[None, :] == jnp.arange(assign.size)[:, None]
    slots = jnp.sum(jnp.where(same, jnp.arange(assign.size)[None, :], 0), axis=1)
    return blocks, (slots.astype(assign.dtype)[None, :], *small[1:])


def first_layer(intra, pair, order, slots_ref, w1_ref, x_ref, blocks, before_ref=None):
    held, rows, _ = blocks[0].shape
    held //= pair
    count, depth, hid = w1_ref.shape
    per_tower = depth // EDIM
    me = lax.axis_index("intra")
    slots = []
    for s, block in zip(order, blocks):
        source = partner(me, -s, intra, pair)
        for q in range(pair):
            for f in range(held):
                slot = slots_ref[0, (source ^ q) * held + f]
                n = len(slots)
                slots.append((slot // per_tower, pl.multiple_of((slot % per_tower) * EDIM, EDIM)))
                for k in range(count):
                    own = jnp.where(slots[n][0] == k, 1.0, 0.0).astype(jnp.bfloat16)
                    x_ref[k * rows : (k + 1) * rows, n * EDIM : (n + 1) * EDIM] = block[q * held + f] * own
    wide = 2 * EDIM
    for h in range(0, hid, wide):
        columns = slice(h, min(h + wide, hid))
        total = None if before_ref is None else before_ref[:, columns]
        for n in range(0, len(slots), 2):
            some = slots[n : n + 2]
            weight = [w1_ref[k, pl.ds(start, EDIM), columns] for k, start in some]
            term = jnp.dot(
                x_ref[:, n * EDIM : (n + len(some)) * EDIM],
                jnp.concatenate(weight, axis=0),
                preferred_element_type=jnp.float32,
            )
            total = term if total is None else total + term
        yield columns, total


def early_kernel(intra, pair, order, slots_ref, w1_ref, *rest):
    blocks, out_ref, x_ref = rest[:-2], rest[-2], rest[-1]
    for columns, total in first_layer(intra, pair, order, slots_ref, w1_ref, x_ref, blocks):
        out_ref[:, columns] = total


def tower_kernel(towers, intra, pair, order, slots_ref, w1_ref, b1_ref, w2_ref, b2_ref, sums_ref, *rest):
    blocks, outs, (x_ref, hidden_ref, y_ref) = rest[: len(order)], rest[len(order) : -3], rest[-3:]
    count, rows, _ = y_ref.shape
    vectors = w2_ref.shape[2] // EDIM
    per = rows // towers
    for columns, total in first_layer(intra, pair, order, slots_ref, w1_ref, x_ref, blocks, sums_ref):
        for k in range(count):
            hidden = total[k * rows : (k + 1) * rows] + b1_ref[k : k + 1, columns]
            hidden_ref[k, :, columns] = jnp.maximum(hidden, 0.0).astype(jnp.bfloat16)
    for k in range(count):
        result = jnp.dot(hidden_ref[k], w2_ref[k], preferred_element_type=jnp.float32)
        y_ref[k] = jnp.maximum(result + b2_ref[k : k + 1, :], 0.0)
    place = lax.axis_index("tower")
    for o, out in zip(offsets(towers), outs):
        start = pl.multiple_of((place ^ o) * per, per)
        pieces = [
            y_ref[k, pl.ds(start, per), v * EDIM : (v + 1) * EDIM]
            for k in range(count)
            for v in range(vectors)
        ]
        out[...] = jnp.concatenate(pieces, axis=0).astype(out.dtype)


def run_towers(slots, w1, b1, w2, b2, blocks, towers, intra, pair):
    order = steps(intra, pair)
    first = max(len(blocks) // 2 - 1, 0)
    early, late = (*blocks[:first], blocks[-1]), tuple(blocks[first:-1])
    held, rows, _ = blocks[0].shape
    count, depth, hid = w1.shape
    width = w2.shape[2]
    local = count * (width // EDIM) * (rows // towers)
    w1 = pltpu.with_memory_space_constraint(w1, pltpu.VMEM)
    w2 = pltpu.with_memory_space_constraint(w2, pltpu.VMEM)
    params = pltpu.CompilerParams(vmem_limit_bytes=16 << 20)
    sums = pl.pallas_call(
        functools.partial(early_kernel, intra, pair, (*order[:first], order[-1])),
        out_shape=pltpu.VMEM((count * rows, hid), jnp.float32),
        in_specs=[pl.BlockSpec(memory_space=pltpu.SMEM)]
        + [pl.BlockSpec(memory_space=pltpu.VMEM)] * (1 + len(early)),
        out_specs=pl.BlockSpec(memory_space=pltpu.VMEM),
        scratch_shapes=[pltpu.VMEM((count * rows, len(early) * held * EDIM), jnp.bfloat16)],
        compiler_params=params,
        cost_estimate=pl.CostEstimate(
            flops=2 * count * rows * depth * hid, bytes_accessed=0, transcendentals=0
        ),
        name="towers_early",
    )(slots, w1, *early)
    return pl.pallas_call(
        functools.partial(tower_kernel, towers, intra, pair, order[first:-1]),
        out_shape=[pltpu.VMEM((local, EDIM), jnp.bfloat16)] * towers,
        in_specs=[pl.BlockSpec(memory_space=pltpu.SMEM)]
        + [pl.BlockSpec(memory_space=pltpu.VMEM)] * (5 + len(late)),
        out_specs=[pl.BlockSpec(memory_space=pltpu.VMEM)] * towers,
        scratch_shapes=[
            pltpu.VMEM((count * rows, max(len(late), 1) * held * EDIM), jnp.bfloat16),
            pltpu.VMEM((count, rows, hid), jnp.bfloat16),
            pltpu.VMEM((count, rows, width), jnp.float32),
        ],
        compiler_params=params,
        name="towers",
    )(slots, w1, b1, w2, b2, sums, *late)


def interact_kernel(towers, proj_ref, *rest):
    blocks, out, all_ref = rest[:towers], rest[towers], rest[towers + 1]
    per, count, _ = out.shape
    local = blocks[0].shape[0]
    place = lax.axis_index("tower")
    for o, block in zip(offsets(towers), blocks):
        start = pl.multiple_of((place ^ o) * local, local)
        all_ref[pl.ds(start, local), :] = block[...].astype(jnp.float32)
    group = max(1, min(per, 128 // count))
    proj = jnp.concatenate([proj_ref[...]] * (2 * group), axis=0)
    for first in range(0, per, group):
        samples = range(first, first + group)
        vectors = [all_ref[pl.ds(d, count, stride=per), :] for d in samples]
        vectors = jnp.concatenate(vectors, axis=0).astype(jnp.bfloat16)
        gram = lax.dot_general(
            vectors, vectors, (((1,), (1,)), ((), ())), preferred_element_type=jnp.float32
        )
        gram = gram * (1.0 / EDIM)
        column = lax.broadcasted_iota(jnp.int32, (count, gram.shape[1]), 1)
        own = [
            jnp.where(
                (column >= g * count) & (column < (g + 1) * count),
                gram[g * count : (g + 1) * count, :],
                0.0,
            )
            for g in range(group)
        ]
        gram = jnp.concatenate(own, axis=0)
        high = gram.astype(jnp.bfloat16)
        low = (gram - high.astype(jnp.float32)).astype(jnp.bfloat16)
        result = jnp.dot(
            jnp.concatenate([high, low], axis=1), proj, preferred_element_type=jnp.float32
        )
        for g, d in enumerate(samples):
            out[d] = result[g * count : (g + 1) * count, :].astype(out.dtype)


def interact(proj, blocks):
    towers = len(blocks)
    local = blocks[0].shape[0]
    count = proj.shape[0]
    per = towers * local // count
    return pl.pallas_call(
        functools.partial(interact_kernel, towers),
        out_shape=jax.ShapeDtypeStruct((per, count, EDIM), jnp.bfloat16),
        in_specs=[pl.BlockSpec(memory_space=pltpu.VMEM)] * (1 + towers),
        out_specs=pl.BlockSpec(memory_space=pltpu.VMEM),
        scratch_shapes=[pltpu.VMEM((towers * local, EDIM), jnp.float32)],
        compiler_params=pltpu.CompilerParams(vmem_limit_bytes=8 << 20),
        name="interact",
    )(proj, *blocks)


def shards(
    embeddings,
    feature_assign,
    sample_owner,
    first_weight,
    first_bias,
    tower_weight,
    tower_bias,
    proj_weight,
):
    towers, intra = lax.axis_size("tower"), lax.axis_size("intra")
    small = (feature_assign, first_bias, tower_bias, proj_weight)
    ahead = 10_000 * (first_weight.size + tower_weight.size)
    pair = 2 if intra % 2 == 0 else 1
    blocks, small = gather_blocks(sample_owner, embeddings, small, towers, intra, pair, ahead)
    slots, first_bias, tower_bias, proj_weight = small
    blocks = exchange_chips(blocks, intra, pair)
    vectors = run_towers(
        slots, first_weight, first_bias, tower_weight, tower_bias, blocks, towers, intra, pair
    )
    vectors = exchange_groups(vectors, towers, intra)
    return interact(proj_weight, vectors)


def solution(mesh):
    return jax.shard_map(
        shards,
        mesh=mesh,
        in_specs=(
            P(None, ("tower", "intra")),
            P("tower", None),
            P(),
            P("tower", None, None),
            P("tower", None),
            P("tower", None, None),
            P("tower", None),
            P(),
        ),
        out_specs=P(("tower", "intra"), None, None),
        check_vma=False,
    )
```

```python
import functools

import jax
import jax.numpy as jnp
from jax import lax
from jax.experimental import pallas as pl
from jax.experimental.pallas import tpu as pltpu
from jax.sharding import PartitionSpec as P

EDIM = 128
FEW_SAMPLES = 1024


def offsets(size):
    return range(size - 1, -1, -1)


def steps(intra, pair):
    return (*range(1, intra // pair), 0)


def ring_place(chip, chips):
    place = chip
    bits = (chips - 1).bit_length() if chips & (chips - 1) == 0 else 0
    for n in range(1, bits):
        place = place ^ (chip >> n)
    return place


def ring_chip(place, chips):
    return place ^ (place >> 1) if chips & (chips - 1) == 0 else place


def partner(me, step, intra, pair):
    chips = intra // pair
    place = (ring_place(me // pair, chips) + step + chips) % chips
    return ring_chip(place, chips) * pair + (me % pair + (pair - 1 if step else 0)) % pair


def exchange_chips(blocks, intra, pair):
    return [
        lax.ppermute(block, "intra", [(i, partner(i, s, intra, pair)) for i in range(intra)]) if s else block
        for block, s in zip(blocks, steps(intra, pair))
    ]


def other_core(intra):
    return 1 if intra > 1 else 0


def exchange_groups(blocks, towers, intra):
    received = []
    for block, o in zip(blocks, offsets(towers)):
        pairs = [
            (t * intra + i, (t ^ o) * intra + (i ^ other_core(intra)))
            for t in range(towers)
            for i in range(intra)
        ]
        received.append(lax.ppermute(block, ("tower", "intra"), pairs) if o else block)
    return received


def load_kernel(count, owner_hbm, emb_hbm, *rest):
    small, (picks_ref, emb_ref, slots_ref), copies = rest[:count], rest[count : count + 3], rest[count + 3 : -3]
    owner_ref, assign_ref, sems = rest[-3:]
    targets = (assign_ref, *copies)
    pairs = [(owner_hbm, owner_ref), (emb_hbm, emb_ref), *zip(small, targets)]
    loads = [pltpu.make_async_copy(a, b, sems.at[i]) for i, (a, b) in enumerate(pairs)]
    for load in loads:
        load.start()
    samples = emb_ref.shape[0]
    loads[0].wait()
    owner = jnp.broadcast_to(owner_ref[...].reshape(1, samples), (samples, samples))
    picks = lax.broadcasted_iota(jnp.int32, (samples, samples), 0) == owner
    picks_ref[...] = jnp.where(picks, 1.0, 0.0).astype(jnp.bfloat16)
    loads[2].wait()
    for slot in range(assign_ref.shape[1]):
        slots_ref[0, assign_ref[0, slot]] = slot
    for load in (loads[1], *loads[3:]):
        load.wait()


def gather_kernel(towers, intra, pair, picks_ref, *rest):
    parts, outs, acc_ref = rest[:pair], rest[pair:-1], rest[-1]
    samples, width = parts[0].shape
    per = samples // (towers * intra)
    held = width // EDIM
    me, place = lax.axis_index("intra"), lax.axis_index("tower")
    for q, part in enumerate(parts):
        acc_ref[:, q * width : (q + 1) * width] = lax.dot_general(
            picks_ref[...], part[...], (((0,), (0,)), ((), ())), preferred_element_type=jnp.float32
        )
    for s, out in zip(steps(intra, pair), outs):
        block = partner(me, s, intra, pair)
        owners = [jnp.where(place == t, block, block ^ other_core(intra)) for t in range(towers)]
        starts = [pl.multiple_of((t * intra + owners[t]) * per, per) for t in range(towers)]
        for f in range(pair * held):
            columns = slice(f * EDIM, (f + 1) * EDIM)
            rows = [acc_ref[pl.ds(start, per), columns] for start in starts]
            out[f] = jnp.concatenate(rows, axis=0).astype(out.dtype)


def gather_blocks(owner, embeddings, small, towers, intra, pair, ahead):
    samples, width = embeddings.shape
    rows, held = samples // intra, pair * width // EDIM
    parts = [lax.ppermute(embeddings, "intra", [(i, i ^ q) for i in range(intra)]) for q in range(1, pair)]
    if samples <= FEW_SAMPLES:
        given = [pltpu.with_memory_space_constraint(a, pltpu.HBM) for a in (owner, embeddings, *small)]
        picks, embeddings, *small = pl.pallas_call(
            functools.partial(load_kernel, len(small)),
            out_shape=[
                pltpu.VMEM((samples, samples), jnp.bfloat16),
                pltpu.VMEM(embeddings.shape, embeddings.dtype),
                pltpu.SMEM(small[0].shape, small[0].dtype),
            ]
            + [pltpu.VMEM(a.shape, a.dtype) for a in small[1:]],
            in_specs=[pl.BlockSpec(memory_space=pltpu.HBM)] * len(given),
            out_specs=[pl.BlockSpec(memory_space=pltpu.VMEM)] * 2
            + [pl.BlockSpec(memory_space=pltpu.SMEM)]
            + [pl.BlockSpec(memory_space=pltpu.VMEM)] * (len(small) - 1),
            scratch_shapes=[
                pltpu.VMEM(owner.shape, owner.dtype),
                pltpu.SMEM(small[0].shape, small[0].dtype),
                pltpu.SemaphoreType.DMA((len(given),)),
            ],
            compiler_params=pltpu.CompilerParams(vmem_limit_bytes=8 << 20),
            name="load",
        )(*given)
        blocks = pl.pallas_call(
            functools.partial(gather_kernel, towers, intra, pair),
            out_shape=[pltpu.VMEM((held, rows, EDIM), embeddings.dtype)] * (intra // pair),
            in_specs=[pl.BlockSpec(memory_space=pltpu.VMEM)] * (1 + pair),
            out_specs=[pl.BlockSpec(memory_space=pltpu.VMEM)] * (intra // pair),
            scratch_shapes=[pltpu.VMEM((samples, pair * width), jnp.float32)],
            compiler_params=pltpu.CompilerParams(vmem_limit_bytes=8 << 20),
            cost_estimate=pl.CostEstimate(flops=ahead, bytes_accessed=0, transcendentals=0),
            name="gather_rows",
        )(picks, embeddings, *parts)
        return blocks, small
    order = owner.reshape(towers, intra, -1)
    crossed = order[:, jnp.arange(intra) ^ other_core(intra)]
    own = jnp.arange(towers)[:, None, None] == lax.axis_index("tower")
    order = jnp.where(own, order, crossed).transpose(1, 0, 2)
    me = lax.axis_index("intra")
    table = jnp.concatenate([embeddings, *parts], axis=1)
    blocks = []
    for s in steps(intra, pair):
        mine = lax.dynamic_index_in_dim(order, partner(me, s, intra, pair), keepdims=False).reshape(-1)
        blocks.append(jnp.take(table, mine, axis=0).reshape(rows, held, EDIM).transpose(1, 0, 2))
    assign = small[0][0]
    same = assign[None, :] == jnp.arange(assign.size)[:, None]
    slots = jnp.sum(jnp.where(same, jnp.arange(assign.size)[None, :], 0), axis=1)
    return blocks, (slots.astype(assign.dtype)[None, :], *small[1:])


def first_layer(intra, pair, order, slots_ref, w1_ref, x_ref, blocks, before_ref=None):
    held, rows, _ = blocks[0].shape
    held //= pair
    count, depth, hid = w1_ref.shape
    per_tower = depth // EDIM
    me = lax.axis_index("intra")
    slots = []
    for s, block in zip(order, blocks):
        source = partner(me, -s, intra, pair)
        for q in range(pair):
            for f in range(held):
                slot = slots_ref[0, (source ^ q) * held + f]
                n = len(slots)
                slots.append((slot // per_tower, pl.multiple_of((slot % per_tower) * EDIM, EDIM)))
                for k in range(count):
                    own = jnp.where(slots[n][0] == k, 1.0, 0.0).astype(jnp.bfloat16)
                    x_ref[k * rows : (k + 1) * rows, n * EDIM : (n + 1) * EDIM] = block[q * held + f] * own
    wide = 2 * EDIM
    for h in range(0, hid, wide):
        columns = slice(h, min(h + wide, hid))
        total = None if before_ref is None else before_ref[:, columns]
        for n in range(0, len(slots), 2):
            some = slots[n : n + 2]
            weight = [w1_ref[k, pl.ds(start, EDIM), columns] for k, start in some]
            term = jnp.dot(
                x_ref[:, n * EDIM : (n + len(some)) * EDIM],
                jnp.concatenate(weight, axis=0),
                preferred_element_type=jnp.float32,
            )
            total = term if total is None else total + term
        yield columns, total


def early_kernel(intra, pair, order, slots_ref, w1_ref, *rest):
    blocks, out_ref, x_ref = rest[:-2], rest[-2], rest[-1]
    for columns, total in first_layer(intra, pair, order, slots_ref, w1_ref, x_ref, blocks):
        out_ref[:, columns] = total


def tower_kernel(towers, intra, pair, order, slots_ref, w1_ref, b1_ref, w2_ref, b2_ref, sums_ref, *rest):
    blocks, outs, (x_ref, hidden_ref, y_ref) = rest[: len(order)], rest[len(order) : -3], rest[-3:]
    count, rows, _ = y_ref.shape
    vectors = w2_ref.shape[2] // EDIM
    per = rows // towers
    for columns, total in first_layer(intra, pair, order, slots_ref, w1_ref, x_ref, blocks, sums_ref):
        for k in range(count):
            hidden = total[k * rows : (k + 1) * rows] + b1_ref[k : k + 1, columns]
            hidden_ref[k, :, columns] = jnp.maximum(hidden, 0.0).astype(jnp.bfloat16)
    for k in range(count):
        result = jnp.dot(hidden_ref[k], w2_ref[k], preferred_element_type=jnp.float32)
        y_ref[k] = jnp.maximum(result + b2_ref[k : k + 1, :], 0.0)
    place = lax.axis_index("tower")
    for o, out in zip(offsets(towers), outs):
        start = pl.multiple_of((place ^ o) * per, per)
        pieces = [
            y_ref[k, pl.ds(start, per), v * EDIM : (v + 1) * EDIM]
            for k in range(count)
            for v in range(vectors)
        ]
        out[...] = jnp.concatenate(pieces, axis=0).astype(out.dtype)


def run_towers(slots, w1, b1, w2, b2, blocks, towers, intra, pair):
    order = steps(intra, pair)
    first = max(len(blocks) // 2 - 1, 0)
    early, late = (*blocks[:first], blocks[-1]), tuple(blocks[first:-1])
    held, rows, _ = blocks[0].shape
    count, depth, hid = w1.shape
    width = w2.shape[2]
    local = count * (width // EDIM) * (rows // towers)
    w1 = pltpu.with_memory_space_constraint(w1, pltpu.VMEM)
    w2 = pltpu.with_memory_space_constraint(w2, pltpu.VMEM)
    params = pltpu.CompilerParams(vmem_limit_bytes=16 << 20)
    sums = pl.pallas_call(
        functools.partial(early_kernel, intra, pair, (*order[:first], order[-1])),
        out_shape=pltpu.VMEM((count * rows, hid), jnp.float32),
        in_specs=[pl.BlockSpec(memory_space=pltpu.SMEM)]
        + [pl.BlockSpec(memory_space=pltpu.VMEM)] * (1 + len(early)),
        out_specs=pl.BlockSpec(memory_space=pltpu.VMEM),
        scratch_shapes=[pltpu.VMEM((count * rows, len(early) * held * EDIM), jnp.bfloat16)],
        compiler_params=params,
        cost_estimate=pl.CostEstimate(
            flops=2 * count * rows * depth * hid, bytes_accessed=0, transcendentals=0
        ),
        name="towers_early",
    )(slots, w1, *early)
    return pl.pallas_call(
        functools.partial(tower_kernel, towers, intra, pair, order[first:-1]),
        out_shape=[pltpu.VMEM((local, EDIM), jnp.bfloat16)] * towers,
        in_specs=[pl.BlockSpec(memory_space=pltpu.SMEM)]
        + [pl.BlockSpec(memory_space=pltpu.VMEM)] * (5 + len(late)),
        out_specs=[pl.BlockSpec(memory_space=pltpu.VMEM)] * towers,
        scratch_shapes=[
            pltpu.VMEM((count * rows, max(len(late), 1) * held * EDIM), jnp.bfloat16),
            pltpu.VMEM((count, rows, hid), jnp.bfloat16),
            pltpu.VMEM((count, rows, width), jnp.float32),
        ],
        compiler_params=params,
        name="towers",
    )(slots, w1, b1, w2, b2, sums, *late)


def interact_kernel(towers, proj_ref, *rest):
    blocks, out, all_ref = rest[:towers], rest[towers], rest[towers + 1]
    per, count, _ = out.shape
    local = blocks[0].shape[0]
    place = lax.axis_index("tower")
    for o, block in zip(offsets(towers), blocks):
        start = pl.multiple_of((place ^ o) * local, local)
        all_ref[pl.ds(start, local), :] = block[...].astype(jnp.float32)
    group = max(1, min(per, 128 // count))
    proj = jnp.concatenate([proj_ref[...]] * (2 * group), axis=0)
    for first in range(0, per, group):
        samples = range(first, first + group)
        vectors = [all_ref[pl.ds(d, count, stride=per), :] for d in samples]
        vectors = jnp.concatenate(vectors, axis=0).astype(jnp.bfloat16)
        gram = lax.dot_general(
            vectors, vectors, (((1,), (1,)), ((), ())), preferred_element_type=jnp.float32
        )
        gram = gram * (1.0 / EDIM)
        column = lax.broadcasted_iota(jnp.int32, (count, gram.shape[1]), 1)
        own = [
            jnp.where(
                (column >= g * count) & (column < (g + 1) * count),
                gram[g * count : (g + 1) * count, :],
                0.0,
            )
            for g in range(group)
        ]
        gram = jnp.concatenate(own, axis=0)
        high = gram.astype(jnp.bfloat16)
        low = (gram - high.astype(jnp.float32)).astype(jnp.bfloat16)
        result = jnp.dot(
            jnp.concatenate([high, low], axis=1), proj, preferred_element_type=jnp.float32
        )
        for g, d in enumerate(samples):
            out[d] = result[g * count : (g + 1) * count, :].astype(out.dtype)


def interact(proj, blocks):
    towers = len(blocks)
    local = blocks[0].shape[0]
    count = proj.shape[0]
    per = towers * local // count
    return pl.pallas_call(
        functools.partial(interact_kernel, towers),
        out_shape=jax.ShapeDtypeStruct((per, count, EDIM), jnp.bfloat16),
        in_specs=[pl.BlockSpec(memory_space=pltpu.VMEM)] * (1 + towers),
        out_specs=pl.BlockSpec(memory_space=pltpu.VMEM),
        scratch_shapes=[pltpu.VMEM((towers * local, EDIM), jnp.float32)],
        compiler_params=pltpu.CompilerParams(vmem_limit_bytes=8 << 20),
        name="interact",
    )(proj, *blocks)


def shards(
    embeddings,
    feature_assign,
    sample_owner,
    first_weight,
    first_bias,
    tower_weight,
    tower_bias,
    proj_weight,
):
    towers, intra = lax.axis_size("tower"), lax.axis_size("intra")
    small = (feature_assign, first_bias, tower_bias, proj_weight)
    ahead = 10_000 * (first_weight.size + tower_weight.size)
    pair = 2 if intra % 2 == 0 else 1
    blocks, small = gather_blocks(sample_owner, embeddings, small, towers, intra, pair, ahead)
    slots, first_bias, tower_bias, proj_weight = small
    blocks = exchange_chips(blocks, intra, pair)
    vectors = run_towers(
        slots, first_weight, first_bias, tower_weight, tower_bias, blocks, towers, intra, pair
    )
    vectors = exchange_groups(vectors, towers, intra)
    return interact(proj_weight, vectors)


def solution(mesh):
    return jax.shard_map(
        shards,
        mesh=mesh,
        in_specs=(
            P(None, ("tower", "intra")),
            P("tower", None),
            P(),
            P("tower", None, None),
            P("tower", None),
            P("tower", None, None),
            P("tower", None),
            P(),
        ),
        out_specs=P(("tower", "intra"), None, None),
        check_vma=False,
    )
```

```python
import functools

import jax
import jax.numpy as jnp
from jax import lax
from jax.experimental import pallas as pl
from jax.experimental.pallas import tpu as pltpu
from jax.sharding import PartitionSpec as P

EDIM = 128
FEW_SAMPLES = 1024


def offsets(size):
    return range(size - 1, -1, -1)


def steps(intra, pair):
    return (*range(1, intra // pair), 0)


def ring_place(chip, chips):
    place = chip
    bits = (chips - 1).bit_length() if chips & (chips - 1) == 0 else 0
    for n in range(1, bits):
        place = place ^ (chip >> n)
    return place


def ring_chip(place, chips):
    return place ^ (place >> 1) if chips & (chips - 1) == 0 else place


def partner(me, step, intra, pair):
    chips = intra // pair
    place = (ring_place(me // pair, chips) + step + chips) % chips
    return ring_chip(place, chips) * pair + (me % pair + (pair - 1 if step else 0)) % pair


def exchange_chips(blocks, intra, pair):
    return [
        lax.ppermute(block, "intra", [(i, partner(i, s, intra, pair)) for i in range(intra)]) if s else block
        for block, s in zip(blocks, steps(intra, pair))
    ]


def other_core(intra):
    return 1 if intra > 1 else 0


def exchange_groups(blocks, towers, intra):
    received = []
    for block, o in zip(blocks, offsets(towers)):
        pairs = [
            (t * intra + i, (t ^ o) * intra + (i ^ other_core(intra)))
            for t in range(towers)
            for i in range(intra)
        ]
        received.append(lax.ppermute(block, ("tower", "intra"), pairs) if o else block)
    return received


def load_kernel(count, owner_hbm, emb_hbm, *rest):
    small, (picks_ref, emb_ref, slots_ref), copies = rest[:count], rest[count : count + 3], rest[count + 3 : -3]
    owner_ref, assign_ref, sems = rest[-3:]
    targets = (assign_ref, *copies)
    pairs = [(owner_hbm, owner_ref), (emb_hbm, emb_ref), *zip(small, targets)]
    loads = [pltpu.make_async_copy(a, b, sems.at[i]) for i, (a, b) in enumerate(pairs)]
    for load in loads:
        load.start()
    samples = emb_ref.shape[0]
    loads[0].wait()
    owner = jnp.broadcast_to(owner_ref[...].reshape(1, samples), (samples, samples))
    picks = lax.broadcasted_iota(jnp.int32, (samples, samples), 0) == owner
    picks_ref[...] = jnp.where(picks, 1.0, 0.0).astype(jnp.bfloat16)
    loads[2].wait()
    for slot in range(assign_ref.shape[1]):
        slots_ref[0, assign_ref[0, slot]] = slot
    for load in (loads[1], *loads[3:]):
        load.wait()


def gather_kernel(towers, intra, pair, picks_ref, *rest):
    parts, outs, acc_ref = rest[:pair], rest[pair:-1], rest[-1]
    samples, width = parts[0].shape
    per = samples // (towers * intra)
    held = width // EDIM
    me, place = lax.axis_index("intra"), lax.axis_index("tower")
    for q, part in enumerate(parts):
        acc_ref[:, q * width : (q + 1) * width] = lax.dot_general(
            picks_ref[...], part[...], (((0,), (0,)), ((), ())), preferred_element_type=jnp.float32
        )
    for s, out in zip(steps(intra, pair), outs):
        block = partner(me, s, intra, pair)
        owners = [jnp.where(place == t, block, block ^ other_core(intra)) for t in range(towers)]
        starts = [pl.multiple_of((t * intra + owners[t]) * per, per) for t in range(towers)]
        for f in range(pair * held):
            columns = slice(f * EDIM, (f + 1) * EDIM)
            rows = [acc_ref[pl.ds(start, per), columns] for start in starts]
            out[f] = jnp.concatenate(rows, axis=0).astype(out.dtype)


def gather_blocks(owner, embeddings, small, towers, intra, pair, ahead):
    samples, width = embeddings.shape
    rows, held = samples // intra, pair * width // EDIM
    parts = [lax.ppermute(embeddings, "intra", [(i, i ^ q) for i in range(intra)]) for q in range(1, pair)]
    if samples <= FEW_SAMPLES:
        given = [pltpu.with_memory_space_constraint(a, pltpu.HBM) for a in (owner, embeddings, *small)]
        picks, embeddings, *small = pl.pallas_call(
            functools.partial(load_kernel, len(small)),
            out_shape=[
                pltpu.VMEM((samples, samples), jnp.bfloat16),
                pltpu.VMEM(embeddings.shape, embeddings.dtype),
                pltpu.SMEM(small[0].shape, small[0].dtype),
            ]
            + [pltpu.VMEM(a.shape, a.dtype) for a in small[1:]],
            in_specs=[pl.BlockSpec(memory_space=pltpu.HBM)] * len(given),
            out_specs=[pl.BlockSpec(memory_space=pltpu.VMEM)] * 2
            + [pl.BlockSpec(memory_space=pltpu.SMEM)]
            + [pl.BlockSpec(memory_space=pltpu.VMEM)] * (len(small) - 1),
            scratch_shapes=[
                pltpu.VMEM(owner.shape, owner.dtype),
                pltpu.SMEM(small[0].shape, small[0].dtype),
                pltpu.SemaphoreType.DMA((len(given),)),
            ],
            compiler_params=pltpu.CompilerParams(vmem_limit_bytes=8 << 20),
            name="load",
        )(*given)
        blocks = pl.pallas_call(
            functools.partial(gather_kernel, towers, intra, pair),
            out_shape=[pltpu.VMEM((held, rows, EDIM), embeddings.dtype)] * (intra // pair),
            in_specs=[pl.BlockSpec(memory_space=pltpu.VMEM)] * (1 + pair),
            out_specs=[pl.BlockSpec(memory_space=pltpu.VMEM)] * (intra // pair),
            scratch_shapes=[pltpu.VMEM((samples, pair * width), jnp.float32)],
            compiler_params=pltpu.CompilerParams(vmem_limit_bytes=8 << 20),
            cost_estimate=pl.CostEstimate(flops=ahead, bytes_accessed=0, transcendentals=0),
            name="gather_rows",
        )(picks, embeddings, *parts)
        return blocks, small
    order = owner.reshape(towers, intra, -1)
    crossed = order[:, jnp.arange(intra) ^ other_core(intra)]
    own = jnp.arange(towers)[:, None, None] == lax.axis_index("tower")
    order = jnp.where(own, order, crossed).transpose(1, 0, 2)
    me = lax.axis_index("intra")
    table = jnp.concatenate([embeddings, *parts], axis=1)
    blocks = []
    for s in steps(intra, pair):
        mine = lax.dynamic_index_in_dim(order, partner(me, s, intra, pair), keepdims=False).reshape(-1)
        blocks.append(jnp.take(table, mine, axis=0).reshape(rows, held, EDIM).transpose(1, 0, 2))
    assign = small[0][0]
    same = assign[None, :] == jnp.arange(assign.size)[:, None]
    slots = jnp.sum(jnp.where(same, jnp.arange(assign.size)[None, :], 0), axis=1)
    return blocks, (slots.astype(assign.dtype)[None, :], *small[1:])


def first_layer(intra, pair, order, slots_ref, w1_ref, x_ref, blocks, before_ref=None):
    held, rows, _ = blocks[0].shape
    held //= pair
    count, depth, hid = w1_ref.shape
    per_tower = depth // EDIM
    me = lax.axis_index("intra")
    slots = []
    for s, block in zip(order, blocks):
        source = partner(me, -s, intra, pair)
        for q in range(pair):
            for f in range(held):
                slot = slots_ref[0, (source ^ q) * held + f]
                n = len(slots)
                slots.append((slot // per_tower, pl.multiple_of((slot % per_tower) * EDIM, EDIM)))
                for k in range(count):
                    own = jnp.where(slots[n][0] == k, 1.0, 0.0).astype(jnp.bfloat16)
                    x_ref[k * rows : (k + 1) * rows, n * EDIM : (n + 1) * EDIM] = block[q * held + f] * own
    wide = 2 * EDIM
    for h in range(0, hid, wide):
        columns = slice(h, min(h + wide, hid))
        total = None if before_ref is None else before_ref[:, columns]
        for n in range(0, len(slots), 2):
            some = slots[n : n + 2]
            weight = [w1_ref[k, pl.ds(start, EDIM), columns] for k, start in some]
            term = jnp.dot(
                x_ref[:, n * EDIM : (n + len(some)) * EDIM],
                jnp.concatenate(weight, axis=0),
                preferred_element_type=jnp.float32,
            )
            total = term if total is None else total + term
        yield columns, total


def early_kernel(intra, pair, order, slots_ref, w1_ref, *rest):
    blocks, before, (out_ref, x_ref) = rest[: len(order)], rest[len(order) : -2], rest[-2:]
    for columns, total in first_layer(intra, pair, order, slots_ref, w1_ref, x_ref, blocks, *before):
        out_ref[:, columns] = total


def tower_kernel(towers, intra, pair, order, slots_ref, w1_ref, b1_ref, w2_ref, b2_ref, sums_ref, *rest):
    blocks, outs, (x_ref, hidden_ref, y_ref) = rest[: len(order)], rest[len(order) : -3], rest[-3:]
    count, rows, _ = y_ref.shape
    vectors = w2_ref.shape[2] // EDIM
    per = rows // towers
    for columns, total in first_layer(intra, pair, order, slots_ref, w1_ref, x_ref, blocks, sums_ref):
        for k in range(count):
            hidden = total[k * rows : (k + 1) * rows] + b1_ref[k : k + 1, columns]
            hidden_ref[k, :, columns] = jnp.maximum(hidden, 0.0).astype(jnp.bfloat16)
    for k in range(count):
        result = jnp.dot(hidden_ref[k], w2_ref[k], preferred_element_type=jnp.float32)
        y_ref[k] = jnp.maximum(result + b2_ref[k : k + 1, :], 0.0)
    place = lax.axis_index("tower")
    for o, out in zip(offsets(towers), outs):
        start = pl.multiple_of((place ^ o) * per, per)
        pieces = [
            y_ref[k, pl.ds(start, per), v * EDIM : (v + 1) * EDIM]
            for k in range(count)
            for v in range(vectors)
        ]
        out[...] = jnp.concatenate(pieces, axis=0).astype(out.dtype)


def run_towers(slots, w1, b1, w2, b2, blocks, towers, intra, pair):
    order = steps(intra, pair)
    remote = len(blocks) - 1
    cuts = (0, max(remote // 2, min(remote - 1, 1)), remote - 1)
    stages = [[-1, *range(*cuts[:2])], [*range(*cuts[1:])]]
    late = [remote - 1] if remote else []
    held, rows, _ = blocks[0].shape
    count, depth, hid = w1.shape
    width = w2.shape[2]
    local = count * (width // EDIM) * (rows // towers)
    w1 = pltpu.with_memory_space_constraint(w1, pltpu.VMEM)
    w2 = pltpu.with_memory_space_constraint(w2, pltpu.VMEM)
    params = pltpu.CompilerParams(vmem_limit_bytes=16 << 20)
    sums = ()
    for stage in stages:
        if not stage:
            continue
        sums = pl.pallas_call(
            functools.partial(early_kernel, intra, pair, [order[n] for n in stage]),
            out_shape=[pltpu.VMEM((count * rows, hid), jnp.float32)],
            in_specs=[pl.BlockSpec(memory_space=pltpu.SMEM)]
            + [pl.BlockSpec(memory_space=pltpu.VMEM)] * (1 + len(stage) + len(sums)),
            out_specs=[pl.BlockSpec(memory_space=pltpu.VMEM)],
            scratch_shapes=[pltpu.VMEM((count * rows, len(stage) * held * EDIM), jnp.bfloat16)],
            compiler_params=params,
            cost_estimate=pl.CostEstimate(
                flops=2 * count * rows * depth * hid, bytes_accessed=0, transcendentals=0
            ),
            name="towers_early",
        )(slots, w1, *(blocks[n] for n in stage), *sums)
    return pl.pallas_call(
        functools.partial(tower_kernel, towers, intra, pair, [order[n] for n in late]),
        out_shape=[pltpu.VMEM((local, EDIM), jnp.bfloat16)] * towers,
        in_specs=[pl.BlockSpec(memory_space=pltpu.SMEM)]
        + [pl.BlockSpec(memory_space=pltpu.VMEM)] * (5 + len(late)),
        out_specs=[pl.BlockSpec(memory_space=pltpu.VMEM)] * towers,
        scratch_shapes=[
            pltpu.VMEM((count * rows, max(len(late), 1) * held * EDIM), jnp.bfloat16),
            pltpu.VMEM((count, rows, hid), jnp.bfloat16),
            pltpu.VMEM((count, rows, width), jnp.float32),
        ],
        compiler_params=params,
        name="towers",
    )(slots, w1, b1, w2, b2, *sums, *(blocks[n] for n in late))


def interact_kernel(towers, proj_ref, *rest):
    blocks, out, all_ref = rest[:towers], rest[towers], rest[towers + 1]
    per, count, _ = out.shape
    local = blocks[0].shape[0]
    place = lax.axis_index("tower")
    for o, block in zip(offsets(towers), blocks):
        start = pl.multiple_of((place ^ o) * local, local)
        all_ref[pl.ds(start, local), :] = block[...].astype(jnp.float32)
    group = max(1, min(per, 128 // count))
    proj = jnp.concatenate([proj_ref[...]] * (2 * group), axis=0)
    for first in range(0, per, group):
        samples = range(first, first + group)
        vectors = [all_ref[pl.ds(d, count, stride=per), :] for d in samples]
        vectors = jnp.concatenate(vectors, axis=0).astype(jnp.bfloat16)
        gram = lax.dot_general(
            vectors, vectors, (((1,), (1,)), ((), ())), preferred_element_type=jnp.float32
        )
        gram = gram * (1.0 / EDIM)
        column = lax.broadcasted_iota(jnp.int32, (count, gram.shape[1]), 1)
        own = [
            jnp.where(
                (column >= g * count) & (column < (g + 1) * count),
                gram[g * count : (g + 1) * count, :],
                0.0,
            )
            for g in range(group)
        ]
        gram = jnp.concatenate(own, axis=0)
        high = gram.astype(jnp.bfloat16)
        low = (gram - high.astype(jnp.float32)).astype(jnp.bfloat16)
        result = jnp.dot(
            jnp.concatenate([high, low], axis=1), proj, preferred_element_type=jnp.float32
        )
        for g, d in enumerate(samples):
            out[d] = result[g * count : (g + 1) * count, :].astype(out.dtype)


def interact(proj, blocks):
    towers = len(blocks)
    local = blocks[0].shape[0]
    count = proj.shape[0]
    per = towers * local // count
    return pl.pallas_call(
        functools.partial(interact_kernel, towers),
        out_shape=jax.ShapeDtypeStruct((per, count, EDIM), jnp.bfloat16),
        in_specs=[pl.BlockSpec(memory_space=pltpu.VMEM)] * (1 + towers),
        out_specs=pl.BlockSpec(memory_space=pltpu.VMEM),
        scratch_shapes=[pltpu.VMEM((towers * local, EDIM), jnp.float32)],
        compiler_params=pltpu.CompilerParams(vmem_limit_bytes=8 << 20),
        name="interact",
    )(proj, *blocks)


def shards(
    embeddings,
    feature_assign,
    sample_owner,
    first_weight,
    first_bias,
    tower_weight,
    tower_bias,
    proj_weight,
):
    towers, intra = lax.axis_size("tower"), lax.axis_size("intra")
    small = (feature_assign, first_bias, tower_bias, proj_weight)
    ahead = 10_000 * (first_weight.size + tower_weight.size)
    pair = 2 if intra % 2 == 0 else 1
    blocks, small = gather_blocks(sample_owner, embeddings, small, towers, intra, pair, ahead)
    slots, first_bias, tower_bias, proj_weight = small
    blocks = exchange_chips(blocks, intra, pair)
    vectors = run_towers(
        slots, first_weight, first_bias, tower_weight, tower_bias, blocks, towers, intra, pair
    )
    vectors = exchange_groups(vectors, towers, intra)
    return interact(proj_weight, vectors)


def solution(mesh):
    return jax.shard_map(
        shards,
        mesh=mesh,
        in_specs=(
            P(None, ("tower", "intra")),
            P("tower", None),
            P(),
            P("tower", None, None),
            P("tower", None),
            P("tower", None, None),
            P("tower", None),
            P(),
        ),
        out_specs=P(("tower", "intra"), None, None),
        check_vma=False,
    )
```

```python
import functools

import jax
import jax.numpy as jnp
from jax import lax
from jax.experimental import pallas as pl
from jax.experimental.pallas import tpu as pltpu
from jax.sharding import PartitionSpec as P

EDIM = 128
FEW_SAMPLES = 1024


def rounds(towers, pair):
    return range(towers // pair - 1, -1, -1)


def steps(intra, pair):
    return (*range(1, intra // pair), 0)


def ring_place(chip, chips):
    place = chip
    bits = (chips - 1).bit_length() if chips & (chips - 1) == 0 else 0
    for n in range(1, bits):
        place = place ^ (chip >> n)
    return place


def ring_chip(place, chips):
    return place ^ (place >> 1) if chips & (chips - 1) == 0 else place


def partner(me, step, intra, pair):
    chips = intra // pair
    place = (ring_place(me // pair, chips) + step + chips) % chips
    return ring_chip(place, chips) * pair + (me % pair + (pair - 1 if step else 0)) % pair


def exchange_chips(blocks, intra, pair):
    return [
        lax.ppermute(block, "intra", [(i, partner(i, s, intra, pair)) for i in range(intra)]) if s else block
        for block, s in zip(blocks, steps(intra, pair))
    ]


def exchange_groups(blocks, towers, intra, pair):
    half = towers // pair
    received = []
    for block, j in zip(blocks, rounds(towers, pair)):
        pairs = [
            (t * intra + i, (t ^ (j + i % pair * half)) * intra + i)
            for t in range(towers)
            for i in range(intra)
        ]
        received.append(lax.ppermute(block, ("tower", "intra"), pairs))
    swaps = [(i, i ^ q) for q in range(1, pair) for i in range(intra)]
    return [*received, *(lax.ppermute(block, "intra", swaps) for block in received if swaps)]


def load_kernel(count, owner_hbm, emb_hbm, *rest):
    small, (picks_ref, emb_ref, slots_ref), copies = rest[:count], rest[count : count + 3], rest[count + 3 : -3]
    owner_ref, assign_ref, sems = rest[-3:]
    targets = (assign_ref, *copies)
    pairs = [(owner_hbm, owner_ref), (emb_hbm, emb_ref), *zip(small, targets)]
    loads = [pltpu.make_async_copy(a, b, sems.at[i]) for i, (a, b) in enumerate(pairs)]
    for load in loads:
        load.start()
    samples = emb_ref.shape[0]
    loads[0].wait()
    owner = jnp.broadcast_to(owner_ref[...].reshape(1, samples), (samples, samples))
    picks = lax.broadcasted_iota(jnp.int32, (samples, samples), 0) == owner
    picks_ref[...] = jnp.where(picks, 1.0, 0.0).astype(jnp.bfloat16)
    loads[2].wait()
    for slot in range(assign_ref.shape[1]):
        slots_ref[0, assign_ref[0, slot]] = slot
    for load in (loads[1], *loads[3:]):
        load.wait()


def gather_kernel(towers, intra, pair, picks_ref, *rest):
    parts, outs, acc_ref = rest[:pair], rest[pair:-1], rest[-1]
    samples, width = parts[0].shape
    per = samples // (towers * intra)
    held, half = width // EDIM, towers // pair
    me, place = lax.axis_index("intra"), lax.axis_index("tower")
    for q, part in enumerate(parts):
        acc_ref[:, q * width : (q + 1) * width] = lax.dot_general(
            picks_ref[...], part[...], (((0,), (0,)), ((), ())), preferred_element_type=jnp.float32
        )
    for s, out in zip(steps(intra, pair), outs):
        block = partner(me, s, intra, pair)
        starts = [
            pl.multiple_of(
                ((place ^ (j + block % pair * half)) * intra + block // pair * pair + e) * per, per
            )
            for j in range(half)
            for e in range(pair)
        ]
        for f in range(pair * held):
            columns = slice(f * EDIM, (f + 1) * EDIM)
            rows = [acc_ref[pl.ds(start, per), columns] for start in starts]
            out[f] = jnp.concatenate(rows, axis=0).astype(out.dtype)


def gather_blocks(owner, embeddings, small, towers, intra, pair, ahead):
    samples, width = embeddings.shape
    rows, held = samples // intra, pair * width // EDIM
    parts = [lax.ppermute(embeddings, "intra", [(i, i ^ q) for i in range(intra)]) for q in range(1, pair)]
    if samples <= FEW_SAMPLES:
        given = [pltpu.with_memory_space_constraint(a, pltpu.HBM) for a in (owner, embeddings, *small)]
        picks, embeddings, *small = pl.pallas_call(
            functools.partial(load_kernel, len(small)),
            out_shape=[
                pltpu.VMEM((samples, samples), jnp.bfloat16),
                pltpu.VMEM(embeddings.shape, embeddings.dtype),
                pltpu.SMEM(small[0].shape, small[0].dtype),
            ]
            + [pltpu.VMEM(a.shape, a.dtype) for a in small[1:]],
            in_specs=[pl.BlockSpec(memory_space=pltpu.HBM)] * len(given),
            out_specs=[pl.BlockSpec(memory_space=pltpu.VMEM)] * 2
            + [pl.BlockSpec(memory_space=pltpu.SMEM)]
            + [pl.BlockSpec(memory_space=pltpu.VMEM)] * (len(small) - 1),
            scratch_shapes=[
                pltpu.VMEM(owner.shape, owner.dtype),
                pltpu.SMEM(small[0].shape, small[0].dtype),
                pltpu.SemaphoreType.DMA((len(given),)),
            ],
            compiler_params=pltpu.CompilerParams(vmem_limit_bytes=8 << 20),
            name="load",
        )(*given)
        blocks = pl.pallas_call(
            functools.partial(gather_kernel, towers, intra, pair),
            out_shape=[pltpu.VMEM((held, rows, EDIM), embeddings.dtype)] * (intra // pair),
            in_specs=[pl.BlockSpec(memory_space=pltpu.VMEM)] * (1 + pair),
            out_specs=[pl.BlockSpec(memory_space=pltpu.VMEM)] * (intra // pair),
            scratch_shapes=[pltpu.VMEM((samples, pair * width), jnp.float32)],
            compiler_params=pltpu.CompilerParams(vmem_limit_bytes=8 << 20),
            cost_estimate=pl.CostEstimate(flops=ahead, bytes_accessed=0, transcendentals=0),
            name="gather_rows",
        )(picks, embeddings, *parts)
        return blocks, small
    order = owner.reshape(towers, intra, -1)
    place, half = lax.axis_index("tower"), towers // pair
    me = lax.axis_index("intra")
    table = jnp.concatenate([embeddings, *parts], axis=1)
    blocks = []
    for s in steps(intra, pair):
        block = partner(me, s, intra, pair)
        groups = place ^ (jnp.arange(half) + block % pair * half)
        mine = order[groups[:, None], block // pair * pair + jnp.arange(pair)[None, :]].reshape(-1)
        blocks.append(jnp.take(table, mine, axis=0).reshape(rows, held, EDIM).transpose(1, 0, 2))
    assign = small[0][0]
    same = assign[None, :] == jnp.arange(assign.size)[:, None]
    slots = jnp.sum(jnp.where(same, jnp.arange(assign.size)[None, :], 0), axis=1)
    return blocks, (slots.astype(assign.dtype)[None, :], *small[1:])


def first_layer(intra, pair, order, slots_ref, w1_ref, x_ref, blocks, before_ref=None):
    held, rows, _ = blocks[0].shape
    held //= pair
    count, depth, hid = w1_ref.shape
    per_tower = depth // EDIM
    me = lax.axis_index("intra")
    slots = []
    for s, block in zip(order, blocks):
        source = partner(me, -s, intra, pair)
        for q in range(pair):
            for f in range(held):
                slot = slots_ref[0, (source ^ q) * held + f]
                n = len(slots)
                slots.append((slot // per_tower, pl.multiple_of((slot % per_tower) * EDIM, EDIM)))
                for k in range(count):
                    own = jnp.where(slots[n][0] == k, 1.0, 0.0).astype(jnp.bfloat16)
                    x_ref[k * rows : (k + 1) * rows, n * EDIM : (n + 1) * EDIM] = block[q * held + f] * own
    wide = 2 * EDIM
    for h in range(0, hid, wide):
        columns = slice(h, min(h + wide, hid))
        total = None if before_ref is None else before_ref[:, columns]
        for n in range(0, len(slots), 2):
            some = slots[n : n + 2]
            weight = [w1_ref[k, pl.ds(start, EDIM), columns] for k, start in some]
            term = jnp.dot(
                x_ref[:, n * EDIM : (n + len(some)) * EDIM],
                jnp.concatenate(weight, axis=0),
                preferred_element_type=jnp.float32,
            )
            total = term if total is None else total + term
        yield columns, total


def early_kernel(intra, pair, order, slots_ref, w1_ref, *rest):
    blocks, before, (out_ref, x_ref) = rest[: len(order)], rest[len(order) : -2], rest[-2:]
    for columns, total in first_layer(intra, pair, order, slots_ref, w1_ref, x_ref, blocks, *before):
        out_ref[:, columns] = total


def tower_kernel(towers, intra, pair, order, slots_ref, w1_ref, b1_ref, w2_ref, b2_ref, sums_ref, *rest):
    blocks, outs, (x_ref, hidden_ref, y_ref) = rest[: len(order)], rest[len(order) : -3], rest[-3:]
    count, rows, _ = y_ref.shape
    vectors = w2_ref.shape[2] // EDIM
    per = rows // towers
    for columns, total in first_layer(intra, pair, order, slots_ref, w1_ref, x_ref, blocks, sums_ref):
        for k in range(count):
            hidden = total[k * rows : (k + 1) * rows] + b1_ref[k : k + 1, columns]
            hidden_ref[k, :, columns] = jnp.maximum(hidden, 0.0).astype(jnp.bfloat16)
    for k in range(count):
        result = jnp.dot(hidden_ref[k], w2_ref[k], preferred_element_type=jnp.float32)
        y_ref[k] = jnp.maximum(result + b2_ref[k : k + 1, :], 0.0)
    for j, out in zip(rounds(towers, pair), outs):
        pieces = [
            y_ref[k, n * per : (n + 1) * per, v * EDIM : (v + 1) * EDIM]
            for n in range(j * pair, (j + 1) * pair)
            for k in range(count)
            for v in range(vectors)
        ]
        out[...] = jnp.concatenate(pieces, axis=0).astype(out.dtype)


def run_towers(slots, w1, b1, w2, b2, blocks, towers, intra, pair):
    order = steps(intra, pair)
    remote = len(blocks) - 1
    cuts = (0, max(remote // 2, min(remote - 1, 1)), remote - 1)
    stages = [[-1, *range(*cuts[:2])], [*range(*cuts[1:])]]
    late = [remote - 1] if remote else []
    held, rows, _ = blocks[0].shape
    count, depth, hid = w1.shape
    width = w2.shape[2]
    local = pair * count * (width // EDIM) * (rows // towers)
    w1 = pltpu.with_memory_space_constraint(w1, pltpu.VMEM)
    w2 = pltpu.with_memory_space_constraint(w2, pltpu.VMEM)
    params = pltpu.CompilerParams(vmem_limit_bytes=16 << 20)
    sums = ()
    for stage in stages:
        if not stage:
            continue
        sums = pl.pallas_call(
            functools.partial(early_kernel, intra, pair, [order[n] for n in stage]),
            out_shape=[pltpu.VMEM((count * rows, hid), jnp.float32)],
            in_specs=[pl.BlockSpec(memory_space=pltpu.SMEM)]
            + [pl.BlockSpec(memory_space=pltpu.VMEM)] * (1 + len(stage) + len(sums)),
            out_specs=[pl.BlockSpec(memory_space=pltpu.VMEM)],
            scratch_shapes=[pltpu.VMEM((count * rows, len(stage) * held * EDIM), jnp.bfloat16)],
            compiler_params=params,
            cost_estimate=pl.CostEstimate(
                flops=2 * count * rows * depth * hid, bytes_accessed=0, transcendentals=0
            ),
            name="towers_early",
        )(slots, w1, *(blocks[n] for n in stage), *sums)
    return pl.pallas_call(
        functools.partial(tower_kernel, towers, intra, pair, [order[n] for n in late]),
        out_shape=[pltpu.VMEM((local, EDIM), jnp.bfloat16)] * (towers // pair),
        in_specs=[pl.BlockSpec(memory_space=pltpu.SMEM)]
        + [pl.BlockSpec(memory_space=pltpu.VMEM)] * (5 + len(late)),
        out_specs=[pl.BlockSpec(memory_space=pltpu.VMEM)] * (towers // pair),
        scratch_shapes=[
            pltpu.VMEM((count * rows, max(len(late), 1) * held * EDIM), jnp.bfloat16),
            pltpu.VMEM((count, rows, hid), jnp.bfloat16),
            pltpu.VMEM((count, rows, width), jnp.float32),
        ],
        compiler_params=params,
        name="towers",
    )(slots, w1, b1, w2, b2, *sums, *(blocks[n] for n in late))


def interact_kernel(towers, pair, proj_ref, *rest):
    blocks, out, all_ref = rest[:towers], rest[towers], rest[towers + 1]
    per, count, _ = out.shape
    local, half = blocks[0].shape[0] // pair, towers // pair
    place, core = lax.axis_index("tower"), lax.axis_index("intra") % pair
    own = pl.multiple_of(core * local, local)
    for n, block in enumerate(blocks):
        offset = rounds(towers, pair)[n % half] + (core ^ (n // half)) * half
        start = pl.multiple_of((place ^ offset) * local, local)
        all_ref[pl.ds(start, local), :] = block[pl.ds(own, local), :].astype(jnp.float32)
    group = max(1, min(per, 128 // count))
    proj = jnp.concatenate([proj_ref[...]] * (2 * group), axis=0)
    for first in range(0, per, group):
        samples = range(first, first + group)
        vectors = [all_ref[pl.ds(d, count, stride=per), :] for d in samples]
        vectors = jnp.concatenate(vectors, axis=0).astype(jnp.bfloat16)
        gram = lax.dot_general(
            vectors, vectors, (((1,), (1,)), ((), ())), preferred_element_type=jnp.float32
        )
        gram = gram * (1.0 / EDIM)
        column = lax.broadcasted_iota(jnp.int32, (count, gram.shape[1]), 1)
        own = [
            jnp.where(
                (column >= g * count) & (column < (g + 1) * count),
                gram[g * count : (g + 1) * count, :],
                0.0,
            )
            for g in range(group)
        ]
        gram = jnp.concatenate(own, axis=0)
        high = gram.astype(jnp.bfloat16)
        low = (gram - high.astype(jnp.float32)).astype(jnp.bfloat16)
        result = jnp.dot(
            jnp.concatenate([high, low], axis=1), proj, preferred_element_type=jnp.float32
        )
        for g, d in enumerate(samples):
            out[d] = result[g * count : (g + 1) * count, :].astype(out.dtype)


def interact(proj, blocks, pair):
    towers = len(blocks)
    local = blocks[0].shape[0] // pair
    count = proj.shape[0]
    per = towers * local // count
    return pl.pallas_call(
        functools.partial(interact_kernel, towers, pair),
        out_shape=jax.ShapeDtypeStruct((per, count, EDIM), jnp.bfloat16),
        in_specs=[pl.BlockSpec(memory_space=pltpu.VMEM)] * (1 + towers),
        out_specs=pl.BlockSpec(memory_space=pltpu.VMEM),
        scratch_shapes=[pltpu.VMEM((towers * local, EDIM), jnp.float32)],
        compiler_params=pltpu.CompilerParams(vmem_limit_bytes=8 << 20),
        name="interact",
    )(proj, *blocks)


def shards(
    embeddings,
    feature_assign,
    sample_owner,
    first_weight,
    first_bias,
    tower_weight,
    tower_bias,
    proj_weight,
):
    towers, intra = lax.axis_size("tower"), lax.axis_size("intra")
    small = (feature_assign, first_bias, tower_bias, proj_weight)
    ahead = 10_000 * (first_weight.size + tower_weight.size)
    pair = 2 if intra % 2 == 0 and towers % 2 == 0 else 1
    blocks, small = gather_blocks(sample_owner, embeddings, small, towers, intra, pair, ahead)
    slots, first_bias, tower_bias, proj_weight = small
    blocks = exchange_chips(blocks, intra, pair)
    vectors = run_towers(
        slots, first_weight, first_bias, tower_weight, tower_bias, blocks, towers, intra, pair
    )
    vectors = exchange_groups(vectors, towers, intra, pair)
    return interact(proj_weight, vectors, pair)


def solution(mesh):
    return jax.shard_map(
        shards,
        mesh=mesh,
        in_specs=(
            P(None, ("tower", "intra")),
            P("tower", None),
            P(),
            P("tower", None, None),
            P("tower", None),
            P("tower", None, None),
            P("tower", None),
            P(),
        ),
        out_specs=P(("tower", "intra"), None, None),
        check_vma=False,
    )
```

```python
import functools

import jax
import jax.numpy as jnp
from jax import lax
from jax.experimental import pallas as pl
from jax.experimental.pallas import tpu as pltpu
from jax.sharding import PartitionSpec as P

EDIM = 128
FEW_SAMPLES = 1024


def offsets(size):
    return range(size - 1, -1, -1)


def steps(intra, pair):
    return (*range(1, intra // pair), 0)


def partner(me, step, intra, pair):
    chips = intra // pair
    return (me // pair + step + chips) % chips * pair + (me % pair + (pair - 1 if step else 0)) % pair


def exchange_chips(blocks, intra, pair):
    received, put_off = [], []
    for block, s in zip(blocks[:-1], steps(intra, pair)):
        pairs = [(i, partner(i, s, intra, pair)) for i in range(intra)]
        if s == intra // pair // 2:
            put_off.append((s, block, pairs[-pair:]))
            pairs = pairs[:-pair]
        received.append((s, lax.ppermute(block, "intra", pairs)))
    for s, block, pairs in put_off:
        received.append((s, lax.ppermute(block, "intra", pairs)))
    return [*received, (0, blocks[-1])]


def other_core(intra):
    return 1 if intra > 1 else 0


def exchange_groups(blocks, towers, intra):
    received = []
    for block, o in zip(blocks, offsets(towers)):
        pairs = [
            (t * intra + i, (t ^ o) * intra + (i ^ other_core(intra)))
            for t in range(towers)
            for i in range(intra)
        ]
        received.append(lax.ppermute(block, ("tower", "intra"), pairs) if o else block)
    return received


def load_kernel(count, owner_hbm, emb_hbm, *rest):
    small, (picks_ref, emb_ref, slots_ref), copies = rest[:count], rest[count : count + 3], rest[count + 3 : -3]
    owner_ref, assign_ref, sems = rest[-3:]
    targets = (assign_ref, *copies)
    pairs = [(owner_hbm, owner_ref), (emb_hbm, emb_ref), *zip(small, targets)]
    loads = [pltpu.make_async_copy(a, b, sems.at[i]) for i, (a, b) in enumerate(pairs)]
    for load in loads:
        load.start()
    samples = emb_ref.shape[0]
    loads[0].wait()
    owner = jnp.broadcast_to(owner_ref[...].reshape(1, samples), (samples, samples))
    picks = lax.broadcasted_iota(jnp.int32, (samples, samples), 0) == owner
    picks_ref[...] = jnp.where(picks, 1.0, 0.0).astype(jnp.bfloat16)
    loads[2].wait()
    for slot in range(assign_ref.shape[1]):
        slots_ref[0, assign_ref[0, slot]] = slot
    for load in (loads[1], *loads[3:]):
        load.wait()


def gather_kernel(towers, intra, pair, picks_ref, *rest):
    parts, outs, acc_ref = rest[:pair], rest[pair:-1], rest[-1]
    samples, width = parts[0].shape
    per = samples // (towers * intra)
    held = width // EDIM
    me, place = lax.axis_index("intra"), lax.axis_index("tower")
    for q, part in enumerate(parts):
        acc_ref[:, q * width : (q + 1) * width] = lax.dot_general(
            picks_ref[...], part[...], (((0,), (0,)), ((), ())), preferred_element_type=jnp.float32
        )
    for s, out in zip(steps(intra, pair), outs):
        block = partner(me, s, intra, pair)
        owners = [jnp.where(place == t, block, block ^ other_core(intra)) for t in range(towers)]
        starts = [pl.multiple_of((t * intra + owners[t]) * per, per) for t in range(towers)]
        for f in range(pair * held):
            columns = slice(f * EDIM, (f + 1) * EDIM)
            rows = [acc_ref[pl.ds(start, per), columns] for start in starts]
            out[f] = jnp.concatenate(rows, axis=0).astype(out.dtype)


def gather_blocks(owner, embeddings, small, towers, intra, pair, ahead):
    samples, width = embeddings.shape
    rows, held = samples // intra, pair * width // EDIM
    parts = [lax.ppermute(embeddings, "intra", [(i, i ^ q) for i in range(intra)]) for q in range(1, pair)]
    if samples <= FEW_SAMPLES:
        given = [pltpu.with_memory_space_constraint(a, pltpu.HBM) for a in (owner, embeddings, *small)]
        picks, embeddings, *small = pl.pallas_call(
            functools.partial(load_kernel, len(small)),
            out_shape=[
                pltpu.VMEM((samples, samples), jnp.bfloat16),
                pltpu.VMEM(embeddings.shape, embeddings.dtype),
                pltpu.SMEM(small[0].shape, small[0].dtype),
            ]
            + [pltpu.VMEM(a.shape, a.dtype) for a in small[1:]],
            in_specs=[pl.BlockSpec(memory_space=pltpu.HBM)] * len(given),
            out_specs=[pl.BlockSpec(memory_space=pltpu.VMEM)] * 2
            + [pl.BlockSpec(memory_space=pltpu.SMEM)]
            + [pl.BlockSpec(memory_space=pltpu.VMEM)] * (len(small) - 1),
            scratch_shapes=[
                pltpu.VMEM(owner.shape, owner.dtype),
                pltpu.SMEM(small[0].shape, small[0].dtype),
                pltpu.SemaphoreType.DMA((len(given),)),
            ],
            compiler_params=pltpu.CompilerParams(vmem_limit_bytes=8 << 20),
            name="load",
        )(*given)
        blocks = pl.pallas_call(
            functools.partial(gather_kernel, towers, intra, pair),
            out_shape=[pltpu.VMEM((held, rows, EDIM), embeddings.dtype)] * (intra // pair),
            in_specs=[pl.BlockSpec(memory_space=pltpu.VMEM)] * (1 + pair),
            out_specs=[pl.BlockSpec(memory_space=pltpu.VMEM)] * (intra // pair),
            scratch_shapes=[pltpu.VMEM((samples, pair * width), jnp.float32)],
            compiler_params=pltpu.CompilerParams(vmem_limit_bytes=8 << 20),
            cost_estimate=pl.CostEstimate(flops=ahead, bytes_accessed=0, transcendentals=0),
            name="gather_rows",
        )(picks, embeddings, *parts)
        return blocks, small
    order = owner.reshape(towers, intra, -1)
    crossed = order[:, jnp.arange(intra) ^ other_core(intra)]
    own = jnp.arange(towers)[:, None, None] == lax.axis_index("tower")
    order = jnp.where(own, order, crossed).transpose(1, 0, 2)
    me = lax.axis_index("intra")
    table = jnp.concatenate([embeddings, *parts], axis=1)
    blocks = []
    for s in steps(intra, pair):
        mine = lax.dynamic_index_in_dim(order, partner(me, s, intra, pair), keepdims=False).reshape(-1)
        blocks.append(jnp.take(table, mine, axis=0).reshape(rows, held, EDIM).transpose(1, 0, 2))
    assign = small[0][0]
    same = assign[None, :] == jnp.arange(assign.size)[:, None]
    slots = jnp.sum(jnp.where(same, jnp.arange(assign.size)[None, :], 0), axis=1)
    return blocks, (slots.astype(assign.dtype)[None, :], *small[1:])


def first_layer(intra, pair, order, slots_ref, w1_ref, x_ref, blocks, before_ref=None):
    held, rows, _ = blocks[0].shape
    held //= pair
    count, depth, hid = w1_ref.shape
    per_tower = depth // EDIM
    me = lax.axis_index("intra")
    slots = []
    for s, block in zip(order, blocks):
        source = partner(me, -s, intra, pair)
        for q in range(pair):
            for f in range(held):
                slot = slots_ref[0, (source ^ q) * held + f]
                n = len(slots)
                slots.append((slot // per_tower, pl.multiple_of((slot % per_tower) * EDIM, EDIM)))
                for k in range(count):
                    own = jnp.where(slots[n][0] == k, 1.0, 0.0).astype(jnp.bfloat16)
                    x_ref[k * rows : (k + 1) * rows, n * EDIM : (n + 1) * EDIM] = block[q * held + f] * own
    wide = 2 * EDIM
    for h in range(0, hid, wide):
        columns = slice(h, min(h + wide, hid))
        total = None if before_ref is None else before_ref[:, columns]
        for n in range(0, len(slots), 2):
            some = slots[n : n + 2]
            weight = [w1_ref[k, pl.ds(start, EDIM), columns] for k, start in some]
            term = jnp.dot(
                x_ref[:, n * EDIM : (n + len(some)) * EDIM],
                jnp.concatenate(weight, axis=0),
                preferred_element_type=jnp.float32,
            )
            total = term if total is None else total + term
        yield columns, total


def early_kernel(intra, pair, order, slots_ref, w1_ref, *rest):
    blocks, before, (out_ref, x_ref) = rest[: len(order)], rest[len(order) : -2], rest[-2:]
    for columns, total in first_layer(intra, pair, order, slots_ref, w1_ref, x_ref, blocks, *before):
        out_ref[:, columns] = total


def tower_kernel(towers, intra, pair, order, slots_ref, w1_ref, b1_ref, w2_ref, b2_ref, sums_ref, *rest):
    blocks, outs, (x_ref, hidden_ref, y_ref) = rest[: len(order)], rest[len(order) : -3], rest[-3:]
    count, rows, _ = y_ref.shape
    vectors = w2_ref.shape[2] // EDIM
    per = rows // towers
    for columns, total in first_layer(intra, pair, order, slots_ref, w1_ref, x_ref, blocks, sums_ref):
        for k in range(count):
            hidden = total[k * rows : (k + 1) * rows] + b1_ref[k : k + 1, columns]
            hidden_ref[k, :, columns] = jnp.maximum(hidden, 0.0).astype(jnp.bfloat16)
    for k in range(count):
        result = jnp.dot(hidden_ref[k], w2_ref[k], preferred_element_type=jnp.float32)
        y_ref[k] = jnp.maximum(result + b2_ref[k : k + 1, :], 0.0)
    place = lax.axis_index("tower")
    for o, out in zip(offsets(towers), outs):
        start = pl.multiple_of((place ^ o) * per, per)
        pieces = [
            y_ref[k, pl.ds(start, per), v * EDIM : (v + 1) * EDIM]
            for k in range(count)
            for v in range(vectors)
        ]
        out[...] = jnp.concatenate(pieces, axis=0).astype(out.dtype)


def run_towers(slots, w1, b1, w2, b2, blocks, towers, intra, pair):
    order, blocks = zip(*blocks)
    remote = len(blocks) - 1
    last = max(remote - 2, 0)
    cuts = (0, (last + 1) // 2, last)
    stages = [[-1, *range(*cuts[:2])], [*range(*cuts[1:])]]
    late = [*range(last, remote)]
    held, rows, _ = blocks[0].shape
    count, depth, hid = w1.shape
    width = w2.shape[2]
    local = count * (width // EDIM) * (rows // towers)
    w1 = pltpu.with_memory_space_constraint(w1, pltpu.VMEM)
    w2 = pltpu.with_memory_space_constraint(w2, pltpu.VMEM)
    params = pltpu.CompilerParams(vmem_limit_bytes=16 << 20)
    sums = ()
    for stage in stages:
        if not stage:
            continue
        sums = pl.pallas_call(
            functools.partial(early_kernel, intra, pair, [order[n] for n in stage]),
            out_shape=[pltpu.VMEM((count * rows, hid), jnp.float32)],
            in_specs=[pl.BlockSpec(memory_space=pltpu.SMEM)]
            + [pl.BlockSpec(memory_space=pltpu.VMEM)] * (1 + len(stage) + len(sums)),
            out_specs=[pl.BlockSpec(memory_space=pltpu.VMEM)],
            scratch_shapes=[pltpu.VMEM((count * rows, len(stage) * held * EDIM), jnp.bfloat16)],
            compiler_params=params,
            cost_estimate=pl.CostEstimate(
                flops=2 * count * rows * depth * hid, bytes_accessed=0, transcendentals=0
            ),
            name="towers_early",
        )(slots, w1, *(blocks[n] for n in stage), *sums)
    return pl.pallas_call(
        functools.partial(tower_kernel, towers, intra, pair, [order[n] for n in late]),
        out_shape=[pltpu.VMEM((local, EDIM), jnp.bfloat16)] * towers,
        in_specs=[pl.BlockSpec(memory_space=pltpu.SMEM)]
        + [pl.BlockSpec(memory_space=pltpu.VMEM)] * (5 + len(late)),
        out_specs=[pl.BlockSpec(memory_space=pltpu.VMEM)] * towers,
        scratch_shapes=[
            pltpu.VMEM((count * rows, max(len(late), 1) * held * EDIM), jnp.bfloat16),
            pltpu.VMEM((count, rows, hid), jnp.bfloat16),
            pltpu.VMEM((count, rows, width), jnp.float32),
        ],
        compiler_params=params,
        name="towers",
    )(slots, w1, b1, w2, b2, *sums, *(blocks[n] for n in late))


def interact_kernel(towers, proj_ref, *rest):
    blocks, out, all_ref = rest[:towers], rest[towers], rest[towers + 1]
    per, count, _ = out.shape
    local = blocks[0].shape[0]
    place = lax.axis_index("tower")
    for o, block in zip(offsets(towers), blocks):
        start = pl.multiple_of((place ^ o) * local, local)
        all_ref[pl.ds(start, local), :] = block[...].astype(jnp.float32)
    group = max(1, min(per, 128 // count))
    proj = jnp.concatenate([proj_ref[...]] * (2 * group), axis=0)
    for first in range(0, per, group):
        samples = range(first, first + group)
        vectors = [all_ref[pl.ds(d, count, stride=per), :] for d in samples]
        vectors = jnp.concatenate(vectors, axis=0).astype(jnp.bfloat16)
        gram = lax.dot_general(
            vectors, vectors, (((1,), (1,)), ((), ())), preferred_element_type=jnp.float32
        )
        gram = gram * (1.0 / EDIM)
        column = lax.broadcasted_iota(jnp.int32, (count, gram.shape[1]), 1)
        own = [
            jnp.where(
                (column >= g * count) & (column < (g + 1) * count),
                gram[g * count : (g + 1) * count, :],
                0.0,
            )
            for g in range(group)
        ]
        gram = jnp.concatenate(own, axis=0)
        high = gram.astype(jnp.bfloat16)
        low = (gram - high.astype(jnp.float32)).astype(jnp.bfloat16)
        result = jnp.dot(
            jnp.concatenate([high, low], axis=1), proj, preferred_element_type=jnp.float32
        )
        for g, d in enumerate(samples):
            out[d] = result[g * count : (g + 1) * count, :].astype(out.dtype)


def interact(proj, blocks):
    towers = len(blocks)
    local = blocks[0].shape[0]
    count = proj.shape[0]
    per = towers * local // count
    return pl.pallas_call(
        functools.partial(interact_kernel, towers),
        out_shape=jax.ShapeDtypeStruct((per, count, EDIM), jnp.bfloat16),
        in_specs=[pl.BlockSpec(memory_space=pltpu.VMEM)] * (1 + towers),
        out_specs=pl.BlockSpec(memory_space=pltpu.VMEM),
        scratch_shapes=[pltpu.VMEM((towers * local, EDIM), jnp.float32)],
        compiler_params=pltpu.CompilerParams(vmem_limit_bytes=8 << 20),
        name="interact",
    )(proj, *blocks)


def shards(
    embeddings,
    feature_assign,
    sample_owner,
    first_weight,
    first_bias,
    tower_weight,
    tower_bias,
    proj_weight,
):
    towers, intra = lax.axis_size("tower"), lax.axis_size("intra")
    small = (feature_assign, first_bias, tower_bias, proj_weight)
    ahead = 10_000 * (first_weight.size + tower_weight.size)
    pair = 2 if intra % 2 == 0 else 1
    blocks, small = gather_blocks(sample_owner, embeddings, small, towers, intra, pair, ahead)
    slots, first_bias, tower_bias, proj_weight = small
    blocks = exchange_chips(blocks, intra, pair)
    vectors = run_towers(
        slots, first_weight, first_bias, tower_weight, tower_bias, blocks, towers, intra, pair
    )
    vectors = exchange_groups(vectors, towers, intra)
    return interact(proj_weight, vectors)


def solution(mesh):
    return jax.shard_map(
        shards,
        mesh=mesh,
        in_specs=(
            P(None, ("tower", "intra")),
            P("tower", None),
            P(),
            P("tower", None, None),
            P("tower", None),
            P("tower", None, None),
            P("tower", None),
            P(),
        ),
        out_specs=P(("tower", "intra"), None, None),
        check_vma=False,
    )
```

```python
import functools

import jax
import jax.numpy as jnp
from jax import lax
from jax.experimental import pallas as pl
from jax.experimental.pallas import tpu as pltpu
from jax.sharding import PartitionSpec as P

EDIM = 128
FEW_SAMPLES = 1024


def offsets(size):
    return range(size - 1, -1, -1)


def steps(intra, pair):
    return (*range(1, intra // pair), 0)


def ring_place(chip, chips):
    place = chip
    bits = (chips - 1).bit_length() if chips & (chips - 1) == 0 else 0
    for n in range(1, bits):
        place = place ^ (chip >> n)
    return place


def ring_chip(place, chips):
    return place ^ (place >> 1) if chips & (chips - 1) == 0 else place


def partner(me, step, intra, pair):
    chips = intra // pair
    place = (ring_place(me // pair, chips) + step + chips) % chips
    return ring_chip(place, chips) * pair + (me % pair + (pair - 1 if step else 0)) % pair


def exchange_chips(blocks, intra, pair):
    return [
        lax.ppermute(block, "intra", [(i, partner(i, s, intra, pair)) for i in range(intra)]) if s else block
        for block, s in zip(blocks, steps(intra, pair))
    ]


def other_core(intra):
    return 1 if intra > 1 else 0


def exchange_groups(blocks, towers, intra):
    received = []
    for block, o in zip(blocks, offsets(towers)):
        pairs = [
            (t * intra + i, (t ^ o) * intra + (i ^ other_core(intra)))
            for t in range(towers)
            for i in range(intra)
        ]
        received.append(lax.ppermute(block, ("tower", "intra"), pairs) if o else block)
    return received


def load_kernel(count, owner_hbm, emb_hbm, *rest):
    small, (picks_ref, emb_ref, slots_ref), copies = rest[:count], rest[count : count + 3], rest[count + 3 : -3]
    owner_ref, assign_ref, sems = rest[-3:]
    targets = (assign_ref, *copies)
    pairs = [(owner_hbm, owner_ref), (emb_hbm, emb_ref), *zip(small, targets)]
    loads = [pltpu.make_async_copy(a, b, sems.at[i]) for i, (a, b) in enumerate(pairs)]
    for load in loads:
        load.start()
    samples = emb_ref.shape[0]
    loads[0].wait()
    owner = jnp.broadcast_to(owner_ref[...].reshape(1, samples), (samples, samples))
    picks = lax.broadcasted_iota(jnp.int32, (samples, samples), 0) == owner
    picks_ref[...] = jnp.where(picks, 1.0, 0.0).astype(jnp.bfloat16)
    loads[2].wait()
    for slot in range(assign_ref.shape[1]):
        slots_ref[0, assign_ref[0, slot]] = slot
    for load in (loads[1], *loads[3:]):
        load.wait()


def gather_kernel(towers, intra, pair, picks_ref, *rest):
    parts, outs, acc_ref = rest[:pair], rest[pair:-1], rest[-1]
    samples, width = parts[0].shape
    per = samples // (towers * intra)
    held = width // EDIM
    me, place = lax.axis_index("intra"), lax.axis_index("tower")
    for q, part in enumerate(parts):
        acc_ref[:, q * width : (q + 1) * width] = lax.dot_general(
            picks_ref[...], part[...], (((0,), (0,)), ((), ())), preferred_element_type=jnp.float32
        )
    for s, out in zip(steps(intra, pair), outs):
        block = partner(me, s, intra, pair)
        owners = [jnp.where(place == t, block, block ^ other_core(intra)) for t in range(towers)]
        starts = [pl.multiple_of((t * intra + owners[t]) * per, per) for t in range(towers)]
        for f in range(pair * held):
            columns = slice(f * EDIM, (f + 1) * EDIM)
            rows = [acc_ref[pl.ds(start, per), columns] for start in starts]
            out[f] = jnp.concatenate(rows, axis=0).astype(out.dtype)


def gather_blocks(owner, embeddings, small, towers, intra, pair, ahead):
    samples, width = embeddings.shape
    rows, held = samples // intra, pair * width // EDIM
    parts = [lax.ppermute(embeddings, "intra", [(i, i ^ q) for i in range(intra)]) for q in range(1, pair)]
    if samples <= FEW_SAMPLES:
        given = [pltpu.with_memory_space_constraint(a, pltpu.HBM) for a in (owner, embeddings, *small)]
        picks, embeddings, *small = pl.pallas_call(
            functools.partial(load_kernel, len(small)),
            out_shape=[
                pltpu.VMEM((samples, samples), jnp.bfloat16),
                pltpu.VMEM(embeddings.shape, embeddings.dtype),
                pltpu.SMEM(small[0].shape, small[0].dtype),
            ]
            + [pltpu.VMEM(a.shape, a.dtype) for a in small[1:]],
            in_specs=[pl.BlockSpec(memory_space=pltpu.HBM)] * len(given),
            out_specs=[pl.BlockSpec(memory_space=pltpu.VMEM)] * 2
            + [pl.BlockSpec(memory_space=pltpu.SMEM)]
            + [pl.BlockSpec(memory_space=pltpu.VMEM)] * (len(small) - 1),
            scratch_shapes=[
                pltpu.VMEM(owner.shape, owner.dtype),
                pltpu.SMEM(small[0].shape, small[0].dtype),
                pltpu.SemaphoreType.DMA((len(given),)),
            ],
            compiler_params=pltpu.CompilerParams(vmem_limit_bytes=8 << 20),
            name="load",
        )(*given)
        blocks = pl.pallas_call(
            functools.partial(gather_kernel, towers, intra, pair),
            out_shape=[pltpu.VMEM((held, rows, EDIM), embeddings.dtype)] * (intra // pair),
            in_specs=[pl.BlockSpec(memory_space=pltpu.VMEM)] * (1 + pair),
            out_specs=[pl.BlockSpec(memory_space=pltpu.VMEM)] * (intra // pair),
            scratch_shapes=[pltpu.VMEM((samples, pair * width), jnp.float32)],
            compiler_params=pltpu.CompilerParams(vmem_limit_bytes=8 << 20),
            cost_estimate=pl.CostEstimate(flops=ahead, bytes_accessed=0, transcendentals=0),
            name="gather_rows",
        )(picks, embeddings, *parts)
        return blocks, small
    order = owner.reshape(towers, intra, -1)
    crossed = order[:, jnp.arange(intra) ^ other_core(intra)]
    own = jnp.arange(towers)[:, None, None] == lax.axis_index("tower")
    order = jnp.where(own, order, crossed).transpose(1, 0, 2)
    me = lax.axis_index("intra")
    table = jnp.concatenate([embeddings, *parts], axis=1)
    blocks = []
    for s in steps(intra, pair):
        mine = lax.dynamic_index_in_dim(order, partner(me, s, intra, pair), keepdims=False).reshape(-1)
        blocks.append(jnp.take(table, mine, axis=0).reshape(rows, held, EDIM).transpose(1, 0, 2))
    assign = small[0][0]
    same = assign[None, :] == jnp.arange(assign.size)[:, None]
    slots = jnp.sum(jnp.where(same, jnp.arange(assign.size)[None, :], 0), axis=1)
    return blocks, (slots.astype(assign.dtype)[None, :], *small[1:])


def first_layer(intra, pair, order, slots_ref, w1_ref, x_ref, blocks, before_ref=None):
    held, rows, _ = blocks[0].shape
    held //= pair
    count, depth, hid = w1_ref.shape
    per_tower = depth // EDIM
    me = lax.axis_index("intra")
    slots = []
    for s, block in zip(order, blocks):
        source = partner(me, -s, intra, pair)
        for q in range(pair):
            for f in range(held):
                slot = slots_ref[0, (source ^ q) * held + f]
                n = len(slots)
                slots.append((slot // per_tower, pl.multiple_of((slot % per_tower) * EDIM, EDIM)))
                for k in range(count):
                    own = jnp.where(slots[n][0] == k, 1.0, 0.0).astype(jnp.bfloat16)
                    x_ref[k * rows : (k + 1) * rows, n * EDIM : (n + 1) * EDIM] = block[q * held + f] * own
    wide = 2 * EDIM
    for h in range(0, hid, wide):
        columns = slice(h, min(h + wide, hid))
        weight = [w1_ref[k, pl.ds(start, EDIM), columns] for k, start in slots]
        total = jnp.dot(x_ref[...], jnp.concatenate(weight, axis=0), preferred_element_type=jnp.float32)
        if before_ref is not None:
            total = total + before_ref[:, columns]
        yield columns, total


def early_kernel(intra, pair, order, slots_ref, w1_ref, *rest):
    blocks, before, (out_ref, x_ref) = rest[: len(order)], rest[len(order) : -2], rest[-2:]
    for columns, total in first_layer(intra, pair, order, slots_ref, w1_ref, x_ref, blocks, *before):
        out_ref[:, columns] = total


def tower_kernel(towers, intra, pair, order, slots_ref, w1_ref, b1_ref, w2_ref, b2_ref, sums_ref, *rest):
    blocks, outs, (x_ref, y_ref) = rest[: len(order)], rest[len(order) : -2], rest[-2:]
    count, rows, _ = y_ref.shape
    vectors = w2_ref.shape[2] // EDIM
    per = rows // towers
    results = [None] * count
    for columns, total in first_layer(intra, pair, order, slots_ref, w1_ref, x_ref, blocks, sums_ref):
        for k in range(count):
            hidden = total[k * rows : (k + 1) * rows] + b1_ref[k : k + 1, columns]
            hidden = jnp.maximum(hidden, 0.0).astype(jnp.bfloat16)
            term = jnp.dot(hidden, w2_ref[k, columns, :], preferred_element_type=jnp.float32)
            results[k] = term if results[k] is None else results[k] + term
    for k in range(count):
        y_ref[k] = jnp.maximum(results[k] + b2_ref[k : k + 1, :], 0.0)
    place = lax.axis_index("tower")
    for o, out in zip(offsets(towers), outs):
        start = pl.multiple_of((place ^ o) * per, per)
        pieces = [
            y_ref[k, pl.ds(start, per), v * EDIM : (v + 1) * EDIM]
            for k in range(count)
            for v in range(vectors)
        ]
        out[...] = jnp.concatenate(pieces, axis=0).astype(out.dtype)


def run_towers(slots, w1, b1, w2, b2, blocks, towers, intra, pair):
    order = steps(intra, pair)
    remote = len(blocks) - 1
    cuts = (0, max(remote // 2, min(remote - 1, 1)), remote - 1)
    stages = [[-1, *range(*cuts[:2])], [*range(*cuts[1:])]]
    late = [remote - 1] if remote else []
    held, rows, _ = blocks[0].shape
    count, depth, hid = w1.shape
    width = w2.shape[2]
    local = count * (width // EDIM) * (rows // towers)
    w1 = pltpu.with_memory_space_constraint(w1, pltpu.VMEM)
    w2 = pltpu.with_memory_space_constraint(w2, pltpu.VMEM)
    params = pltpu.CompilerParams(vmem_limit_bytes=16 << 20)
    sums = ()
    for stage in stages:
        if not stage:
            continue
        sums = pl.pallas_call(
            functools.partial(early_kernel, intra, pair, [order[n] for n in stage]),
            out_shape=[pltpu.VMEM((count * rows, hid), jnp.float32)],
            in_specs=[pl.BlockSpec(memory_space=pltpu.SMEM)]
            + [pl.BlockSpec(memory_space=pltpu.VMEM)] * (1 + len(stage) + len(sums)),
            out_specs=[pl.BlockSpec(memory_space=pltpu.VMEM)],
            scratch_shapes=[pltpu.VMEM((count * rows, len(stage) * held * EDIM), jnp.bfloat16)],
            compiler_params=params,
            cost_estimate=pl.CostEstimate(
                flops=2 * count * rows * depth * hid, bytes_accessed=0, transcendentals=0
            ),
            name="towers_early",
        )(slots, w1, *(blocks[n] for n in stage), *sums)
    return pl.pallas_call(
        functools.partial(tower_kernel, towers, intra, pair, [order[n] for n in late]),
        out_shape=[pltpu.VMEM((local, EDIM), jnp.bfloat16)] * towers,
        in_specs=[pl.BlockSpec(memory_space=pltpu.SMEM)]
        + [pl.BlockSpec(memory_space=pltpu.VMEM)] * (5 + len(late)),
        out_specs=[pl.BlockSpec(memory_space=pltpu.VMEM)] * towers,
        scratch_shapes=[
            pltpu.VMEM((count * rows, max(len(late), 1) * held * EDIM), jnp.bfloat16),
            pltpu.VMEM((count, rows, width), jnp.float32),
        ],
        compiler_params=params,
        name="towers",
    )(slots, w1, b1, w2, b2, *sums, *(blocks[n] for n in late))


def interact_kernel(towers, proj_ref, *rest):
    blocks, out, all_ref = rest[:towers], rest[towers], rest[towers + 1]
    per, count, _ = out.shape
    local = blocks[0].shape[0]
    place = lax.axis_index("tower")
    for o, block in zip(offsets(towers), blocks):
        start = pl.multiple_of((place ^ o) * local, local)
        all_ref[pl.ds(start, local), :] = block[...].astype(jnp.float32)
    group = max(1, min(per, 128 // count))
    proj = jnp.concatenate([proj_ref[...]] * (2 * group), axis=0)
    for first in range(0, per, group):
        samples = range(first, first + group)
        vectors = [all_ref[pl.ds(d, count, stride=per), :] for d in samples]
        vectors = jnp.concatenate(vectors, axis=0).astype(jnp.bfloat16)
        gram = lax.dot_general(
            vectors, vectors, (((1,), (1,)), ((), ())), preferred_element_type=jnp.float32
        )
        gram = gram * (1.0 / EDIM)
        column = lax.broadcasted_iota(jnp.int32, (count, gram.shape[1]), 1)
        own = [
            jnp.where(
                (column >= g * count) & (column < (g + 1) * count),
                gram[g * count : (g + 1) * count, :],
                0.0,
            )
            for g in range(group)
        ]
        gram = jnp.concatenate(own, axis=0)
        high = gram.astype(jnp.bfloat16)
        low = (gram - high.astype(jnp.float32)).astype(jnp.bfloat16)
        result = jnp.dot(
            jnp.concatenate([high, low], axis=1), proj, preferred_element_type=jnp.float32
        )
        for g, d in enumerate(samples):
            out[d] = result[g * count : (g + 1) * count, :].astype(out.dtype)


def interact(proj, blocks):
    towers = len(blocks)
    local = blocks[0].shape[0]
    count = proj.shape[0]
    per = towers * local // count
    return pl.pallas_call(
        functools.partial(interact_kernel, towers),
        out_shape=jax.ShapeDtypeStruct((per, count, EDIM), jnp.bfloat16),
        in_specs=[pl.BlockSpec(memory_space=pltpu.VMEM)] * (1 + towers),
        out_specs=pl.BlockSpec(memory_space=pltpu.VMEM),
        scratch_shapes=[pltpu.VMEM((towers * local, EDIM), jnp.float32)],
        compiler_params=pltpu.CompilerParams(vmem_limit_bytes=8 << 20),
        name="interact",
    )(proj, *blocks)


def shards(
    embeddings,
    feature_assign,
    sample_owner,
    first_weight,
    first_bias,
    tower_weight,
    tower_bias,
    proj_weight,
):
    towers, intra = lax.axis_size("tower"), lax.axis_size("intra")
    small = (feature_assign, first_bias, tower_bias, proj_weight)
    ahead = 10_000 * (first_weight.size + tower_weight.size)
    pair = 2 if intra % 2 == 0 else 1
    blocks, small = gather_blocks(sample_owner, embeddings, small, towers, intra, pair, ahead)
    slots, first_bias, tower_bias, proj_weight = small
    blocks = exchange_chips(blocks, intra, pair)
    vectors = run_towers(
        slots, first_weight, first_bias, tower_weight, tower_bias, blocks, towers, intra, pair
    )
    vectors = exchange_groups(vectors, towers, intra)
    return interact(proj_weight, vectors)


def solution(mesh):
    return jax.shard_map(
        shards,
        mesh=mesh,
        in_specs=(
            P(None, ("tower", "intra")),
            P("tower", None),
            P(),
            P("tower", None, None),
            P("tower", None),
            P("tower", None, None),
            P("tower", None),
            P(),
        ),
        out_specs=P(("tower", "intra"), None, None),
        check_vma=False,
    )
```

```python
import functools

import jax
import jax.numpy as jnp
from jax import lax
from jax.experimental import pallas as pl
from jax.experimental.pallas import tpu as pltpu
from jax.sharding import PartitionSpec as P

EDIM = 128
FEW_SAMPLES = 1024


def offsets(size):
    return range(size - 1, -1, -1)


def steps(intra, pair):
    return (*range(1, intra // pair), 0)


def ring_place(chip, chips):
    place = chip
    bits = (chips - 1).bit_length() if chips & (chips - 1) == 0 else 0
    for n in range(1, bits):
        place = place ^ (chip >> n)
    return place


def ring_chip(place, chips):
    return place ^ (place >> 1) if chips & (chips - 1) == 0 else place


def partner(me, step, intra, pair):
    chips = intra // pair
    place = (ring_place(me // pair, chips) + step + chips) % chips
    return ring_chip(place, chips) * pair + (me % pair + (pair - 1 if step else 0)) % pair


def exchange_chips(blocks, intra, pair):
    return [
        lax.ppermute(block, "intra", [(i, partner(i, s, intra, pair)) for i in range(intra)]) if s else block
        for block, s in zip(blocks, steps(intra, pair))
    ]


def other_core(intra):
    return 1 if intra > 1 else 0


def exchange_groups(blocks, towers, intra):
    received = []
    for block, o in zip(blocks, offsets(towers)):
        pairs = [
            (t * intra + i, (t ^ o) * intra + (i ^ other_core(intra)))
            for t in range(towers)
            for i in range(intra)
        ]
        received.append(lax.ppermute(block, ("tower", "intra"), pairs) if o else block)
    return received


def load_kernel(towers, intra, pair, count, owner_hbm, emb_hbm, *rest):
    small, (picks_ref, emb_ref, slots_ref), copies = rest[:count], rest[count : count + 3], rest[count + 3 : -3]
    owner_ref, assign_ref, sems = rest[-3:]
    targets = (assign_ref, *copies)
    pairs = [(owner_hbm, owner_ref), (emb_hbm, emb_ref), *zip(small, targets)]
    loads = [pltpu.make_async_copy(a, b, sems.at[i]) for i, (a, b) in enumerate(pairs)]
    for load in loads:
        load.start()
    samples = emb_ref.shape[0]
    per = samples // (towers * intra)
    me, place = lax.axis_index("intra"), lax.axis_index("tower")
    lane = lax.broadcasted_iota(jnp.int32, (per, samples), 1) - lax.broadcasted_iota(jnp.int32, (per, samples), 0)
    chosen = []
    for s in steps(intra, pair):
        block = partner(me, s, intra, pair)
        for t in range(towers):
            owner = jnp.where(place == t, block, block ^ other_core(intra))
            chosen.append(jnp.where(lane == (t * intra + owner) * per, 1.0, 0.0))
    chosen = jnp.concatenate(chosen, axis=0).astype(jnp.bfloat16)
    loads[0].wait()
    owner = jnp.broadcast_to(owner_ref[...].reshape(1, samples), (samples, samples))
    picks = lax.broadcasted_iota(jnp.int32, (samples, samples), 0) == owner
    picks = jnp.where(picks, 1.0, 0.0).astype(jnp.bfloat16)
    picks_ref[...] = lax.dot_general(
        chosen, picks, (((1,), (1,)), ((), ())), preferred_element_type=jnp.float32
    ).astype(jnp.bfloat16)
    loads[2].wait()
    for slot in range(assign_ref.shape[1]):
        slots_ref[0, assign_ref[0, slot]] = slot
    for load in (loads[1], *loads[3:]):
        load.wait()


def gather_kernel(pair, picks_ref, *rest):
    parts, outs = rest[:pair], rest[pair:]
    held = parts[0].shape[1] // EDIM
    rows = outs[0].shape[1]
    for q, part in enumerate(parts):
        ordered = jnp.dot(picks_ref[...], part[...], preferred_element_type=jnp.float32)
        for n, out in enumerate(outs):
            for f in range(held):
                block = ordered[n * rows : (n + 1) * rows, f * EDIM : (f + 1) * EDIM]
                out[q * held + f] = block.astype(out.dtype)


def gather_blocks(owner, embeddings, small, towers, intra, pair, ahead):
    samples, width = embeddings.shape
    rows, held = samples // intra, pair * width // EDIM
    parts = [lax.ppermute(embeddings, "intra", [(i, i ^ q) for i in range(intra)]) for q in range(1, pair)]
    if samples <= FEW_SAMPLES:
        given = [pltpu.with_memory_space_constraint(a, pltpu.HBM) for a in (owner, embeddings, *small)]
        picks, embeddings, *small = pl.pallas_call(
            functools.partial(load_kernel, towers, intra, pair, len(small)),
            out_shape=[
                pltpu.VMEM((samples // pair, samples), jnp.bfloat16),
                pltpu.VMEM(embeddings.shape, embeddings.dtype),
                pltpu.SMEM(small[0].shape, small[0].dtype),
            ]
            + [pltpu.VMEM(a.shape, a.dtype) for a in small[1:]],
            in_specs=[pl.BlockSpec(memory_space=pltpu.HBM)] * len(given),
            out_specs=[pl.BlockSpec(memory_space=pltpu.VMEM)] * 2
            + [pl.BlockSpec(memory_space=pltpu.SMEM)]
            + [pl.BlockSpec(memory_space=pltpu.VMEM)] * (len(small) - 1),
            scratch_shapes=[
                pltpu.VMEM(owner.shape, owner.dtype),
                pltpu.SMEM(small[0].shape, small[0].dtype),
                pltpu.SemaphoreType.DMA((len(given),)),
            ],
            compiler_params=pltpu.CompilerParams(vmem_limit_bytes=8 << 20),
            name="load",
        )(*given)
        blocks = pl.pallas_call(
            functools.partial(gather_kernel, pair),
            out_shape=[pltpu.VMEM((held, rows, EDIM), embeddings.dtype)] * (intra // pair),
            in_specs=[pl.BlockSpec(memory_space=pltpu.VMEM)] * (1 + pair),
            out_specs=[pl.BlockSpec(memory_space=pltpu.VMEM)] * (intra // pair),
            compiler_params=pltpu.CompilerParams(vmem_limit_bytes=8 << 20),
            cost_estimate=pl.CostEstimate(flops=ahead, bytes_accessed=0, transcendentals=0),
            name="gather_rows",
        )(picks, embeddings, *parts)
        return blocks, small
    order = owner.reshape(towers, intra, -1)
    crossed = order[:, jnp.arange(intra) ^ other_core(intra)]
    own = jnp.arange(towers)[:, None, None] == lax.axis_index("tower")
    order = jnp.where(own, order, crossed).transpose(1, 0, 2)
    me = lax.axis_index("intra")
    table = jnp.concatenate([embeddings, *parts], axis=1)
    blocks = []
    for s in steps(intra, pair):
        mine = lax.dynamic_index_in_dim(order, partner(me, s, intra, pair), keepdims=False).reshape(-1)
        blocks.append(jnp.take(table, mine, axis=0).reshape(rows, held, EDIM).transpose(1, 0, 2))
    assign = small[0][0]
    same = assign[None, :] == jnp.arange(assign.size)[:, None]
    slots = jnp.sum(jnp.where(same, jnp.arange(assign.size)[None, :], 0), axis=1)
    return blocks, (slots.astype(assign.dtype)[None, :], *small[1:])


def first_layer(intra, pair, order, slots_ref, w1_ref, x_ref, blocks, before_ref=None):
    held, rows, _ = blocks[0].shape
    held //= pair
    count, depth, hid = w1_ref.shape
    per_tower = depth // EDIM
    me = lax.axis_index("intra")
    slots = []
    for s, block in zip(order, blocks):
        source = partner(me, -s, intra, pair)
        for q in range(pair):
            for f in range(held):
                slot = slots_ref[0, (source ^ q) * held + f]
                n = len(slots)
                slots.append((slot // per_tower, pl.multiple_of((slot % per_tower) * EDIM, EDIM)))
                for k in range(count):
                    own = jnp.where(slots[n][0] == k, 1.0, 0.0).astype(jnp.bfloat16)
                    x_ref[k * rows : (k + 1) * rows, n * EDIM : (n + 1) * EDIM] = block[q * held + f] * own
    wide = 2 * EDIM
    for h in range(0, hid, wide):
        columns = slice(h, min(h + wide, hid))
        total = None if before_ref is None else before_ref[:, columns]
        for n in range(0, len(slots), 2):
            some = slots[n : n + 2]
            weight = [w1_ref[k, pl.ds(start, EDIM), columns] for k, start in some]
            term = jnp.dot(
                x_ref[:, n * EDIM : (n + len(some)) * EDIM],
                jnp.concatenate(weight, axis=0),
                preferred_element_type=jnp.float32,
            )
            total = term if total is None else total + term
        yield columns, total


def early_kernel(intra, pair, order, slots_ref, w1_ref, *rest):
    blocks, before, (out_ref, x_ref) = rest[: len(order)], rest[len(order) : -2], rest[-2:]
    for columns, total in first_layer(intra, pair, order, slots_ref, w1_ref, x_ref, blocks, *before):
        out_ref[:, columns] = total


def tower_kernel(towers, intra, pair, order, slots_ref, w1_ref, b1_ref, w2_ref, b2_ref, sums_ref, *rest):
    blocks, outs, (x_ref, hidden_ref, y_ref) = rest[: len(order)], rest[len(order) : -3], rest[-3:]
    count, rows, _ = y_ref.shape
    vectors = w2_ref.shape[2] // EDIM
    per = rows // towers
    for columns, total in first_layer(intra, pair, order, slots_ref, w1_ref, x_ref, blocks, sums_ref):
        for k in range(count):
            hidden = total[k * rows : (k + 1) * rows] + b1_ref[k : k + 1, columns]
            hidden_ref[k, :, columns] = jnp.maximum(hidden, 0.0).astype(jnp.bfloat16)
    for k in range(count):
        result = jnp.dot(hidden_ref[k], w2_ref[k], preferred_element_type=jnp.float32)
        y_ref[k] = jnp.maximum(result + b2_ref[k : k + 1, :], 0.0)
    place = lax.axis_index("tower")
    for o, out in zip(offsets(towers), outs):
        start = pl.multiple_of((place ^ o) * per, per)
        pieces = [
            y_ref[k, pl.ds(start, per), v * EDIM : (v + 1) * EDIM]
            for k in range(count)
            for v in range(vectors)
        ]
        out[...] = jnp.concatenate(pieces, axis=0).astype(out.dtype)


def run_towers(slots, w1, b1, w2, b2, blocks, towers, intra, pair):
    order = steps(intra, pair)
    remote = len(blocks) - 1
    cuts = (0, max(remote // 2, min(remote - 1, 1)), remote - 1)
    stages = [[-1, *range(*cuts[:2])], [*range(*cuts[1:])]]
    late = [remote - 1] if remote else []
    held, rows, _ = blocks[0].shape
    count, depth, hid = w1.shape
    width = w2.shape[2]
    local = count * (width // EDIM) * (rows // towers)
    w1 = pltpu.with_memory_space_constraint(w1, pltpu.VMEM)
    w2 = pltpu.with_memory_space_constraint(w2, pltpu.VMEM)
    params = pltpu.CompilerParams(vmem_limit_bytes=16 << 20)
    sums = ()
    for stage in stages:
        if not stage:
            continue
        sums = pl.pallas_call(
            functools.partial(early_kernel, intra, pair, [order[n] for n in stage]),
            out_shape=[pltpu.VMEM((count * rows, hid), jnp.float32)],
            in_specs=[pl.BlockSpec(memory_space=pltpu.SMEM)]
            + [pl.BlockSpec(memory_space=pltpu.VMEM)] * (1 + len(stage) + len(sums)),
            out_specs=[pl.BlockSpec(memory_space=pltpu.VMEM)],
            scratch_shapes=[pltpu.VMEM((count * rows, len(stage) * held * EDIM), jnp.bfloat16)],
            compiler_params=params,
            cost_estimate=pl.CostEstimate(
                flops=2 * count * rows * depth * hid, bytes_accessed=0, transcendentals=0
            ),
            name="towers_early",
        )(slots, w1, *(blocks[n] for n in stage), *sums)
    return pl.pallas_call(
        functools.partial(tower_kernel, towers, intra, pair, [order[n] for n in late]),
        out_shape=[pltpu.VMEM((local, EDIM), jnp.bfloat16)] * towers,
        in_specs=[pl.BlockSpec(memory_space=pltpu.SMEM)]
        + [pl.BlockSpec(memory_space=pltpu.VMEM)] * (5 + len(late)),
        out_specs=[pl.BlockSpec(memory_space=pltpu.VMEM)] * towers,
        scratch_shapes=[
            pltpu.VMEM((count * rows, max(len(late), 1) * held * EDIM), jnp.bfloat16),
            pltpu.VMEM((count, rows, hid), jnp.bfloat16),
            pltpu.VMEM((count, rows, width), jnp.float32),
        ],
        compiler_params=params,
        name="towers",
    )(slots, w1, b1, w2, b2, *sums, *(blocks[n] for n in late))


def interact_kernel(towers, proj_ref, *rest):
    blocks, out, all_ref = rest[:towers], rest[towers], rest[towers + 1]
    per, count, _ = out.shape
    local = blocks[0].shape[0]
    place = lax.axis_index("tower")
    for o, block in zip(offsets(towers), blocks):
        start = pl.multiple_of((place ^ o) * local, local)
        all_ref[pl.ds(start, local), :] = block[...].astype(jnp.float32)
    group = max(1, min(per, 128 // count))
    proj = jnp.concatenate([proj_ref[...]] * (2 * group), axis=0)
    for first in range(0, per, group):
        samples = range(first, first + group)
        vectors = [all_ref[pl.ds(d, count, stride=per), :] for d in samples]
        vectors = jnp.concatenate(vectors, axis=0).astype(jnp.bfloat16)
        gram = lax.dot_general(
            vectors, vectors, (((1,), (1,)), ((), ())), preferred_element_type=jnp.float32
        )
        gram = gram * (1.0 / EDIM)
        column = lax.broadcasted_iota(jnp.int32, (count, gram.shape[1]), 1)
        own = [
            jnp.where(
                (column >= g * count) & (column < (g + 1) * count),
                gram[g * count : (g + 1) * count, :],
                0.0,
            )
            for g in range(group)
        ]
        gram = jnp.concatenate(own, axis=0)
        high = gram.astype(jnp.bfloat16)
        low = (gram - high.astype(jnp.float32)).astype(jnp.bfloat16)
        result = jnp.dot(
            jnp.concatenate([high, low], axis=1), proj, preferred_element_type=jnp.float32
        )
        for g, d in enumerate(samples):
            out[d] = result[g * count : (g + 1) * count, :].astype(out.dtype)


def interact(proj, blocks):
    towers = len(blocks)
    local = blocks[0].shape[0]
    count = proj.shape[0]
    per = towers * local // count
    return pl.pallas_call(
        functools.partial(interact_kernel, towers),
        out_shape=jax.ShapeDtypeStruct((per, count, EDIM), jnp.bfloat16),
        in_specs=[pl.BlockSpec(memory_space=pltpu.VMEM)] * (1 + towers),
        out_specs=pl.BlockSpec(memory_space=pltpu.VMEM),
        scratch_shapes=[pltpu.VMEM((towers * local, EDIM), jnp.float32)],
        compiler_params=pltpu.CompilerParams(vmem_limit_bytes=8 << 20),
        name="interact",
    )(proj, *blocks)


def shards(
    embeddings,
    feature_assign,
    sample_owner,
    first_weight,
    first_bias,
    tower_weight,
    tower_bias,
    proj_weight,
):
    towers, intra = lax.axis_size("tower"), lax.axis_size("intra")
    small = (feature_assign, first_bias, tower_bias, proj_weight)
    ahead = 10_000 * (first_weight.size + tower_weight.size)
    pair = 2 if intra % 2 == 0 else 1
    blocks, small = gather_blocks(sample_owner, embeddings, small, towers, intra, pair, ahead)
    slots, first_bias, tower_bias, proj_weight = small
    blocks = exchange_chips(blocks, intra, pair)
    vectors = run_towers(
        slots, first_weight, first_bias, tower_weight, tower_bias, blocks, towers, intra, pair
    )
    vectors = exchange_groups(vectors, towers, intra)
    return interact(proj_weight, vectors)


def solution(mesh):
    return jax.shard_map(
        shards,
        mesh=mesh,
        in_specs=(
            P(None, ("tower", "intra")),
            P("tower", None),
            P(),
            P("tower", None, None),
            P("tower", None),
            P("tower", None, None),
            P("tower", None),
            P(),
        ),
        out_specs=P(("tower", "intra"), None, None),
        check_vma=False,
    )
```

```python
import functools

import jax
import jax.numpy as jnp
from jax import lax
from jax.experimental import pallas as pl
from jax.experimental.pallas import tpu as pltpu
from jax.sharding import PartitionSpec as P

EDIM = 128
FEW_SAMPLES = 1024


def offsets(size):
    return range(size - 1, -1, -1)


def steps(intra, pair):
    return (*range(1, intra // pair), 0)


def partner(me, step, intra, pair):
    chips = intra // pair
    return (me // pair + step + chips) % chips * pair + (me % pair + (pair - 1 if step else 0)) % pair


def exchange_chips(blocks, intra, pair):
    return [
        lax.ppermute(block, "intra", [(i, partner(i, s, intra, pair)) for i in range(intra)]) if s else block
        for block, s in zip(blocks, steps(intra, pair))
    ]


def other_core(intra):
    return 1 if intra > 1 else 0


def exchange_groups(blocks, towers, intra):
    received = []
    for block, o in zip(blocks, offsets(towers)):
        pairs = [
            (t * intra + i, (t ^ o) * intra + (i ^ other_core(intra)))
            for t in range(towers)
            for i in range(intra)
        ]
        received.append(lax.ppermute(block, ("tower", "intra"), pairs) if o else block)
    return received


def load_kernel(towers, intra, pair, count, owner_hbm, emb_hbm, *rest):
    small, (picks_ref, emb_ref, slots_ref), copies = rest[:count], rest[count : count + 3], rest[count + 3 : -3]
    owner_ref, assign_ref, sems = rest[-3:]
    targets = (assign_ref, *copies)
    pairs = [(owner_hbm, owner_ref), (emb_hbm, emb_ref), *zip(small, targets)]
    loads = [pltpu.make_async_copy(a, b, sems.at[i]) for i, (a, b) in enumerate(pairs)]
    for load in loads:
        load.start()
    samples = emb_ref.shape[0]
    per = samples // (towers * intra)
    me, place = lax.axis_index("intra"), lax.axis_index("tower")
    lane = lax.broadcasted_iota(jnp.int32, (per, samples), 1) - lax.broadcasted_iota(jnp.int32, (per, samples), 0)
    chosen = []
    for s in steps(intra, pair):
        block = partner(me, s, intra, pair)
        for t in range(towers):
            owner = jnp.where(place == t, block, block ^ other_core(intra))
            chosen.append(jnp.where(lane == (t * intra + owner) * per, 1.0, 0.0))
    chosen = jnp.concatenate(chosen, axis=0).astype(jnp.bfloat16)
    loads[0].wait()
    owner = jnp.broadcast_to(owner_ref[...].reshape(1, samples), (samples, samples))
    picks = lax.broadcasted_iota(jnp.int32, (samples, samples), 0) == owner
    picks = jnp.where(picks, 1.0, 0.0).astype(jnp.bfloat16)
    picks_ref[...] = lax.dot_general(
        chosen, picks, (((1,), (1,)), ((), ())), preferred_element_type=jnp.float32
    ).astype(jnp.bfloat16)
    loads[2].wait()
    for slot in range(assign_ref.shape[1]):
        slots_ref[0, assign_ref[0, slot]] = slot
    for load in (loads[1], *loads[3:]):
        load.wait()


def gather_kernel(pair, picks_ref, *rest):
    parts, outs = rest[:pair], rest[pair:]
    held = parts[0].shape[1] // EDIM
    rows = outs[0].shape[1]
    for q, part in enumerate(parts):
        ordered = jnp.dot(picks_ref[...], part[...], preferred_element_type=jnp.float32)
        for n, out in enumerate(outs):
            for f in range(held):
                block = ordered[n * rows : (n + 1) * rows, f * EDIM : (f + 1) * EDIM]
                out[q * held + f] = block.astype(out.dtype)


def gather_blocks(owner, embeddings, small, towers, intra, pair, ahead):
    samples, width = embeddings.shape
    rows, held = samples // intra, pair * width // EDIM
    parts = [lax.ppermute(embeddings, "intra", [(i, i ^ q) for i in range(intra)]) for q in range(1, pair)]
    if samples <= FEW_SAMPLES:
        given = [pltpu.with_memory_space_constraint(a, pltpu.HBM) for a in (owner, embeddings, *small)]
        picks, embeddings, *small = pl.pallas_call(
            functools.partial(load_kernel, towers, intra, pair, len(small)),
            out_shape=[
                pltpu.VMEM((samples // pair, samples), jnp.bfloat16),
                pltpu.VMEM(embeddings.shape, embeddings.dtype),
                pltpu.SMEM(small[0].shape, small[0].dtype),
            ]
            + [pltpu.VMEM(a.shape, a.dtype) for a in small[1:]],
            in_specs=[pl.BlockSpec(memory_space=pltpu.HBM)] * len(given),
            out_specs=[pl.BlockSpec(memory_space=pltpu.VMEM)] * 2
            + [pl.BlockSpec(memory_space=pltpu.SMEM)]
            + [pl.BlockSpec(memory_space=pltpu.VMEM)] * (len(small) - 1),
            scratch_shapes=[
                pltpu.VMEM(owner.shape, owner.dtype),
                pltpu.SMEM(small[0].shape, small[0].dtype),
                pltpu.SemaphoreType.DMA((len(given),)),
            ],
            compiler_params=pltpu.CompilerParams(vmem_limit_bytes=8 << 20),
            name="load",
        )(*given)
        blocks = pl.pallas_call(
            functools.partial(gather_kernel, pair),
            out_shape=[pltpu.VMEM((held, rows, EDIM), embeddings.dtype)] * (intra // pair),
            in_specs=[pl.BlockSpec(memory_space=pltpu.VMEM)] * (1 + pair),
            out_specs=[pl.BlockSpec(memory_space=pltpu.VMEM)] * (intra // pair),
            compiler_params=pltpu.CompilerParams(vmem_limit_bytes=8 << 20),
            cost_estimate=pl.CostEstimate(flops=ahead, bytes_accessed=0, transcendentals=0),
            name="gather_rows",
        )(picks, embeddings, *parts)
        return blocks, small
    order = owner.reshape(towers, intra, -1)
    crossed = order[:, jnp.arange(intra) ^ other_core(intra)]
    own = jnp.arange(towers)[:, None, None] == lax.axis_index("tower")
    order = jnp.where(own, order, crossed).transpose(1, 0, 2)
    me = lax.axis_index("intra")
    table = jnp.concatenate([embeddings, *parts], axis=1)
    blocks = []
    for s in steps(intra, pair):
        mine = lax.dynamic_index_in_dim(order, partner(me, s, intra, pair), keepdims=False).reshape(-1)
        blocks.append(jnp.take(table, mine, axis=0).reshape(rows, held, EDIM).transpose(1, 0, 2))
    assign = small[0][0]
    same = assign[None, :] == jnp.arange(assign.size)[:, None]
    slots = jnp.sum(jnp.where(same, jnp.arange(assign.size)[None, :], 0), axis=1)
    return blocks, (slots.astype(assign.dtype)[None, :], *small[1:])


def first_layer(intra, pair, order, slots_ref, w1_ref, x_ref, blocks, before_ref=None):
    held, rows, _ = blocks[0].shape
    held //= pair
    count, depth, hid = w1_ref.shape
    per_tower = depth // EDIM
    me = lax.axis_index("intra")
    slots = []
    for s, block in zip(order, blocks):
        source = partner(me, -s, intra, pair)
        for q in range(pair):
            for f in range(held):
                slot = slots_ref[0, (source ^ q) * held + f]
                n = len(slots)
                slots.append((slot // per_tower, pl.multiple_of((slot % per_tower) * EDIM, EDIM)))
                for k in range(count):
                    own = jnp.where(slots[n][0] == k, 1.0, 0.0).astype(jnp.bfloat16)
                    x_ref[k * rows : (k + 1) * rows, n * EDIM : (n + 1) * EDIM] = block[q * held + f] * own
    wide = 2 * EDIM
    for h in range(0, hid, wide):
        columns = slice(h, min(h + wide, hid))
        total = None if before_ref is None else before_ref[:, columns]
        for n in range(0, len(slots), 2):
            some = slots[n : n + 2]
            weight = [w1_ref[k, pl.ds(start, EDIM), columns] for k, start in some]
            term = jnp.dot(
                x_ref[:, n * EDIM : (n + len(some)) * EDIM],
                jnp.concatenate(weight, axis=0),
                preferred_element_type=jnp.float32,
            )
            total = term if total is None else total + term
        yield columns, total


def early_kernel(intra, pair, order, slots_ref, w1_ref, *rest):
    blocks, before, (out_ref, x_ref) = rest[: len(order)], rest[len(order) : -2], rest[-2:]
    for columns, total in first_layer(intra, pair, order, slots_ref, w1_ref, x_ref, blocks, *before):
        out_ref[:, columns] = total


def tower_kernel(towers, intra, pair, order, slots_ref, w1_ref, b1_ref, w2_ref, b2_ref, sums_ref, *rest):
    blocks, outs, (x_ref, hidden_ref, y_ref) = rest[: len(order)], rest[len(order) : -3], rest[-3:]
    count, rows, _ = y_ref.shape
    vectors = w2_ref.shape[2] // EDIM
    per = rows // towers
    for columns, total in first_layer(intra, pair, order, slots_ref, w1_ref, x_ref, blocks, sums_ref):
        for k in range(count):
            hidden = total[k * rows : (k + 1) * rows] + b1_ref[k : k + 1, columns]
            hidden_ref[k, :, columns] = jnp.maximum(hidden, 0.0).astype(jnp.bfloat16)
    for k in range(count):
        result = jnp.dot(hidden_ref[k], w2_ref[k], preferred_element_type=jnp.float32)
        y_ref[k] = jnp.maximum(result + b2_ref[k : k + 1, :], 0.0)
    place = lax.axis_index("tower")
    for o, out in zip(offsets(towers), outs):
        start = pl.multiple_of((place ^ o) * per, per)
        pieces = [
            y_ref[k, pl.ds(start, per), v * EDIM : (v + 1) * EDIM]
            for k in range(count)
            for v in range(vectors)
        ]
        out[...] = jnp.concatenate(pieces, axis=0).astype(out.dtype)


def run_towers(slots, w1, b1, w2, b2, blocks, towers, intra, pair):
    order = steps(intra, pair)
    remote = len(blocks) - 1
    cuts = (0, max(remote // 2, min(remote - 1, 1)), remote - 1)
    stages = [[-1, *range(*cuts[:2])], [*range(*cuts[1:])]]
    late = [remote - 1] if remote else []
    held, rows, _ = blocks[0].shape
    count, depth, hid = w1.shape
    width = w2.shape[2]
    local = count * (width // EDIM) * (rows // towers)
    w1 = pltpu.with_memory_space_constraint(w1, pltpu.VMEM)
    w2 = pltpu.with_memory_space_constraint(w2, pltpu.VMEM)
    params = pltpu.CompilerParams(vmem_limit_bytes=16 << 20)
    sums = ()
    for stage in stages:
        if not stage:
            continue
        sums = pl.pallas_call(
            functools.partial(early_kernel, intra, pair, [order[n] for n in stage]),
            out_shape=[pltpu.VMEM((count * rows, hid), jnp.float32)],
            in_specs=[pl.BlockSpec(memory_space=pltpu.SMEM)]
            + [pl.BlockSpec(memory_space=pltpu.VMEM)] * (1 + len(stage) + len(sums)),
            out_specs=[pl.BlockSpec(memory_space=pltpu.VMEM)],
            scratch_shapes=[pltpu.VMEM((count * rows, len(stage) * held * EDIM), jnp.bfloat16)],
            compiler_params=params,
            cost_estimate=pl.CostEstimate(
                flops=2 * count * rows * depth * hid, bytes_accessed=0, transcendentals=0
            ),
            name="towers_early",
        )(slots, w1, *(blocks[n] for n in stage), *sums)
    return pl.pallas_call(
        functools.partial(tower_kernel, towers, intra, pair, [order[n] for n in late]),
        out_shape=[pltpu.VMEM((local, EDIM), jnp.bfloat16)] * towers,
        in_specs=[pl.BlockSpec(memory_space=pltpu.SMEM)]
        + [pl.BlockSpec(memory_space=pltpu.VMEM)] * (5 + len(late)),
        out_specs=[pl.BlockSpec(memory_space=pltpu.VMEM)] * towers,
        scratch_shapes=[
            pltpu.VMEM((count * rows, max(len(late), 1) * held * EDIM), jnp.bfloat16),
            pltpu.VMEM((count, rows, hid), jnp.bfloat16),
            pltpu.VMEM((count, rows, width), jnp.float32),
        ],
        compiler_params=params,
        name="towers",
    )(slots, w1, b1, w2, b2, *sums, *(blocks[n] for n in late))


def interact_kernel(towers, proj_ref, *rest):
    blocks, out, all_ref = rest[:towers], rest[towers], rest[towers + 1]
    per, count, _ = out.shape
    local = blocks[0].shape[0]
    place = lax.axis_index("tower")
    for o, block in zip(offsets(towers), blocks):
        start = pl.multiple_of((place ^ o) * local, local)
        all_ref[pl.ds(start, local), :] = block[...].astype(jnp.float32)
    group = max(1, min(per, 128 // count))
    proj = jnp.concatenate([proj_ref[...]] * (2 * group), axis=0)
    for first in range(0, per, group):
        samples = range(first, first + group)
        vectors = [all_ref[pl.ds(d, count, stride=per), :] for d in samples]
        vectors = jnp.concatenate(vectors, axis=0).astype(jnp.bfloat16)
        gram = lax.dot_general(
            vectors, vectors, (((1,), (1,)), ((), ())), preferred_element_type=jnp.float32
        )
        gram = gram * (1.0 / EDIM)
        column = lax.broadcasted_iota(jnp.int32, (count, gram.shape[1]), 1)
        own = [
            jnp.where(
                (column >= g * count) & (column < (g + 1) * count),
                gram[g * count : (g + 1) * count, :],
                0.0,
            )
            for g in range(group)
        ]
        gram = jnp.concatenate(own, axis=0)
        high = gram.astype(jnp.bfloat16)
        low = (gram - high.astype(jnp.float32)).astype(jnp.bfloat16)
        result = jnp.dot(
            jnp.concatenate([high, low], axis=1), proj, preferred_element_type=jnp.float32
        )
        for g, d in enumerate(samples):
            out[d] = result[g * count : (g + 1) * count, :].astype(out.dtype)


def interact(proj, blocks):
    towers = len(blocks)
    local = blocks[0].shape[0]
    count = proj.shape[0]
    per = towers * local // count
    return pl.pallas_call(
        functools.partial(interact_kernel, towers),
        out_shape=jax.ShapeDtypeStruct((per, count, EDIM), jnp.bfloat16),
        in_specs=[pl.BlockSpec(memory_space=pltpu.VMEM)] * (1 + towers),
        out_specs=pl.BlockSpec(memory_space=pltpu.VMEM),
        scratch_shapes=[pltpu.VMEM((towers * local, EDIM), jnp.float32)],
        compiler_params=pltpu.CompilerParams(vmem_limit_bytes=8 << 20),
        name="interact",
    )(proj, *blocks)


def shards(
    embeddings,
    feature_assign,
    sample_owner,
    first_weight,
    first_bias,
    tower_weight,
    tower_bias,
    proj_weight,
):
    towers, intra = lax.axis_size("tower"), lax.axis_size("intra")
    small = (feature_assign, first_bias, tower_bias, proj_weight)
    ahead = 10_000 * (first_weight.size + tower_weight.size)
    pair = 2 if intra % 2 == 0 else 1
    blocks, small = gather_blocks(sample_owner, embeddings, small, towers, intra, pair, ahead)
    slots, first_bias, tower_bias, proj_weight = small
    blocks = exchange_chips(blocks, intra, pair)
    vectors = run_towers(
        slots, first_weight, first_bias, tower_weight, tower_bias, blocks, towers, intra, pair
    )
    vectors = exchange_groups(vectors, towers, intra)
    return interact(proj_weight, vectors)


def solution(mesh):
    return jax.shard_map(
        shards,
        mesh=mesh,
        in_specs=(
            P(None, ("tower", "intra")),
            P("tower", None),
            P(),
            P("tower", None, None),
            P("tower", None),
            P("tower", None, None),
            P("tower", None),
            P(),
        ),
        out_specs=P(("tower", "intra"), None, None),
        check_vma=False,
    )
```

```python
import functools

import jax
import jax.numpy as jnp
from jax import lax
from jax.experimental import pallas as pl
from jax.experimental.pallas import tpu as pltpu
from jax.sharding import PartitionSpec as P

EDIM = 128
FEW_SAMPLES = 1024


def offsets(size):
    return range(size - 1, -1, -1)


def steps(intra, pair):
    return (*range(1, intra // pair), 0)


def ring_place(chip, chips):
    place = chip
    bits = (chips - 1).bit_length() if chips & (chips - 1) == 0 else 0
    for n in range(1, bits):
        place = place ^ (chip >> n)
    return place


def ring_chip(place, chips):
    return place ^ (place >> 1) if chips & (chips - 1) == 0 else place


def partner(me, step, intra, pair):
    chips = intra // pair
    place = (ring_place(me // pair, chips) + step + chips) % chips
    return ring_chip(place, chips) * pair + me % pair


def exchange_chips(blocks, intra, pair):
    return [
        lax.ppermute(block, "intra", [(i, partner(i, s, intra, pair)) for i in range(intra)]) if s else block
        for block, s in zip(blocks, steps(intra, pair))
    ]


def other_core(intra):
    return 1 if intra > 1 else 0


def exchange_groups(blocks, towers, intra):
    received = []
    for block, o in zip(blocks, offsets(towers)):
        pairs = [
            (t * intra + i, (t ^ o) * intra + (i ^ other_core(intra)))
            for t in range(towers)
            for i in range(intra)
        ]
        received.append(lax.ppermute(block, ("tower", "intra"), pairs) if o else block)
    return received


def load_kernel(towers, intra, pair, count, owner_hbm, emb_hbm, *rest):
    small, (picks_ref, emb_ref, slots_ref), copies = rest[:count], rest[count : count + 3], rest[count + 3 : -3]
    owner_ref, assign_ref, sems = rest[-3:]
    targets = (assign_ref, *copies)
    pairs = [(owner_hbm, owner_ref), (emb_hbm, emb_ref), *zip(small, targets)]
    loads = [pltpu.make_async_copy(a, b, sems.at[i]) for i, (a, b) in enumerate(pairs)]
    for load in loads:
        load.start()
    samples = emb_ref.shape[0]
    per = samples // (towers * intra)
    me, place = lax.axis_index("intra"), lax.axis_index("tower")
    lane = lax.broadcasted_iota(jnp.int32, (per, samples), 1) - lax.broadcasted_iota(jnp.int32, (per, samples), 0)
    chosen = []
    for s in steps(intra, pair):
        block = partner(me, s, intra, pair)
        for t in range(towers):
            owner = jnp.where(place == t, block, block ^ other_core(intra))
            chosen.append(jnp.where(lane == (t * intra + owner) * per, 1.0, 0.0))
    chosen = jnp.concatenate(chosen, axis=0).astype(jnp.bfloat16)
    loads[0].wait()
    owner = jnp.broadcast_to(owner_ref[...].reshape(1, samples), (samples, samples))
    picks = lax.broadcasted_iota(jnp.int32, (samples, samples), 0) == owner
    picks = jnp.where(picks, 1.0, 0.0).astype(jnp.bfloat16)
    picks_ref[...] = lax.dot_general(
        chosen, picks, (((1,), (1,)), ((), ())), preferred_element_type=jnp.float32
    ).astype(jnp.bfloat16)
    loads[2].wait()
    for slot in range(assign_ref.shape[1]):
        slots_ref[0, assign_ref[0, slot]] = slot
    for load in (loads[1], *loads[3:]):
        load.wait()


def gather_kernel(pair, picks_ref, *rest):
    parts, outs = rest[:pair], rest[pair:]
    held = parts[0].shape[1] // EDIM
    rows = outs[0].shape[1]
    for q, part in enumerate(parts):
        ordered = jnp.dot(picks_ref[...], part[...], preferred_element_type=jnp.float32)
        for n, out in enumerate(outs):
            for f in range(held):
                block = ordered[n * rows : (n + 1) * rows, f * EDIM : (f + 1) * EDIM]
                out[q * held + f] = block.astype(out.dtype)


def gather_blocks(owner, embeddings, small, towers, intra, pair, ahead):
    samples, width = embeddings.shape
    rows, held = samples // intra, pair * width // EDIM
    parts = [lax.ppermute(embeddings, "intra", [(i, i ^ q) for i in range(intra)]) for q in range(1, pair)]
    if samples <= FEW_SAMPLES:
        given = [pltpu.with_memory_space_constraint(a, pltpu.HBM) for a in (owner, embeddings, *small)]
        picks, embeddings, *small = pl.pallas_call(
            functools.partial(load_kernel, towers, intra, pair, len(small)),
            out_shape=[
                pltpu.VMEM((samples // pair, samples), jnp.bfloat16),
                pltpu.VMEM(embeddings.shape, embeddings.dtype),
                pltpu.SMEM(small[0].shape, small[0].dtype),
            ]
            + [pltpu.VMEM(a.shape, a.dtype) for a in small[1:]],
            in_specs=[pl.BlockSpec(memory_space=pltpu.HBM)] * len(given),
            out_specs=[pl.BlockSpec(memory_space=pltpu.VMEM)] * 2
            + [pl.BlockSpec(memory_space=pltpu.SMEM)]
            + [pl.BlockSpec(memory_space=pltpu.VMEM)] * (len(small) - 1),
            scratch_shapes=[
                pltpu.VMEM(owner.shape, owner.dtype),
                pltpu.SMEM(small[0].shape, small[0].dtype),
                pltpu.SemaphoreType.DMA((len(given),)),
            ],
            compiler_params=pltpu.CompilerParams(vmem_limit_bytes=8 << 20),
            name="load",
        )(*given)
        blocks = pl.pallas_call(
            functools.partial(gather_kernel, pair),
            out_shape=[pltpu.VMEM((held, rows, EDIM), embeddings.dtype)] * (intra // pair),
            in_specs=[pl.BlockSpec(memory_space=pltpu.VMEM)] * (1 + pair),
            out_specs=[pl.BlockSpec(memory_space=pltpu.VMEM)] * (intra // pair),
            compiler_params=pltpu.CompilerParams(vmem_limit_bytes=8 << 20),
            cost_estimate=pl.CostEstimate(flops=ahead, bytes_accessed=0, transcendentals=0),
            name="gather_rows",
        )(picks, embeddings, *parts)
        return blocks, small
    order = owner.reshape(towers, intra, -1)
    crossed = order[:, jnp.arange(intra) ^ other_core(intra)]
    own = jnp.arange(towers)[:, None, None] == lax.axis_index("tower")
    order = jnp.where(own, order, crossed).transpose(1, 0, 2)
    me = lax.axis_index("intra")
    table = jnp.concatenate([embeddings, *parts], axis=1)
    blocks = []
    for s in steps(intra, pair):
        mine = lax.dynamic_index_in_dim(order, partner(me, s, intra, pair), keepdims=False).reshape(-1)
        blocks.append(jnp.take(table, mine, axis=0).reshape(rows, held, EDIM).transpose(1, 0, 2))
    assign = small[0][0]
    same = assign[None, :] == jnp.arange(assign.size)[:, None]
    slots = jnp.sum(jnp.where(same, jnp.arange(assign.size)[None, :], 0), axis=1)
    return blocks, (slots.astype(assign.dtype)[None, :], *small[1:])


def first_layer(intra, pair, order, slots_ref, w1_ref, x_ref, blocks, before_ref=None):
    held, rows, _ = blocks[0].shape
    held //= pair
    count, depth, hid = w1_ref.shape
    per_tower = depth // EDIM
    me = lax.axis_index("intra")
    slots = []
    for s, block in zip(order, blocks):
        source = partner(me, -s, intra, pair)
        for q in range(pair):
            for f in range(held):
                slot = slots_ref[0, (source ^ q) * held + f]
                n = len(slots)
                slots.append((slot // per_tower, pl.multiple_of((slot % per_tower) * EDIM, EDIM)))
                for k in range(count):
                    own = jnp.where(slots[n][0] == k, 1.0, 0.0).astype(jnp.bfloat16)
                    x_ref[k * rows : (k + 1) * rows, n * EDIM : (n + 1) * EDIM] = block[q * held + f] * own
    wide = 2 * EDIM
    for h in range(0, hid, wide):
        columns = slice(h, min(h + wide, hid))
        total = None if before_ref is None else before_ref[:, columns]
        for n in range(0, len(slots), 2):
            some = slots[n : n + 2]
            weight = [w1_ref[k, pl.ds(start, EDIM), columns] for k, start in some]
            term = jnp.dot(
                x_ref[:, n * EDIM : (n + len(some)) * EDIM],
                jnp.concatenate(weight, axis=0),
                preferred_element_type=jnp.float32,
            )
            total = term if total is None else total + term
        yield columns, total


def early_kernel(intra, pair, order, slots_ref, w1_ref, *rest):
    blocks, before, (out_ref, x_ref) = rest[: len(order)], rest[len(order) : -2], rest[-2:]
    for columns, total in first_layer(intra, pair, order, slots_ref, w1_ref, x_ref, blocks, *before):
        out_ref[:, columns] = total


def tower_kernel(towers, intra, pair, order, slots_ref, w1_ref, b1_ref, w2_ref, b2_ref, sums_ref, *rest):
    blocks, outs, (x_ref, hidden_ref, y_ref) = rest[: len(order)], rest[len(order) : -3], rest[-3:]
    count, rows, _ = y_ref.shape
    vectors = w2_ref.shape[2] // EDIM
    per = rows // towers
    for columns, total in first_layer(intra, pair, order, slots_ref, w1_ref, x_ref, blocks, sums_ref):
        for k in range(count):
            hidden = total[k * rows : (k + 1) * rows] + b1_ref[k : k + 1, columns]
            hidden_ref[k, :, columns] = jnp.maximum(hidden, 0.0).astype(jnp.bfloat16)
    for k in range(count):
        result = jnp.dot(hidden_ref[k], w2_ref[k], preferred_element_type=jnp.float32)
        y_ref[k] = jnp.maximum(result + b2_ref[k : k + 1, :], 0.0)
    place = lax.axis_index("tower")
    for o, out in zip(offsets(towers), outs):
        start = pl.multiple_of((place ^ o) * per, per)
        pieces = [
            y_ref[k, pl.ds(start, per), v * EDIM : (v + 1) * EDIM]
            for k in range(count)
            for v in range(vectors)
        ]
        out[...] = jnp.concatenate(pieces, axis=0).astype(out.dtype)


def run_towers(slots, w1, b1, w2, b2, blocks, towers, intra, pair):
    order = steps(intra, pair)
    remote = len(blocks) - 1
    cuts = (0, max(remote // 2, min(remote - 1, 1)), remote - 1)
    stages = [[-1, *range(*cuts[:2])], [*range(*cuts[1:])]]
    late = [remote - 1] if remote else []
    held, rows, _ = blocks[0].shape
    count, depth, hid = w1.shape
    width = w2.shape[2]
    local = count * (width // EDIM) * (rows // towers)
    w1 = pltpu.with_memory_space_constraint(w1, pltpu.VMEM)
    w2 = pltpu.with_memory_space_constraint(w2, pltpu.VMEM)
    params = pltpu.CompilerParams(vmem_limit_bytes=16 << 20)
    sums = ()
    for stage in stages:
        if not stage:
            continue
        sums = pl.pallas_call(
            functools.partial(early_kernel, intra, pair, [order[n] for n in stage]),
            out_shape=[pltpu.VMEM((count * rows, hid), jnp.float32)],
            in_specs=[pl.BlockSpec(memory_space=pltpu.SMEM)]
            + [pl.BlockSpec(memory_space=pltpu.VMEM)] * (1 + len(stage) + len(sums)),
            out_specs=[pl.BlockSpec(memory_space=pltpu.VMEM)],
            scratch_shapes=[pltpu.VMEM((count * rows, len(stage) * held * EDIM), jnp.bfloat16)],
            compiler_params=params,
            cost_estimate=pl.CostEstimate(
                flops=2 * count * rows * depth * hid, bytes_accessed=0, transcendentals=0
            ),
            name="towers_early",
        )(slots, w1, *(blocks[n] for n in stage), *sums)
    return pl.pallas_call(
        functools.partial(tower_kernel, towers, intra, pair, [order[n] for n in late]),
        out_shape=[pltpu.VMEM((local, EDIM), jnp.bfloat16)] * towers,
        in_specs=[pl.BlockSpec(memory_space=pltpu.SMEM)]
        + [pl.BlockSpec(memory_space=pltpu.VMEM)] * (5 + len(late)),
        out_specs=[pl.BlockSpec(memory_space=pltpu.VMEM)] * towers,
        scratch_shapes=[
            pltpu.VMEM((count * rows, max(len(late), 1) * held * EDIM), jnp.bfloat16),
            pltpu.VMEM((count, rows, hid), jnp.bfloat16),
            pltpu.VMEM((count, rows, width), jnp.float32),
        ],
        compiler_params=params,
        name="towers",
    )(slots, w1, b1, w2, b2, *sums, *(blocks[n] for n in late))


def interact_kernel(towers, proj_ref, *rest):
    blocks, out, all_ref = rest[:towers], rest[towers], rest[towers + 1]
    per, count, _ = out.shape
    local = blocks[0].shape[0]
    place = lax.axis_index("tower")
    for o, block in zip(offsets(towers), blocks):
        start = pl.multiple_of((place ^ o) * local, local)
        all_ref[pl.ds(start, local), :] = block[...].astype(jnp.float32)
    group = max(1, min(per, 128 // count))
    proj = jnp.concatenate([proj_ref[...]] * (2 * group), axis=0)
    for first in range(0, per, group):
        samples = range(first, first + group)
        vectors = [all_ref[pl.ds(d, count, stride=per), :] for d in samples]
        vectors = jnp.concatenate(vectors, axis=0).astype(jnp.bfloat16)
        gram = lax.dot_general(
            vectors, vectors, (((1,), (1,)), ((), ())), preferred_element_type=jnp.float32
        )
        gram = gram * (1.0 / EDIM)
        column = lax.broadcasted_iota(jnp.int32, (count, gram.shape[1]), 1)
        own = [
            jnp.where(
                (column >= g * count) & (column < (g + 1) * count),
                gram[g * count : (g + 1) * count, :],
                0.0,
            )
            for g in range(group)
        ]
        gram = jnp.concatenate(own, axis=0)
        high = gram.astype(jnp.bfloat16)
        low = (gram - high.astype(jnp.float32)).astype(jnp.bfloat16)
        result = jnp.dot(
            jnp.concatenate([high, low], axis=1), proj, preferred_element_type=jnp.float32
        )
        for g, d in enumerate(samples):
            out[d] = result[g * count : (g + 1) * count, :].astype(out.dtype)


def interact(proj, blocks):
    towers = len(blocks)
    local = blocks[0].shape[0]
    count = proj.shape[0]
    per = towers * local // count
    return pl.pallas_call(
        functools.partial(interact_kernel, towers),
        out_shape=jax.ShapeDtypeStruct((per, count, EDIM), jnp.bfloat16),
        in_specs=[pl.BlockSpec(memory_space=pltpu.VMEM)] * (1 + towers),
        out_specs=pl.BlockSpec(memory_space=pltpu.VMEM),
        scratch_shapes=[pltpu.VMEM((towers * local, EDIM), jnp.float32)],
        compiler_params=pltpu.CompilerParams(vmem_limit_bytes=8 << 20),
        name="interact",
    )(proj, *blocks)


def shards(
    embeddings,
    feature_assign,
    sample_owner,
    first_weight,
    first_bias,
    tower_weight,
    tower_bias,
    proj_weight,
):
    towers, intra = lax.axis_size("tower"), lax.axis_size("intra")
    small = (feature_assign, first_bias, tower_bias, proj_weight)
    ahead = 10_000 * (first_weight.size + tower_weight.size)
    pair = 2 if intra % 2 == 0 else 1
    blocks, small = gather_blocks(sample_owner, embeddings, small, towers, intra, pair, ahead)
    slots, first_bias, tower_bias, proj_weight = small
    blocks = exchange_chips(blocks, intra, pair)
    vectors = run_towers(
        slots, first_weight, first_bias, tower_weight, tower_bias, blocks, towers, intra, pair
    )
    vectors = exchange_groups(vectors, towers, intra)
    return interact(proj_weight, vectors)


def solution(mesh):
    return jax.shard_map(
        shards,
        mesh=mesh,
        in_specs=(
            P(None, ("tower", "intra")),
            P("tower", None),
            P(),
            P("tower", None, None),
            P("tower", None),
            P("tower", None, None),
            P("tower", None),
            P(),
        ),
        out_specs=P(("tower", "intra"), None, None),
        check_vma=False,
    )
```

```python
import functools

import jax
import jax.numpy as jnp
from jax import lax
from jax.experimental import pallas as pl
from jax.experimental.pallas import tpu as pltpu
from jax.sharding import PartitionSpec as P

EDIM = 128
FEW_SAMPLES = 1024


def offsets(size):
    return sorted(range(size), key=lambda o: (-o.bit_count(), o))


def steps(intra, pair):
    return (*range(1, intra // pair), 0)


def ring_place(chip, chips):
    place = chip
    bits = (chips - 1).bit_length() if chips & (chips - 1) == 0 else 0
    for n in range(1, bits):
        place = place ^ (chip >> n)
    return place


def ring_chip(place, chips):
    return place ^ (place >> 1) if chips & (chips - 1) == 0 else place


def partner(me, step, intra, pair):
    chips = intra // pair
    place = (ring_place(me // pair, chips) + step + chips) % chips
    return ring_chip(place, chips) * pair + (me % pair + (pair - 1 if step else 0)) % pair


def exchange_chips(blocks, intra, pair):
    return [
        lax.ppermute(block, "intra", [(i, partner(i, s, intra, pair)) for i in range(intra)]) if s else block
        for block, s in zip(blocks, steps(intra, pair))
    ]


def other_core(intra):
    return 1 if intra > 1 else 0


def exchange_groups(blocks, towers, intra):
    received = []
    for block, o in zip(blocks, offsets(towers)):
        pairs = [
            (t * intra + i, (t ^ o) * intra + (i ^ other_core(intra)))
            for t in range(towers)
            for i in range(intra)
        ]
        received.append(lax.ppermute(block, ("tower", "intra"), pairs) if o else block)
    return received


def load_kernel(towers, intra, pair, count, owner_hbm, emb_hbm, *rest):
    small, (picks_ref, emb_ref, slots_ref), copies = rest[:count], rest[count : count + 3], rest[count + 3 : -3]
    owner_ref, assign_ref, sems = rest[-3:]
    targets = (assign_ref, *copies)
    pairs = [(owner_hbm, owner_ref), (emb_hbm, emb_ref), *zip(small, targets)]
    loads = [pltpu.make_async_copy(a, b, sems.at[i]) for i, (a, b) in enumerate(pairs)]
    for load in loads:
        load.start()
    samples = emb_ref.shape[0]
    per = samples // (towers * intra)
    me, place = lax.axis_index("intra"), lax.axis_index("tower")
    lane = lax.broadcasted_iota(jnp.int32, (per, samples), 1) - lax.broadcasted_iota(jnp.int32, (per, samples), 0)
    chosen = []
    for s in steps(intra, pair):
        block = partner(me, s, intra, pair)
        for t in range(towers):
            owner = jnp.where(place == t, block, block ^ other_core(intra))
            chosen.append(jnp.where(lane == (t * intra + owner) * per, 1.0, 0.0))
    chosen = jnp.concatenate(chosen, axis=0).astype(jnp.bfloat16)
    loads[0].wait()
    owner = jnp.broadcast_to(owner_ref[...].reshape(1, samples), (samples, samples))
    picks = lax.broadcasted_iota(jnp.int32, (samples, samples), 0) == owner
    picks = jnp.where(picks, 1.0, 0.0).astype(jnp.bfloat16)
    picks_ref[...] = lax.dot_general(
        chosen, picks, (((1,), (1,)), ((), ())), preferred_element_type=jnp.float32
    ).astype(jnp.bfloat16)
    loads[2].wait()
    for slot in range(assign_ref.shape[1]):
        slots_ref[0, assign_ref[0, slot]] = slot
    for load in (loads[1], *loads[3:]):
        load.wait()


def gather_kernel(pair, picks_ref, *rest):
    parts, outs = rest[:pair], rest[pair:]
    held = parts[0].shape[1] // EDIM
    rows = outs[0].shape[1]
    for q, part in enumerate(parts):
        ordered = jnp.dot(picks_ref[...], part[...], preferred_element_type=jnp.float32)
        for n, out in enumerate(outs):
            for f in range(held):
                block = ordered[n * rows : (n + 1) * rows, f * EDIM : (f + 1) * EDIM]
                out[q * held + f] = block.astype(out.dtype)


def gather_blocks(owner, embeddings, small, towers, intra, pair, ahead):
    samples, width = embeddings.shape
    rows, held = samples // intra, pair * width // EDIM
    parts = [lax.ppermute(embeddings, "intra", [(i, i ^ q) for i in range(intra)]) for q in range(1, pair)]
    if samples <= FEW_SAMPLES:
        given = [pltpu.with_memory_space_constraint(a, pltpu.HBM) for a in (owner, embeddings, *small)]
        picks, embeddings, *small = pl.pallas_call(
            functools.partial(load_kernel, towers, intra, pair, len(small)),
            out_shape=[
                pltpu.VMEM((samples // pair, samples), jnp.bfloat16),
                pltpu.VMEM(embeddings.shape, embeddings.dtype),
                pltpu.SMEM(small[0].shape, small[0].dtype),
            ]
            + [pltpu.VMEM(a.shape, a.dtype) for a in small[1:]],
            in_specs=[pl.BlockSpec(memory_space=pltpu.HBM)] * len(given),
            out_specs=[pl.BlockSpec(memory_space=pltpu.VMEM)] * 2
            + [pl.BlockSpec(memory_space=pltpu.SMEM)]
            + [pl.BlockSpec(memory_space=pltpu.VMEM)] * (len(small) - 1),
            scratch_shapes=[
                pltpu.VMEM(owner.shape, owner.dtype),
                pltpu.SMEM(small[0].shape, small[0].dtype),
                pltpu.SemaphoreType.DMA((len(given),)),
            ],
            compiler_params=pltpu.CompilerParams(vmem_limit_bytes=8 << 20),
            name="load",
        )(*given)
        blocks = pl.pallas_call(
            functools.partial(gather_kernel, pair),
            out_shape=[pltpu.VMEM((held, rows, EDIM), embeddings.dtype)] * (intra // pair),
            in_specs=[pl.BlockSpec(memory_space=pltpu.VMEM)] * (1 + pair),
            out_specs=[pl.BlockSpec(memory_space=pltpu.VMEM)] * (intra // pair),
            compiler_params=pltpu.CompilerParams(vmem_limit_bytes=8 << 20),
            cost_estimate=pl.CostEstimate(flops=ahead, bytes_accessed=0, transcendentals=0),
            name="gather_rows",
        )(picks, embeddings, *parts)
        return blocks, small
    order = owner.reshape(towers, intra, -1)
    crossed = order[:, jnp.arange(intra) ^ other_core(intra)]
    own = jnp.arange(towers)[:, None, None] == lax.axis_index("tower")
    order = jnp.where(own, order, crossed).transpose(1, 0, 2)
    me = lax.axis_index("intra")
    table = jnp.concatenate([embeddings, *parts], axis=1)
    blocks = []
    for s in steps(intra, pair):
        mine = lax.dynamic_index_in_dim(order, partner(me, s, intra, pair), keepdims=False).reshape(-1)
        blocks.append(jnp.take(table, mine, axis=0).reshape(rows, held, EDIM).transpose(1, 0, 2))
    assign = small[0][0]
    same = assign[None, :] == jnp.arange(assign.size)[:, None]
    slots = jnp.sum(jnp.where(same, jnp.arange(assign.size)[None, :], 0), axis=1)
    return blocks, (slots.astype(assign.dtype)[None, :], *small[1:])


def first_layer(intra, pair, order, slots_ref, w1_ref, x_ref, blocks, before_ref=None):
    held, rows, _ = blocks[0].shape
    held //= pair
    count, depth, hid = w1_ref.shape
    per_tower = depth // EDIM
    me = lax.axis_index("intra")
    slots = []
    for s, block in zip(order, blocks):
        source = partner(me, -s, intra, pair)
        for q in range(pair):
            for f in range(held):
                slot = slots_ref[0, (source ^ q) * held + f]
                n = len(slots)
                slots.append((slot // per_tower, pl.multiple_of((slot % per_tower) * EDIM, EDIM)))
                for k in range(count):
                    own = jnp.where(slots[n][0] == k, 1.0, 0.0).astype(jnp.bfloat16)
                    x_ref[k * rows : (k + 1) * rows, n * EDIM : (n + 1) * EDIM] = block[q * held + f] * own
    wide = 2 * EDIM
    for h in range(0, hid, wide):
        columns = slice(h, min(h + wide, hid))
        total = None if before_ref is None else before_ref[:, columns]
        for n in range(0, len(slots), 2):
            some = slots[n : n + 2]
            weight = [w1_ref[k, pl.ds(start, EDIM), columns] for k, start in some]
            term = jnp.dot(
                x_ref[:, n * EDIM : (n + len(some)) * EDIM],
                jnp.concatenate(weight, axis=0),
                preferred_element_type=jnp.float32,
            )
            total = term if total is None else total + term
        yield columns, total


def early_kernel(intra, pair, order, slots_ref, w1_ref, *rest):
    blocks, before, (out_ref, x_ref) = rest[: len(order)], rest[len(order) : -2], rest[-2:]
    for columns, total in first_layer(intra, pair, order, slots_ref, w1_ref, x_ref, blocks, *before):
        out_ref[:, columns] = total


def tower_kernel(towers, intra, pair, order, slots_ref, w1_ref, b1_ref, w2_ref, b2_ref, sums_ref, *rest):
    blocks, outs, (x_ref, hidden_ref, y_ref) = rest[: len(order)], rest[len(order) : -3], rest[-3:]
    count, rows, _ = y_ref.shape
    vectors = w2_ref.shape[2] // EDIM
    per = rows // towers
    for columns, total in first_layer(intra, pair, order, slots_ref, w1_ref, x_ref, blocks, sums_ref):
        for k in range(count):
            hidden = total[k * rows : (k + 1) * rows] + b1_ref[k : k + 1, columns]
            hidden_ref[k, :, columns] = jnp.maximum(hidden, 0.0).astype(jnp.bfloat16)
    for k in range(count):
        result = jnp.dot(hidden_ref[k], w2_ref[k], preferred_element_type=jnp.float32)
        y_ref[k] = jnp.maximum(result + b2_ref[k : k + 1, :], 0.0)
    place = lax.axis_index("tower")
    for o, out in zip(offsets(towers), outs):
        start = pl.multiple_of((place ^ o) * per, per)
        pieces = [
            y_ref[k, pl.ds(start, per), v * EDIM : (v + 1) * EDIM]
            for k in range(count)
            for v in range(vectors)
        ]
        out[...] = jnp.concatenate(pieces, axis=0).astype(out.dtype)


def run_towers(slots, w1, b1, w2, b2, blocks, towers, intra, pair):
    order = steps(intra, pair)
    remote = len(blocks) - 1
    cuts = (0, max(remote // 2, min(remote - 1, 1)), remote - 1)
    stages = [[-1, *range(*cuts[:2])], [*range(*cuts[1:])]]
    late = [remote - 1] if remote else []
    held, rows, _ = blocks[0].shape
    count, depth, hid = w1.shape
    width = w2.shape[2]
    local = count * (width // EDIM) * (rows // towers)
    w1 = pltpu.with_memory_space_constraint(w1, pltpu.VMEM)
    w2 = pltpu.with_memory_space_constraint(w2, pltpu.VMEM)
    params = pltpu.CompilerParams(vmem_limit_bytes=16 << 20)
    sums = ()
    for stage in stages:
        if not stage:
            continue
        sums = pl.pallas_call(
            functools.partial(early_kernel, intra, pair, [order[n] for n in stage]),
            out_shape=[pltpu.VMEM((count * rows, hid), jnp.float32)],
            in_specs=[pl.BlockSpec(memory_space=pltpu.SMEM)]
            + [pl.BlockSpec(memory_space=pltpu.VMEM)] * (1 + len(stage) + len(sums)),
            out_specs=[pl.BlockSpec(memory_space=pltpu.VMEM)],
            scratch_shapes=[pltpu.VMEM((count * rows, len(stage) * held * EDIM), jnp.bfloat16)],
            compiler_params=params,
            cost_estimate=pl.CostEstimate(
                flops=2 * count * rows * depth * hid, bytes_accessed=0, transcendentals=0
            ),
            name="towers_early",
        )(slots, w1, *(blocks[n] for n in stage), *sums)
    return pl.pallas_call(
        functools.partial(tower_kernel, towers, intra, pair, [order[n] for n in late]),
        out_shape=[pltpu.VMEM((local, EDIM), jnp.bfloat16)] * towers,
        in_specs=[pl.BlockSpec(memory_space=pltpu.SMEM)]
        + [pl.BlockSpec(memory_space=pltpu.VMEM)] * (5 + len(late)),
        out_specs=[pl.BlockSpec(memory_space=pltpu.VMEM)] * towers,
        scratch_shapes=[
            pltpu.VMEM((count * rows, max(len(late), 1) * held * EDIM), jnp.bfloat16),
            pltpu.VMEM((count, rows, hid), jnp.bfloat16),
            pltpu.VMEM((count, rows, width), jnp.float32),
        ],
        compiler_params=params,
        name="towers",
    )(slots, w1, b1, w2, b2, *sums, *(blocks[n] for n in late))


def interact_kernel(towers, proj_ref, *rest):
    blocks, out, all_ref = rest[:towers], rest[towers], rest[towers + 1]
    per, count, _ = out.shape
    local = blocks[0].shape[0]
    place = lax.axis_index("tower")
    for o, block in zip(offsets(towers), blocks):
        start = pl.multiple_of((place ^ o) * local, local)
        all_ref[pl.ds(start, local), :] = block[...].astype(jnp.float32)
    group = max(1, min(per, 128 // count))
    proj = jnp.concatenate([proj_ref[...]] * (2 * group), axis=0)
    for first in range(0, per, group):
        samples = range(first, first + group)
        vectors = [all_ref[pl.ds(d, count, stride=per), :] for d in samples]
        vectors = jnp.concatenate(vectors, axis=0).astype(jnp.bfloat16)
        gram = lax.dot_general(
            vectors, vectors, (((1,), (1,)), ((), ())), preferred_element_type=jnp.float32
        )
        gram = gram * (1.0 / EDIM)
        column = lax.broadcasted_iota(jnp.int32, (count, gram.shape[1]), 1)
        own = [
            jnp.where(
                (column >= g * count) & (column < (g + 1) * count),
                gram[g * count : (g + 1) * count, :],
                0.0,
            )
            for g in range(group)
        ]
        gram = jnp.concatenate(own, axis=0)
        high = gram.astype(jnp.bfloat16)
        low = (gram - high.astype(jnp.float32)).astype(jnp.bfloat16)
        result = jnp.dot(
            jnp.concatenate([high, low], axis=1), proj, preferred_element_type=jnp.float32
        )
        for g, d in enumerate(samples):
            out[d] = result[g * count : (g + 1) * count, :].astype(out.dtype)


def interact(proj, blocks):
    towers = len(blocks)
    local = blocks[0].shape[0]
    count = proj.shape[0]
    per = towers * local // count
    return pl.pallas_call(
        functools.partial(interact_kernel, towers),
        out_shape=jax.ShapeDtypeStruct((per, count, EDIM), jnp.bfloat16),
        in_specs=[pl.BlockSpec(memory_space=pltpu.VMEM)] * (1 + towers),
        out_specs=pl.BlockSpec(memory_space=pltpu.VMEM),
        scratch_shapes=[pltpu.VMEM((towers * local, EDIM), jnp.float32)],
        compiler_params=pltpu.CompilerParams(vmem_limit_bytes=8 << 20),
        name="interact",
    )(proj, *blocks)


def shards(
    embeddings,
    feature_assign,
    sample_owner,
    first_weight,
    first_bias,
    tower_weight,
    tower_bias,
    proj_weight,
):
    towers, intra = lax.axis_size("tower"), lax.axis_size("intra")
    small = (feature_assign, first_bias, tower_bias, proj_weight)
    ahead = 10_000 * (first_weight.size + tower_weight.size)
    pair = 2 if intra % 2 == 0 else 1
    blocks, small = gather_blocks(sample_owner, embeddings, small, towers, intra, pair, ahead)
    slots, first_bias, tower_bias, proj_weight = small
    blocks = exchange_chips(blocks, intra, pair)
    vectors = run_towers(
        slots, first_weight, first_bias, tower_weight, tower_bias, blocks, towers, intra, pair
    )
    vectors = exchange_groups(vectors, towers, intra)
    return interact(proj_weight, vectors)


def solution(mesh):
    return jax.shard_map(
        shards,
        mesh=mesh,
        in_specs=(
            P(None, ("tower", "intra")),
            P("tower", None),
            P(),
            P("tower", None, None),
            P("tower", None),
            P("tower", None, None),
            P("tower", None),
            P(),
        ),
        out_specs=P(("tower", "intra"), None, None),
        check_vma=False,
    )
```

```python
import functools

import jax
import jax.numpy as jnp
from jax import lax
from jax.experimental import pallas as pl
from jax.experimental.pallas import tpu as pltpu
from jax.sharding import PartitionSpec as P

EDIM = 128
FEW_SAMPLES = 1024


def offsets(size):
    return range(size - 1, -1, -1)


def steps(intra, pair):
    return (*range(1, intra // pair), 0)


def ring_place(chip, chips):
    place = chip
    bits = (chips - 1).bit_length() if chips & (chips - 1) == 0 else 0
    for n in range(1, bits):
        place = place ^ (chip >> n)
    return place


def ring_chip(place, chips):
    return place ^ (place >> 1) if chips & (chips - 1) == 0 else place


def partner(me, step, intra, pair):
    chips = intra // pair
    place = (ring_place(me // pair, chips) + step + chips) % chips
    return ring_chip(place, chips) * pair + (me % pair + (pair - 1 if step else 0)) % pair


def exchange_chips(blocks, intra, pair):
    return [
        lax.ppermute(block, "intra", [(i, partner(i, s, intra, pair)) for i in range(intra)]) if s else block
        for block, s in zip(blocks, steps(intra, pair))
    ]


def other_core(intra):
    return 1 if intra > 1 else 0


def exchange_groups(blocks, towers, intra):
    received = []
    for block, o in zip(blocks, offsets(towers)):
        pairs = [
            (t * intra + i, (t ^ o) * intra + (i ^ other_core(intra)))
            for t in range(towers)
            for i in range(intra)
        ]
        received.append(lax.ppermute(block, ("tower", "intra"), pairs) if o else block)
    return received


def load_kernel(towers, intra, pair, count, owner_hbm, emb_hbm, *rest):
    small, (picks_ref, emb_ref, slots_ref), copies = rest[:count], rest[count : count + 3], rest[count + 3 : -3]
    owner_ref, assign_ref, sems = rest[-3:]
    targets = (assign_ref, *copies)
    pairs = [(owner_hbm, owner_ref), (emb_hbm, emb_ref), *zip(small, targets)]
    loads = [pltpu.make_async_copy(a, b, sems.at[i]) for i, (a, b) in enumerate(pairs)]
    for load in loads:
        load.start()
    samples = emb_ref.shape[0]
    per = samples // (towers * intra)
    me, place = lax.axis_index("intra"), lax.axis_index("tower")
    lane = lax.broadcasted_iota(jnp.int32, (per, samples), 1) - lax.broadcasted_iota(jnp.int32, (per, samples), 0)
    chosen = []
    for s in steps(intra, pair):
        block = partner(me, s, intra, pair)
        for t in range(towers):
            owner = jnp.where(place == t, block, block ^ other_core(intra))
            chosen.append(jnp.where(lane == (t * intra + owner) * per, 1.0, 0.0))
    chosen = jnp.concatenate(chosen, axis=0).astype(jnp.bfloat16)
    loads[0].wait()
    owner = jnp.broadcast_to(owner_ref[...].reshape(1, samples), (samples, samples))
    picks = lax.broadcasted_iota(jnp.int32, (samples, samples), 0) == owner
    picks = jnp.where(picks, 1.0, 0.0).astype(jnp.bfloat16)
    picks_ref[...] = lax.dot_general(
        chosen, picks, (((1,), (1,)), ((), ())), preferred_element_type=jnp.float32
    ).astype(jnp.bfloat16)
    loads[2].wait()
    for slot in range(assign_ref.shape[1]):
        slots_ref[0, assign_ref[0, slot]] = slot
    for load in (loads[1], *loads[3:]):
        load.wait()


def gather_kernel(pair, picks_ref, *rest):
    parts, outs = rest[:pair], rest[pair:]
    held = parts[0].shape[1] // EDIM
    rows = outs[0].shape[1]
    for q, part in enumerate(parts):
        ordered = jnp.dot(picks_ref[...], part[...], preferred_element_type=jnp.float32)
        for n, out in enumerate(outs):
            for f in range(held):
                block = ordered[n * rows : (n + 1) * rows, f * EDIM : (f + 1) * EDIM]
                out[q * held + f] = block.astype(out.dtype)


def gather_blocks(owner, embeddings, small, towers, intra, pair, ahead):
    samples, width = embeddings.shape
    rows, held = samples // intra, pair * width // EDIM
    parts = [lax.ppermute(embeddings, "intra", [(i, i ^ q) for i in range(intra)]) for q in range(1, pair)]
    if samples <= FEW_SAMPLES:
        given = [pltpu.with_memory_space_constraint(a, pltpu.HBM) for a in (owner, embeddings, *small)]
        picks, embeddings, *small = pl.pallas_call(
            functools.partial(load_kernel, towers, intra, pair, len(small)),
            out_shape=[
                pltpu.VMEM((samples // pair, samples), jnp.bfloat16),
                pltpu.VMEM(embeddings.shape, embeddings.dtype),
                pltpu.SMEM(small[0].shape, small[0].dtype),
            ]
            + [pltpu.VMEM(a.shape, a.dtype) for a in small[1:]],
            in_specs=[pl.BlockSpec(memory_space=pltpu.HBM)] * len(given),
            out_specs=[pl.BlockSpec(memory_space=pltpu.VMEM)] * 2
            + [pl.BlockSpec(memory_space=pltpu.SMEM)]
            + [pl.BlockSpec(memory_space=pltpu.VMEM)] * (len(small) - 1),
            scratch_shapes=[
                pltpu.VMEM(owner.shape, owner.dtype),
                pltpu.SMEM(small[0].shape, small[0].dtype),
                pltpu.SemaphoreType.DMA((len(given),)),
            ],
            compiler_params=pltpu.CompilerParams(vmem_limit_bytes=8 << 20),
            name="load",
        )(*given)
        blocks = pl.pallas_call(
            functools.partial(gather_kernel, pair),
            out_shape=[pltpu.VMEM((held, rows, EDIM), embeddings.dtype)] * (intra // pair),
            in_specs=[pl.BlockSpec(memory_space=pltpu.VMEM)] * (1 + pair),
            out_specs=[pl.BlockSpec(memory_space=pltpu.VMEM)] * (intra // pair),
            compiler_params=pltpu.CompilerParams(vmem_limit_bytes=8 << 20),
            cost_estimate=pl.CostEstimate(flops=ahead, bytes_accessed=0, transcendentals=0),
            name="gather_rows",
        )(picks, embeddings, *parts)
        return blocks, small
    order = owner.reshape(towers, intra, -1)
    crossed = order[:, jnp.arange(intra) ^ other_core(intra)]
    own = jnp.arange(towers)[:, None, None] == lax.axis_index("tower")
    order = jnp.where(own, order, crossed).transpose(1, 0, 2)
    me = lax.axis_index("intra")
    table = jnp.concatenate([embeddings, *parts], axis=1)
    blocks = []
    for s in steps(intra, pair):
        mine = lax.dynamic_index_in_dim(order, partner(me, s, intra, pair), keepdims=False).reshape(-1)
        blocks.append(jnp.take(table, mine, axis=0).reshape(rows, held, EDIM).transpose(1, 0, 2))
    assign = small[0][0]
    same = assign[None, :] == jnp.arange(assign.size)[:, None]
    slots = jnp.sum(jnp.where(same, jnp.arange(assign.size)[None, :], 0), axis=1)
    return blocks, (slots.astype(assign.dtype)[None, :], *small[1:])


def first_layer(intra, pair, order, slots_ref, w1_ref, x_ref, blocks, before_ref=None):
    held, rows, _ = blocks[0].shape
    held //= pair
    count, depth, hid = w1_ref.shape
    per_tower = depth // EDIM
    me = lax.axis_index("intra")
    slots = []
    for s, block in zip(order, blocks):
        source = partner(me, -s, intra, pair)
        for q in range(pair):
            for f in range(held):
                slot = slots_ref[0, (source ^ q) * held + f]
                n = len(slots)
                slots.append((slot // per_tower, pl.multiple_of((slot % per_tower) * EDIM, EDIM)))
                for k in range(count):
                    own = jnp.where(slots[n][0] == k, 1.0, 0.0).astype(jnp.bfloat16)
                    x_ref[k * rows : (k + 1) * rows, n * EDIM : (n + 1) * EDIM] = block[q * held + f] * own
    wide = 2 * EDIM
    for h in range(0, hid, wide):
        columns = slice(h, min(h + wide, hid))
        total = None if before_ref is None else before_ref[:, columns]
        for n in range(0, len(slots), 2):
            some = slots[n : n + 2]
            weight = [w1_ref[k, pl.ds(start, EDIM), columns] for k, start in some]
            term = jnp.dot(
                x_ref[:, n * EDIM : (n + len(some)) * EDIM],
                jnp.concatenate(weight, axis=0),
                preferred_element_type=jnp.float32,
            )
            total = term if total is None else total + term
        yield columns, total


def early_kernel(intra, pair, order, slots_ref, w1_ref, *rest):
    blocks, before, (out_ref, x_ref) = rest[: len(order)], rest[len(order) : -2], rest[-2:]
    for columns, total in first_layer(intra, pair, order, slots_ref, w1_ref, x_ref, blocks, *before):
        out_ref[:, columns] = total


def tower_kernel(towers, intra, pair, order, slots_ref, w1_ref, b1_ref, w2_ref, b2_ref, sums_ref, *rest):
    blocks, outs, (x_ref, hidden_ref, y_ref) = rest[: len(order)], rest[len(order) : -3], rest[-3:]
    count, rows, _ = y_ref.shape
    vectors = w2_ref.shape[2] // EDIM
    per = rows // towers
    for columns, total in first_layer(intra, pair, order, slots_ref, w1_ref, x_ref, blocks, sums_ref):
        for k in range(count):
            hidden = total[k * rows : (k + 1) * rows] + b1_ref[k : k + 1, columns]
            hidden_ref[k, :, columns] = jnp.maximum(hidden, 0.0).astype(jnp.bfloat16)
    for k in range(count):
        result = jnp.dot(hidden_ref[k], w2_ref[k], preferred_element_type=jnp.float32)
        y_ref[k] = jnp.maximum(result + b2_ref[k : k + 1, :], 0.0)
    place = lax.axis_index("tower")
    for o, out in zip(offsets(towers), outs):
        start = pl.multiple_of((place ^ o) * per, per)
        pieces = [
            y_ref[k, pl.ds(start, per), v * EDIM : (v + 1) * EDIM]
            for k in range(count)
            for v in range(vectors)
        ]
        out[...] = jnp.concatenate(pieces, axis=0).astype(out.dtype)


def run_towers(slots, w1, b1, w2, b2, blocks, towers, intra, pair):
    order = steps(intra, pair)
    remote = len(blocks) - 1
    cuts = (0, max(remote // 2, min(remote - 1, 1)), remote - 1)
    stages = [[-1], [*range(*cuts[:2])], [*range(*cuts[1:])]]
    late = [remote - 1] if remote else []
    held, rows, _ = blocks[0].shape
    count, depth, hid = w1.shape
    width = w2.shape[2]
    local = count * (width // EDIM) * (rows // towers)
    w1 = pltpu.with_memory_space_constraint(w1, pltpu.VMEM)
    w2 = pltpu.with_memory_space_constraint(w2, pltpu.VMEM)
    params = pltpu.CompilerParams(vmem_limit_bytes=16 << 20)
    sums = ()
    for stage in stages:
        if not stage:
            continue
        sums = pl.pallas_call(
            functools.partial(early_kernel, intra, pair, [order[n] for n in stage]),
            out_shape=[pltpu.VMEM((count * rows, hid), jnp.float32)],
            in_specs=[pl.BlockSpec(memory_space=pltpu.SMEM)]
            + [pl.BlockSpec(memory_space=pltpu.VMEM)] * (1 + len(stage) + len(sums)),
            out_specs=[pl.BlockSpec(memory_space=pltpu.VMEM)],
            scratch_shapes=[pltpu.VMEM((count * rows, len(stage) * held * EDIM), jnp.bfloat16)],
            compiler_params=params,
            cost_estimate=pl.CostEstimate(
                flops=2 * count * rows * depth * hid, bytes_accessed=0, transcendentals=0
            ),
            name="towers_early",
        )(slots, w1, *(blocks[n] for n in stage), *sums)
    return pl.pallas_call(
        functools.partial(tower_kernel, towers, intra, pair, [order[n] for n in late]),
        out_shape=[pltpu.VMEM((local, EDIM), jnp.bfloat16)] * towers,
        in_specs=[pl.BlockSpec(memory_space=pltpu.SMEM)]
        + [pl.BlockSpec(memory_space=pltpu.VMEM)] * (5 + len(late)),
        out_specs=[pl.BlockSpec(memory_space=pltpu.VMEM)] * towers,
        scratch_shapes=[
            pltpu.VMEM((count * rows, max(len(late), 1) * held * EDIM), jnp.bfloat16),
            pltpu.VMEM((count, rows, hid), jnp.bfloat16),
            pltpu.VMEM((count, rows, width), jnp.float32),
        ],
        compiler_params=params,
        name="towers",
    )(slots, w1, b1, w2, b2, *sums, *(blocks[n] for n in late))


def interact_kernel(towers, proj_ref, *rest):
    blocks, out, all_ref = rest[:towers], rest[towers], rest[towers + 1]
    per, count, _ = out.shape
    local = blocks[0].shape[0]
    place = lax.axis_index("tower")
    for o, block in zip(offsets(towers), blocks):
        start = pl.multiple_of((place ^ o) * local, local)
        all_ref[pl.ds(start, local), :] = block[...].astype(jnp.float32)
    group = max(1, min(per, 128 // count))
    proj = jnp.concatenate([proj_ref[...]] * (2 * group), axis=0)
    for first in range(0, per, group):
        samples = range(first, first + group)
        vectors = [all_ref[pl.ds(d, count, stride=per), :] for d in samples]
        vectors = jnp.concatenate(vectors, axis=0).astype(jnp.bfloat16)
        gram = lax.dot_general(
            vectors, vectors, (((1,), (1,)), ((), ())), preferred_element_type=jnp.float32
        )
        gram = gram * (1.0 / EDIM)
        column = lax.broadcasted_iota(jnp.int32, (count, gram.shape[1]), 1)
        own = [
            jnp.where(
                (column >= g * count) & (column < (g + 1) * count),
                gram[g * count : (g + 1) * count, :],
                0.0,
            )
            for g in range(group)
        ]
        gram = jnp.concatenate(own, axis=0)
        high = gram.astype(jnp.bfloat16)
        low = (gram - high.astype(jnp.float32)).astype(jnp.bfloat16)
        result = jnp.dot(
            jnp.concatenate([high, low], axis=1), proj, preferred_element_type=jnp.float32
        )
        for g, d in enumerate(samples):
            out[d] = result[g * count : (g + 1) * count, :].astype(out.dtype)


def interact(proj, blocks):
    towers = len(blocks)
    local = blocks[0].shape[0]
    count = proj.shape[0]
    per = towers * local // count
    return pl.pallas_call(
        functools.partial(interact_kernel, towers),
        out_shape=jax.ShapeDtypeStruct((per, count, EDIM), jnp.bfloat16),
        in_specs=[pl.BlockSpec(memory_space=pltpu.VMEM)] * (1 + towers),
        out_specs=pl.BlockSpec(memory_space=pltpu.VMEM),
        scratch_shapes=[pltpu.VMEM((towers * local, EDIM), jnp.float32)],
        compiler_params=pltpu.CompilerParams(vmem_limit_bytes=8 << 20),
        name="interact",
    )(proj, *blocks)


def shards(
    embeddings,
    feature_assign,
    sample_owner,
    first_weight,
    first_bias,
    tower_weight,
    tower_bias,
    proj_weight,
):
    towers, intra = lax.axis_size("tower"), lax.axis_size("intra")
    small = (feature_assign, first_bias, tower_bias, proj_weight)
    ahead = 10_000 * (first_weight.size + tower_weight.size)
    pair = 2 if intra % 2 == 0 else 1
    blocks, small = gather_blocks(sample_owner, embeddings, small, towers, intra, pair, ahead)
    slots, first_bias, tower_bias, proj_weight = small
    blocks = exchange_chips(blocks, intra, pair)
    vectors = run_towers(
        slots, first_weight, first_bias, tower_weight, tower_bias, blocks, towers, intra, pair
    )
    vectors = exchange_groups(vectors, towers, intra)
    return interact(proj_weight, vectors)


def solution(mesh):
    return jax.shard_map(
        shards,
        mesh=mesh,
        in_specs=(
            P(None, ("tower", "intra")),
            P("tower", None),
            P(),
            P("tower", None, None),
            P("tower", None),
            P("tower", None, None),
            P("tower", None),
            P(),
        ),
        out_specs=P(("tower", "intra"), None, None),
        check_vma=False,
    )
```
